128 devices in a mesh: ctx: 8 (over y_hi, z), tp: 16 (over x, y_lo, core).
Axes of the slice: x: 4, y: 4 (y_hi: 2, y_lo: 2; y = y_hi * 2 + y_lo), z: 4, core: 2. Of those that a mesh axis runs over, the one named last changes fastest.
Arguments:
- residual: bfloat16 [2048, 5376], P('ctx'), may hold values from -80 to 80
- stored_blocks: bfloat16 [896, 96, 768], P(('ctx', 'tp')), may hold values from -0.078125 to 0.078125
- block_list: int32 [896], replicated, may hold values from 0 to 895, as said below
- lengths: int32 [4], replicated, may hold values from 1 to 1536, 2048 in all
- in_gain: float32 [5376], replicated, may hold values from 0.5 to 1.5
- q_gain: float32 [128], replicated, may hold values from 0.25 to 1.75
- k_gain: float32 [128], replicated, may hold values from 0.25 to 1.75
- post_gain: float32 [5376], replicated, may hold values from 0.5 to 1.5
- final_gain: float32 [5376], replicated, may hold values from 0.5 to 1.5
- vocab_table: bfloat16 [147456, 5376], P(('ctx', 'tp')), may hold values from -1 to 1
- actions: int32 [2048], replicated, may hold values from 0 to 147455
- old_logprob: float32 [2048], P(('ctx', 'tp')), may hold values from -16 to -6
Outputs:
- ref_logprob: float32 [2048], P(('ctx', 'tp'))
- log_ratio: float32 [2048], P(('ctx', 'tp'))
The draws below stay inside these ranges and needn't reach their ends.
Inputs may be any that keep to these rules, and one draw needn't show every extreme that they name: block_list holds every number of 0 to 895 once; the 7 slots of one storage device (slots d * 7 onward, d = its index over ctx+tp) belong to 7 different readers t, and the storage devices of one index of ctx together hold exactly 7 blocks of every reader.
All inputs are finite; a program needn't handle non-finite values.
Results may differ from the reference program's by a relative error of at most 0.0034.
Values may be sent and summed in bfloat16 or wider, within the bound.
A program may use at most 128 MiB of HBM per device.

```python
import math
import jax
import jax.numpy as jnp
import numpy as np
from jax import lax

D = 5376
HEADS = 32
KV_HEADS = 16
HEAD_DIM = 128
WINDOW = 1024
QUERY_SCALAR = 168
VOCAB = 147456
BLK_DEV = 7
NSEQ = 4
TOKENS = 2048
NB = 896
BR = 96
RC = 768
N_CTX = 8
N_TP = 16


def draw_block_list(key, part):
    key = jax.random.fold_in(key, 11)
    key_list = jax.random.split(key, 3)
    rows_per_reader = BLK_DEV * N_CTX
    spin_perm = jax.vmap(lambda sub_key: jax.random.permutation(sub_key, N_TP))(jax.random.split(key_list[0], N_CTX))
    offset = jax.vmap(lambda sub_key: jax.random.permutation(sub_key, N_TP))(jax.random.split(key_list[1], N_CTX))
    slot_ids = jnp.arange(BLK_DEV, dtype=jnp.int32)
    column = (offset[:, :, None] + slot_ids[None, None, :]) % N_TP
    reader = jnp.take_along_axis(spin_perm, column.reshape(N_CTX, -1), axis=1).reshape(-1).astype(jnp.int32)
    onehot = (reader[:, None] == jnp.arange(N_TP, dtype=jnp.int32)[None, :]).astype(jnp.int32)
    rank_ids = jnp.sum((jnp.cumsum(onehot, axis=0) - 1) * onehot, axis=1)
    rowperm = jax.vmap(lambda sub_key: jax.random.permutation(sub_key, rows_per_reader))(jax.random.split(key_list[2], N_TP))
    row_block = rowperm[reader, rank_ids]
    return (reader * rows_per_reader + row_block).astype(jnp.int32)


def draw_residual(key, part):
    key = jax.random.fold_in(key, 21)
    key_list = jax.random.split(key, 3)
    row_scale = jnp.exp(jax.random.uniform(key_list[0], (TOKENS, 1), minval=math.log(0.3), maxval=math.log(3.0)))
    col_scale = jnp.exp(jax.random.uniform(key_list[1], (1, D), minval=math.log(0.3), maxval=math.log(3.0)))
    drawn = jax.random.normal(key_list[2], (TOKENS, D))
    return jnp.clip(drawn * row_scale * col_scale, -80.0, 80.0).astype(jnp.bfloat16)


def draw_vocab_table(key, part):
    key = jax.random.fold_in(key, 31)
    key_list = jax.random.split(key, 2)
    jitter = jnp.exp(jax.random.uniform(key_list[0], (VOCAB, 1), minval=math.log(0.9), maxval=math.log(1.1)))
    drawn = jax.random.normal(key_list[1], (VOCAB, D))
    spread = 3.3
    return jnp.clip(drawn * jitter * (spread / math.sqrt(D)), -1.0, 1.0).astype(jnp.bfloat16)


def place_ends(array, own_key, least, top_value):
    index_at = [jax.random.randint(jax.random.fold_in(own_key, axis), (), 0, length) for axis, length in enumerate(array.shape)]
    widest = array.shape.index(max(array.shape))
    neighbour = index_at[:widest] + [(index_at[widest] + 1) % array.shape[widest]] + index_at[widest + 1:]
    return array.at[tuple(index_at)].set(least).at[tuple(neighbour)].set(top_value)


def block_levels(stream_key, shape, cuts, least, top_value):
    def one(axis_at, blocks):
        heights = jax.random.uniform(jax.random.fold_in(jax.random.fold_in(stream_key, 6), axis_at), (blocks,), jnp.float32, least / len(cuts), top_value / len(cuts))
        return jnp.repeat(jnp.exp(heights), shape[axis_at] // blocks).reshape((-1,) + (1,) * (len(shape) - axis_at - 1))

    gain = one(*cuts[0])
    for cut in cuts[1:]:
        gain = gain * one(*cut)
    return gain


def split_up(number_of, total, most, lean):
    loads = [(1 << 20) // math.isqrt(rank ** lean) + 1 for rank in range(2, number_of + 1)]
    surplus, counts = total - most - (number_of - 1), [1] * (number_of - 1)
    while surplus > 0:
        free = [i for i in range(number_of - 1) if counts[i] < most]
        whole, remaining = sum([loads[i] for i in free]), surplus
        for i in free:
            addition = min(most - counts[i], max(1, remaining * loads[i] // whole), surplus)
            counts[i] = counts[i] + addition
            surplus = surplus - addition
    return np.array([most] + counts)


def ragged_sizes(own_key, count, total, limit, slope):
    if count == 2:
        one = jax.random.randint(own_key, (), max(1, total - limit), min(limit, total - 1) + 1)
        return jnp.stack([one, total - one])
    tallies = jnp.asarray(split_up(count, total, limit, slope), jnp.int32)
    couples = (count - 1) // 2
    source_of, taker = tallies[1:1 + 2 * couples:2], tallies[2:2 + 2 * couples:2]
    slack = jnp.minimum(source_of - 1, limit - taker)
    passed = jax.random.randint(jax.random.fold_in(own_key, 1), (couples,), 0, 1 << 20) % (slack + 1)
    tallies = tallies.at[1:1 + 2 * couples:2].set(source_of - passed).at[2:2 + 2 * couples:2].set(taker + passed)
    return tallies[jax.random.permutation(jax.random.fold_in(own_key, 2), count)]


def scatter_about(stream_key, extent, width, reach, cuts=(), kind=jnp.bfloat16):
    gain = block_levels(stream_key, extent, cuts, -0.22, 0.18) if cuts else 1.0
    entries = jax.random.normal(stream_key, extent, jnp.float32) * width * gain
    return jnp.minimum(jnp.maximum(entries, -reach), reach).astype(kind)


def setup_inputs(seed: int = 0) -> dict:
    splits = jax.random.split(jax.random.key(seed), 13)
    residual = draw_residual(jax.random.fold_in(splits[12], 71), 0)
    stored_blocks = scatter_about(splits[1], (NB, BR, RC), D ** -0.5, 0.078125, ((0, 128),))
    block_list = draw_block_list(jax.random.fold_in(splits[12], 71), 0)
    lengths = ragged_sizes(splits[3], NSEQ, TOKENS, TOKENS * 3 // 4, 2).astype(jnp.int32)
    in_gain = jnp.clip(1.0 + 0.1 * jax.random.normal(splits[4], (D,), jnp.float32), 0.5, 1.5)
    q_gain = jnp.clip(1.0 + 0.15 * jax.random.normal(splits[5], (HEAD_DIM,), jnp.float32), 0.25, 1.75)
    k_gain = jnp.clip(1.0 + 0.15 * jax.random.normal(splits[6], (HEAD_DIM,), jnp.float32), 0.25, 1.75)
    post_gain = jnp.clip(1.0 + 0.1 * jax.random.normal(splits[7], (D,), jnp.float32), 0.5, 1.5)
    final_gain = jnp.clip(1.0 + 0.1 * jax.random.normal(splits[8], (D,), jnp.float32), 0.5, 1.5)
    vocab_table = draw_vocab_table(jax.random.fold_in(splits[12], 71), 0)
    actions = place_ends(jax.random.randint(splits[10], (TOKENS,), 0, VOCAB), jax.random.fold_in(splits[10], 1), 0, VOCAB - 1).astype(jnp.int32)
    old_logprob = jnp.clip(-16.0 + 10.0 * jax.random.uniform(splits[11], (TOKENS,), jnp.float32) ** block_levels(splits[11], (TOKENS,), ((0, 128),), -0.2, 0.2), -16.0, -6.0)
    return {"residual": residual, "stored_blocks": stored_blocks, "block_list": block_list, "lengths": lengths, "in_gain": in_gain, "q_gain": q_gain, "k_gain": k_gain, "post_gain": post_gain, "final_gain": final_gain, "vocab_table": vocab_table, "actions": actions, "old_logprob": old_logprob}


epsilon = 1e-06
soft_cap = 30.0
rope_base = 10000.0

def rms_scale(values, gain_vec):
    mean_sq = lax.optimization_barrier(jnp.mean(values * values, axis=-1, keepdims=True))
    return values * lax.rsqrt(mean_sq + epsilon) * gain_vec

def rotate(values, position):
    half_size = values.shape[-1] // 2
    frequency = rope_base ** (-2.0 * jnp.arange(half_size, dtype=jnp.float32) / values.shape[-1])
    angle_rows = position.astype(jnp.float32)[:, None] * frequency[None, :]
    cosine = jnp.cos(angle_rows)
    sine_part = jnp.sin(angle_rows)
    first_half = values[..., :half_size]
    second_half = values[..., half_size:]
    return jnp.concatenate([first_half * cosine - second_half * sine_part, second_half * cosine + first_half * sine_part], axis=-1)

def reference(residual, stored_blocks, block_list, lengths, in_gain, q_gain, k_gain, post_gain, final_gain, vocab_table, actions, old_logprob):
    block_order = jnp.argsort(block_list)
    weights = stored_blocks[block_order].reshape(N_TP, D, -1)
    query_width = HEADS // N_TP * HEAD_DIM
    key_width = KV_HEADS // N_TP * HEAD_DIM
    group_size = HEADS // KV_HEADS
    row_ids = jnp.arange(TOKENS, dtype=jnp.int32)
    seq_starts = (jnp.cumsum(lengths) - lengths).astype(jnp.int32)
    seg_start = lax.optimization_barrier(jnp.max(jnp.where(seq_starts[None, :] <= row_ids[:, None], seq_starts[None, :], 0), axis=1)).astype(jnp.int32)
    position = row_ids - seg_start
    visible = (row_ids[None, :] <= row_ids[:, None]) & (row_ids[:, None] - row_ids[None, :] < WINDOW) & (row_ids[None, :] >= seg_start[:, None])
    normed = rms_scale(residual.astype(jnp.float32), in_gain).astype(jnp.bfloat16)
    score_scale = QUERY_SCALAR ** (-0.5)

    def one_shard(carry_in, weight):
        projected = jnp.dot(normed, weight[:, :query_width + 2 * key_width], preferred_element_type=jnp.float32)
        query_rows = projected[:, :query_width].reshape(TOKENS, -1, HEAD_DIM).transpose(1, 0, 2)
        key_rows = projected[:, query_width:query_width + key_width].reshape(TOKENS, -1, HEAD_DIM).transpose(1, 0, 2)
        value_rows = projected[:, query_width + key_width:].reshape(TOKENS, -1, HEAD_DIM).transpose(1, 0, 2).astype(jnp.bfloat16)
        query_rows = rotate(rms_scale(query_rows, q_gain), position).astype(jnp.bfloat16)
        key_rows = rotate(rms_scale(key_rows, k_gain), position).astype(jnp.bfloat16)
        key_rows = jnp.repeat(key_rows, group_size, axis=0)
        value_rows = jnp.repeat(value_rows, group_size, axis=0)
        scores = jnp.einsum('hqd,hkd->hqk', query_rows.astype(jnp.float32), key_rows.astype(jnp.float32)) * score_scale
        prob_rows = jnp.where(visible[None], jnp.exp(scores), 0.0)
        prob_rows = (prob_rows / lax.optimization_barrier(jnp.sum(prob_rows, axis=2, keepdims=True))).astype(jnp.bfloat16)
        mixed_out = jnp.einsum('hqk,hkd->hqd', prob_rows.astype(jnp.float32), value_rows.astype(jnp.float32)).astype(jnp.bfloat16)
        mixed_flat = mixed_out.transpose(1, 0, 2).reshape(TOKENS, query_width)
        term_rows = lax.dot_general(mixed_flat, weight[:, query_width + 2 * key_width:], (((1,), (1,)), ((), ())), preferred_element_type=jnp.float32)
        return (carry_in + term_rows, None)
    attended, _ = lax.scan(one_shard, jnp.zeros((TOKENS, D), jnp.float32), weights)
    hidden = residual.astype(jnp.float32) + rms_scale(attended, post_gain)
    final = rms_scale(hidden, final_gain).astype(jnp.bfloat16)
    table_blocks = vocab_table.reshape(N_CTX * N_TP, -1, D)
    first_ids = jnp.arange(N_CTX * N_TP, dtype=jnp.int32) * (VOCAB // (N_CTX * N_TP))

    def vocab_step(carry_in, inputs):
        table_block, first_id = inputs
        logits = lax.dot_general(final, table_block, (((1,), (1,)), ((), ())), preferred_element_type=jnp.float32)
        capped = soft_cap * jnp.tanh(logits / soft_cap)
        vocab_ids = first_id + jnp.arange(table_block.shape[0], dtype=jnp.int32)
        hit_mask = vocab_ids[None, :] == actions[:, None]
        exp_sum = carry_in[0] + lax.optimization_barrier(jnp.sum(jnp.exp(capped), axis=1))
        picked_logit = carry_in[1] + lax.optimization_barrier(jnp.sum(jnp.where(hit_mask, capped, 0.0), axis=1))
        return ((exp_sum, picked_logit), None)
    zero_rows = jnp.zeros((TOKENS,), jnp.float32)
    (exp_sum, picked_logit), _ = lax.scan(vocab_step, (zero_rows, zero_rows), (table_blocks, first_ids))
    ref_logprob = picked_logit - jnp.log(exp_sum)
    return (ref_logprob, old_logprob - ref_logprob)
```

```python
import jax
import jax.numpy as jnp
from jax import lax
from jax.experimental import pallas as pl
from jax.experimental.pallas import tpu as pltpu
from jax.sharding import PartitionSpec as P

HEADS = 32
KV_HEADS = 16
HEAD_DIM = 128
WINDOW = 1024
QUERY_SCALAR = 168


epsilon = 1e-06
soft_cap = 30.0
rope_base = 10000.0
MESH = pl.DeviceIdType.MESH
VMEM = pltpu.VMEM
A2_REL = (0, 1, 3, 2)


def coords():
    c = lax.axis_index("ctx")
    t = lax.axis_index("tp")
    return t // 4, (c // 4) * 2 + (t // 2) % 2, c % 4, t % 2


def device_of(x, y, z, k):
    x, y, z, k = x % 4, y % 4, z % 4, k % 2
    return ((y // 2) * 4 + z, x * 4 + (y % 2) * 2 + k)


def axis_of(part, place):
    return (part + place) % 3


def shifted(axis, steps):
    where = list(coords())
    where[axis] = where[axis] + steps
    return device_of(*where)


def sibling():
    x, y, z, k = coords()
    return device_of(x, y, z, k + 1)


def greet(peers):
    barrier = pltpu.get_barrier_semaphore()
    for peer in peers:
        pl.semaphore_signal(barrier, inc=1, device_id=peer, device_id_type=MESH)
    pl.semaphore_wait(barrier, len(peers))


def vocab_kernel(
    fin_ref, table_ref, actions_ref, out_ref,
    buf, table, acc, part_exp, part_hit, st1, r1, st2, r2,
    table_sem, s1, v1, s2, v2, s3, v3, sf, vf, sk, vk, sa, va, sb, vb,
):
    ctx = lax.axis_index("ctx")
    tp = lax.axis_index("tp")
    core = tp % 2
    own = coords()[:3]
    width = fin_ref.shape[1] // 3
    rows = fin_ref.shape[0]
    vocab_rows = table.shape[1]

    def table_copy(p):
        return pltpu.make_async_copy(
            table_ref.at[:, pl.ds(p * width, width)], table.at[p], table_sem.at[p]
        )

    for p in range(3):
        table_copy(p).start()
    for p in range(3):
        buf[p, 0, 0, core, 0] = fin_ref[:, pl.ds(p * width, width)]
    x, y, z, k = coords()
    c_peer = lambda off: ((ctx + off) % 8, tp)
    t_peer = lambda off: (ctx, (tp + off) % 16)
    far_y = device_of(x, y - 1 + 2 * (y % 2), z, k)
    greet([c_peer(o) for o in range(1, 8)] + [t_peer(o) for o in range(1, 16)] + [far_y])

    def send(src, dst, send_sem, recv_sem, peer):
        return pltpu.make_async_remote_copy(
            src_ref=src, dst_ref=dst, send_sem=send_sem, recv_sem=recv_sem,
            device_id=peer, device_id_type=MESH,
        )

    def first(p, step):
        return send(
            buf.at[p, 0, 0, core, 0], buf.at[p, 0, 0, core, 4 - step],
            s1.at[p, step - 1], v1.at[p, step - 1], shifted(axis_of(p, 0), step),
        )

    def second(p, step):
        slot = A2_REL.index(4 - step)
        return send(
            buf.at[p, 0, 0, core], buf.at[p, 0, slot, core],
            s2.at[p, slot], v2.at[p, slot], shifted(axis_of(p, 1), step),
        )

    def third(p, q, step):
        return send(
            buf.at[p, 0, q, core], buf.at[p, 4 - step, q, core],
            s3.at[p, 4 - step, q], v3.at[p, 4 - step, q], shifted(axis_of(p, 2), step),
        )

    def passed(p, slab, q, step):
        return send(
            buf.at[p, slab, q, core], buf.at[p, 2, q, core],
            sf.at[p, q], vf.at[p, q], shifted(axis_of(p, 2), step),
        )

    def across(p, slab, q):
        return send(
            buf.at[p, slab, q, core], buf.at[p, slab, q, core],
            sk.at[p, slab, q], vk.at[p, slab, q], sibling(),
        )

    for p in range(3):
        for step in (1, 3, 2):
            first(p, step).start()
    for p in range(3):
        for step in (1, 3, 2):
            first(p, step).wait_recv()
        for step in (3, 1, 2):
            second(p, step).start()
    for p in range(3):
        for step in (1, 3):
            third(p, 0, step).start()
        across(p, 0, 0).start()

    def own_chunk(p, q):
        second(p, 4 - A2_REL[q]).wait_recv()
        for step in (1, 3):
            third(p, q, step).start()
        across(p, 0, q).start()

    for p in range(3):
        own_chunk(p, 1)

    def slab_of(g):
        return jnp.where(g < 2, 0, jnp.where(g > 5, 2, jnp.where(g % 2 == 0, 3, 1)))

    def half_of(g):
        return jnp.where(g < 2, g, jnp.where(g > 5, g - 6, (g - 2) // 2))

    def arrivals(g):
        slab, half = slab_of(g), half_of(g)

        @pl.when(g == 1)
        def _():
            for q in (2, 3):
                for p in range(3):
                    own_chunk(p, q)

        @pl.when((g > 1) & (g < 6))
        def _():
            for i in range(2):
                q = half * 2 + i
                for p in range(3):
                    pltpu.make_async_remote_copy(
                        src_ref=buf.at[p, 0, q, core], dst_ref=buf.at[p, slab, q, core],
                        send_sem=s3.at[p, slab, q], recv_sem=v3.at[p, slab, q],
                        device_id=sibling(), device_id_type=MESH,
                    ).wait_recv()
                    if i == 0:
                        @pl.when(slab == 3)
                        def _():
                            passed(p, 3, q, 1).start()
                    else:
                        @pl.when(slab == 1)
                        def _():
                            passed(p, 1, q, 3).start()
                    across(p, slab, q).start()

        @pl.when((g > 5) & (g < 8))
        def _():
            for i in range(2):
                q = half * 2 + i
                for p in range(3):
                    passed(p, 3, q, 1).wait_recv()
                    across(p, 2, q).start()

    def place(axis_values, k):
        x, y, z = axis_values
        return ((y // 2) * 4 + z) * 16 + x * 4 + (y % 2) * 2 + k

    def group(g, carry):
        slab, half = slab_of(g), half_of(g)
        for p in range(3):
            for i in range(2):
                across(p, slab, half * 2 + i).wait_recv()

            @pl.when(g == 0)
            def _():
                table_copy(p).wait()

            lhs = buf[p, slab, pl.ds(half * 2, 2)].reshape(16 * rows, width)
            got = lax.dot_general(
                lhs, table[p], (((1,), (1,)), ((), ())), preferred_element_type=jnp.float32
            )
            a1, a2, a3 = (axis_of(p, i) for i in range(3))
            for i in range(2):
                q = half * 2 + i
                rel2 = jnp.where(q < 2, q, 5 - q)
                for kk in range(2):
                    for r1_ in range(4):
                        at = [None] * 3
                        at[a1] = (own[a1] + r1_) % 4
                        at[a2] = (own[a2] + rel2) % 4
                        at[a3] = (own[a3] + slab) % 4
                        d = place(at, kk)
                        m = (i * 2 + kk) * 4 + r1_
                        value = got[m * rows:(m + 1) * rows]
                        acc[d] = acc[d] + value
            if p == 0:
                arrivals(g + 1)
        return carry

    def clear(d, carry):
        acc[d] = jnp.zeros((rows, vocab_rows), jnp.float32)
        return carry

    lax.fori_loop(0, 128, clear, 0)
    lax.fori_loop(0, 8, group, 0)

    first_id = (ctx * 16 + tp) * vocab_rows
    ids = first_id + lax.broadcasted_iota(jnp.int32, (rows, vocab_rows), 1)

    def fold(v):
        total = v[:, :128]
        for i in range(1, vocab_rows // 128):
            total = total + v[:, i * 128:(i + 1) * 128]
        return total

    def tail(d, carry):
        capped = soft_cap * jnp.tanh(acc[d] * (1.0 / soft_cap))
        hit = ids == actions_ref[d]
        part_exp[d] = fold(jnp.exp(capped))
        part_hit[d] = fold(jnp.where(hit, capped, 0.0))
        return carry

    lax.fori_loop(0, 128, tail, 0)
    ones = jnp.ones((8, 128), jnp.float32)
    for c in range(8):
        for row, part in ((0, part_exp), (1, part_hit)):
            got = lax.dot_general(
                ones, part[pl.ds(c * 16, 16)].reshape(16 * rows, 128), (((1,), (1,)), ((), ())),
                preferred_element_type=jnp.float32, precision=lax.Precision.HIGHEST,
            )
            st1[c, row * 8:(row + 1) * 8, :] = got
    def stage1(off):
        return send(st1.at[(ctx + off) % 8], r1.at[off], sa.at[off], va.at[off], c_peer(off))

    def stage2(off):
        return send(st2, r2.at[off], sb.at[off], vb.at[off], t_peer(off))

    for off in range(1, 8):
        stage1(off).start()
    total = st1[ctx]
    for off in range(1, 8):
        stage1(off).wait_recv()
        total = total + r1[off]
    st2[...] = total
    for off in range(1, 16):
        stage2(off).start()
    for off in range(1, 16):
        stage2(off).wait_recv()
        total = total + r2[off]
    out_ref[...] = total[8:] - jnp.log(total[:8])

    for p in range(3):
        for step in (1, 2, 3):
            first(p, step).wait_send()
            second(p, step).wait_send()
        for q in range(4):
            third(p, q, 1).wait_send()
            third(p, q, 3).wait_send()
            passed(p, 3, q, 1).wait_send()
            for slab in range(4):
                across(p, slab, q).wait_send()
    for off in range(1, 8):
        stage1(off).wait_send()
    for off in range(1, 16):
        stage2(off).wait_send()


def vocab_stats(fin, table, actions):
    rows, depth = fin.shape
    width = depth // 3
    vocab_rows = table.shape[0]
    dma = pltpu.SemaphoreType.DMA
    return pl.pallas_call(
        vocab_kernel,
        out_shape=jax.ShapeDtypeStruct((8, 16 * rows), jnp.float32),
        in_specs=[
            pl.BlockSpec(memory_space=VMEM),
            pl.BlockSpec(memory_space=pl.ANY),
            pl.BlockSpec(memory_space=VMEM),
        ],
        out_specs=pl.BlockSpec(memory_space=VMEM),
        scratch_shapes=[
            VMEM((3, 4, 4, 2, 4, rows, width), jnp.bfloat16),
            VMEM((3, vocab_rows, width), jnp.bfloat16),
            VMEM((128, rows, vocab_rows), jnp.float32),
            VMEM((128, rows, 128), jnp.float32),
            VMEM((128, rows, 128), jnp.float32),
            VMEM((8, 16, 16 * rows), jnp.float32),
            VMEM((8, 16, 16 * rows), jnp.float32),
            VMEM((16, 16 * rows), jnp.float32),
            VMEM((16, 16, 16 * rows), jnp.float32),
            dma((3,)),
            dma((3, 3)), dma((3, 3)),
            dma((3, 4)), dma((3, 4)),
            dma((3, 4, 4)), dma((3, 4, 4)),
            dma((3, 4)), dma((3, 4)),
            dma((3, 4, 4)), dma((3, 4, 4)),
            dma((8,)), dma((8,)),
            dma((16,)), dma((16,)),
        ],
        compiler_params=pltpu.CompilerParams(
            collective_id=2, has_side_effects=True, vmem_limit_bytes=60 * 2**20
        ),
        name="vocab_stats",
    )(fin, table, actions.reshape(128, rows, 1))


def from_behind(value, axis, steps):
    count = lax.axis_size(axis)
    leading, last = (max(0, -steps), min(count, count - steps))
    return lax.ppermute(value, axis, [(source, source + steps) for source in range(leading, last)])


def rms_scale(values, gain_vec):
    mean_sq = jnp.mean(values * values, axis=-1, keepdims=True)
    return values * lax.rsqrt(mean_sq + epsilon) * gain_vec


def rotate(values, position):
    half_size = values.shape[-1] // 2
    frequency = rope_base ** (-2.0 * jnp.arange(half_size, dtype=jnp.float32) / values.shape[-1])
    angle_rows = position.astype(jnp.float32)[:, None] * frequency[None, :]
    cosine = jnp.cos(angle_rows)
    sine_part = jnp.sin(angle_rows)
    first_half = values[..., :half_size]
    second_half = values[..., half_size:]
    return jnp.concatenate(
        [
            first_half * cosine - second_half * sine_part,
            second_half * cosine + first_half * sine_part,
        ],
        axis=-1,
    )


def shards(
    residual,
    stored_blocks,
    block_list,
    lengths,
    in_gain,
    q_gain,
    k_gain,
    post_gain,
    final_gain,
    vocab_table,
    actions,
    old_logprob,
):
    ctx_count = lax.axis_size("ctx")
    tp_count = lax.axis_size("tp")
    ctx_index = lax.axis_index("ctx")
    tp_index = lax.axis_index("tp")
    row_count = residual.shape[0]
    blocks_dev = stored_blocks.shape[0]
    rows_per_reader = blocks_dev * ctx_count
    list_grid = block_list.reshape(ctx_count, tp_count, blocks_dev)
    reader_ids = list_grid // rows_per_reader
    row_index_all = list_grid % rows_per_reader
    my_list = lax.dynamic_index_in_dim(
        lax.dynamic_index_in_dim(list_grid, ctx_index, 0, False), tp_index, 0, False
    )
    my_readers = my_list // rows_per_reader
    send_mask = (my_readers[None, :] == jnp.arange(tp_count, dtype=jnp.int32)[:, None]).astype(
        jnp.bfloat16
    )
    outgoing = jnp.einsum(
        "tk,krc->trc", send_mask, stored_blocks, preferred_element_type=jnp.float32
    ).astype(jnp.bfloat16)
    incoming = lax.all_to_all(outgoing, "tp", split_axis=0, concat_axis=0, tiled=True)
    reader_hit = reader_ids == tp_index
    present = jnp.any(reader_hit, axis=2).astype(jnp.int32)
    row_index = jnp.sum(jnp.where(reader_hit, row_index_all, 0), axis=2)
    rank_ids = jnp.cumsum(present, axis=1) - 1
    choose_mask = (
        rank_ids[:, None, :] == jnp.arange(blocks_dev, dtype=jnp.int32)[None, :, None]
    ) & (present[:, None, :] == 1)
    kept_index = jnp.sum(jnp.where(choose_mask, row_index[:, None, :], 0), axis=2).reshape(-1)
    my_choose = lax.dynamic_index_in_dim(choose_mask, ctx_index, 0, False).astype(jnp.bfloat16)
    kept_blocks = jnp.einsum(
        "ks,src->krc", my_choose, incoming, preferred_element_type=jnp.float32
    ).astype(jnp.bfloat16)
    gathered = lax.all_gather(kept_blocks, "ctx", axis=0, tiled=True)
    slot_ids = jnp.arange(kept_index.shape[0], dtype=jnp.int32)
    placement = jnp.sum(
        jnp.where(
            kept_index[None, :] == jnp.arange(rows_per_reader, dtype=jnp.int32)[:, None],
            slot_ids[None, :],
            0,
        ),
        axis=1,
    )
    reader_weight = jnp.take(gathered, placement, axis=0).reshape(residual.shape[1], -1)
    query_width = HEADS // tp_count * HEAD_DIM
    key_width = KV_HEADS // tp_count * HEAD_DIM
    group_size = HEADS // KV_HEADS
    seq_starts = jnp.cumsum(lengths) - lengths
    query_ids = ctx_index * row_count + jnp.arange(row_count, dtype=jnp.int32)
    seg_start = jnp.max(
        jnp.where(seq_starts[None, :] <= query_ids[:, None], seq_starts[None, :], 0), axis=1
    )
    position = query_ids - seg_start
    normed = rms_scale(residual.astype(jnp.float32), in_gain).astype(jnp.bfloat16)
    projected = jnp.dot(
        normed, reader_weight[:, : query_width + 2 * key_width], preferred_element_type=jnp.float32
    )
    query_rows = projected[:, :query_width].reshape(row_count, -1, HEAD_DIM).transpose(1, 0, 2)
    key_rows = (
        projected[:, query_width : query_width + key_width]
        .reshape(row_count, -1, HEAD_DIM)
        .transpose(1, 0, 2)
    )
    value_rows = (
        projected[:, query_width + key_width :].reshape(row_count, -1, HEAD_DIM).transpose(1, 0, 2)
    )
    query_rows = rotate(rms_scale(query_rows, q_gain), position).astype(jnp.bfloat16)
    key_rows = rotate(rms_scale(key_rows, k_gain), position).astype(jnp.bfloat16)
    key_value = jnp.stack([key_rows, value_rows.astype(jnp.bfloat16)])
    reach_count = WINDOW // row_count
    earlier = [from_behind(key_value, "ctx", step_back) for step_back in range(reach_count, 0, -1)]
    before_rows = jnp.concatenate(earlier, axis=2)
    window_kv = jnp.concatenate([before_rows, key_value], axis=2)
    key_ids = (ctx_index - reach_count) * row_count + jnp.arange(
        window_kv.shape[2], dtype=jnp.int32
    )
    visible = (
        (key_ids[None, :] <= query_ids[:, None])
        & (query_ids[:, None] - key_ids[None, :] < WINDOW)
        & (key_ids[None, :] >= seg_start[:, None])
    )
    grouped = query_rows.reshape(-1, group_size, row_count, HEAD_DIM)
    scores = jnp.einsum(
        "hgqd,hkd->hgqk", grouped, window_kv[0], preferred_element_type=jnp.float32
    ) * QUERY_SCALAR ** (-0.5)
    prob_rows = jnp.where(visible, jnp.exp(scores), 0.0)
    prob_rows = (prob_rows / jnp.sum(prob_rows, axis=3, keepdims=True)).astype(jnp.bfloat16)
    mixed_out = jnp.einsum(
        "hgqk,hkd->hgqd", prob_rows, window_kv[1], preferred_element_type=jnp.float32
    ).astype(jnp.bfloat16)
    mixed_flat = (
        mixed_out.reshape(-1, row_count, HEAD_DIM)
        .transpose(1, 0, 2)
        .reshape(row_count, query_width)
    )
    out_columns = reader_weight[:, query_width + 2 * key_width :]
    share_rows = row_count // tp_count
    summed = lax.psum_scatter(
        lax.dot_general(
            mixed_flat, out_columns, (((1,), (1,)), ((), ())), preferred_element_type=jnp.float32
        ),
        "tp",
        scatter_dimension=0,
        tiled=True,
    )
    own_rows = lax.dynamic_slice_in_dim(residual, tp_index * share_rows, share_rows, 0)
    hidden = own_rows.astype(jnp.float32) + rms_scale(summed, post_gain)
    final = rms_scale(hidden, final_gain).astype(jnp.bfloat16)
    all_rows = vocab_stats(final, vocab_table, actions)
    ref_logprob = lax.dynamic_slice_in_dim(all_rows[0], tp_index * share_rows, share_rows, 0)
    return (ref_logprob, old_logprob - ref_logprob)


def solution(mesh):
    return jax.shard_map(
        shards,
        mesh=mesh,
        in_specs=(
            P("ctx", None),
            P(("ctx", "tp"), None, None),
            P(),
            P(),
            P(),
            P(),
            P(),
            P(),
            P(),
            P(("ctx", "tp"), None),
            P(),
            P(("ctx", "tp")),
        ),
        out_specs=(P(("ctx", "tp")), P(("ctx", "tp"))),
        check_vma=False,
    )
```

```python
import jax
import jax.numpy as jnp
from jax import lax
from jax.experimental import pallas as pl
from jax.experimental.pallas import tpu as pltpu
from jax.sharding import PartitionSpec as P

HEADS = 32
KV_HEADS = 16
HEAD_DIM = 128
WINDOW = 1024
QUERY_SCALAR = 168


epsilon = 1e-06
soft_cap = 30.0
rope_base = 10000.0
MESH = pl.DeviceIdType.MESH
VMEM = pltpu.VMEM
A2_REL = (0, 1, 3, 2)


def coords():
    c = lax.axis_index("ctx")
    t = lax.axis_index("tp")
    return t // 4, (c // 4) * 2 + (t // 2) % 2, c % 4, t % 2


def device_of(x, y, z, k):
    x, y, z, k = x % 4, y % 4, z % 4, k % 2
    return ((y // 2) * 4 + z, x * 4 + (y % 2) * 2 + k)


def axis_of(part, place):
    return (part + place) % 3


def shifted(axis, steps):
    where = list(coords())
    where[axis] = where[axis] + steps
    return device_of(*where)


def sibling():
    x, y, z, k = coords()
    return device_of(x, y, z, k + 1)


def greet(peers):
    barrier = pltpu.get_barrier_semaphore()
    for peer in peers:
        pl.semaphore_signal(barrier, inc=1, device_id=peer, device_id_type=MESH)
    pl.semaphore_wait(barrier, len(peers))


def vocab_kernel(
    fin_ref, table_ref, actions_ref, out_ref,
    buf, table, acc, part_exp, part_hit, st1, r1, st2, r2,
    table_sem, s1, v1, s2, v2, s3, v3, sf, vf, sk, vk, sa, va, sb, vb,
):
    ctx = lax.axis_index("ctx")
    tp = lax.axis_index("tp")
    core = tp % 2
    own = coords()[:3]
    width = fin_ref.shape[1] // 3
    rows = fin_ref.shape[0]
    vocab_rows = table.shape[1]

    def table_copy(p):
        return pltpu.make_async_copy(
            table_ref.at[:, pl.ds(p * width, width)], table.at[p], table_sem.at[p]
        )

    for p in range(3):
        table_copy(p).start()
    for p in range(3):
        buf[p, 0, 0, core, 0] = fin_ref[:, pl.ds(p * width, width)]
    x, y, z, k = coords()
    c_peer = lambda off: ((ctx + off) % 8, tp)
    t_peer = lambda off: (ctx, (tp + off) % 16)
    far_y = device_of(x, y - 1 + 2 * (y % 2), z, k)
    greet([c_peer(o) for o in range(1, 8)] + [t_peer(o) for o in range(1, 16)] + [far_y])

    def send(src, dst, send_sem, recv_sem, peer):
        return pltpu.make_async_remote_copy(
            src_ref=src, dst_ref=dst, send_sem=send_sem, recv_sem=recv_sem,
            device_id=peer, device_id_type=MESH,
        )

    def first(p, step):
        return send(
            buf.at[p, 0, 0, core, 0], buf.at[p, 0, 0, core, 4 - step],
            s1.at[p, step - 1], v1.at[p, step - 1], shifted(axis_of(p, 0), step),
        )

    def second(p, step):
        slot = A2_REL.index(4 - step)
        return send(
            buf.at[p, 0, 0, core], buf.at[p, 0, slot, core],
            s2.at[p, slot], v2.at[p, slot], shifted(axis_of(p, 1), step),
        )

    def third(p, q, step):
        return send(
            buf.at[p, 0, q, core], buf.at[p, 4 - step, q, core],
            s3.at[p, 4 - step, q], v3.at[p, 4 - step, q], shifted(axis_of(p, 2), step),
        )

    def passed(p, slab, q, step):
        return send(
            buf.at[p, slab, q, core], buf.at[p, 2, q, core],
            sf.at[p, q], vf.at[p, q], shifted(axis_of(p, 2), step),
        )

    def across(p, slab, q):
        return send(
            buf.at[p, slab, q, core], buf.at[p, slab, q, core],
            sk.at[p, slab, q], vk.at[p, slab, q], sibling(),
        )

    for p in range(3):
        for step in (1, 3, 2):
            first(p, step).start()
    for p in range(3):
        for step in (1, 3, 2):
            first(p, step).wait_recv()
        for step in (3, 1, 2):
            second(p, step).start()
    for p in range(3):
        for step in (1, 3):
            third(p, 0, step).start()
        across(p, 0, 0).start()

    def own_chunk(p, q):
        second(p, 4 - A2_REL[q]).wait_recv()
        for step in (1, 3):
            third(p, q, step).start()
        across(p, 0, q).start()

    for p in range(3):
        own_chunk(p, 1)

    def slab_of(g):
        return jnp.where(g < 2, 0, jnp.where(g > 5, 2, jnp.where(g % 2 == 0, 3, 1)))

    def half_of(g):
        return jnp.where(g < 2, g, jnp.where(g > 5, g - 6, (g - 2) // 2))

    def arrivals(g):
        slab, half = slab_of(g), half_of(g)

        @pl.when(g == 1)
        def _():
            for q in (2, 3):
                for p in range(3):
                    own_chunk(p, q)

        @pl.when((g > 1) & (g < 6))
        def _():
            for i in range(2):
                q = half * 2 + i
                for p in range(3):
                    pltpu.make_async_remote_copy(
                        src_ref=buf.at[p, 0, q, core], dst_ref=buf.at[p, slab, q, core],
                        send_sem=s3.at[p, slab, q], recv_sem=v3.at[p, slab, q],
                        device_id=sibling(), device_id_type=MESH,
                    ).wait_recv()
                    if i == 0:
                        @pl.when(slab == 3)
                        def _():
                            passed(p, 3, q, 1).start()
                    else:
                        @pl.when(slab == 1)
                        def _():
                            passed(p, 1, q, 3).start()
                    across(p, slab, q).start()

        @pl.when((g > 5) & (g < 8))
        def _():
            for i in range(2):
                q = half * 2 + i
                for p in range(3):
                    passed(p, 3, q, 1).wait_recv()
                    across(p, 2, q).start()

    def place(axis_values, k):
        x, y, z = axis_values
        return ((y // 2) * 4 + z) * 16 + x * 4 + (y % 2) * 2 + k

    def group(g, carry):
        slab, half = slab_of(g), half_of(g)
        for p in range(3):
            for i in range(2):
                across(p, slab, half * 2 + i).wait_recv()

            @pl.when(g == 0)
            def _():
                table_copy(p).wait()

            lhs = buf[p, slab, pl.ds(half * 2, 2)].reshape(16 * rows, width)
            got = lax.dot_general(
                lhs, table[p], (((1,), (1,)), ((), ())), preferred_element_type=jnp.float32
            )
            a1, a2, a3 = (axis_of(p, i) for i in range(3))
            for i in range(2):
                q = half * 2 + i
                rel2 = jnp.where(q < 2, q, 5 - q)
                for kk in range(2):
                    for r1_ in range(4):
                        at = [None] * 3
                        at[a1] = (own[a1] + r1_) % 4
                        at[a2] = (own[a2] + rel2) % 4
                        at[a3] = (own[a3] + slab) % 4
                        d = place(at, kk)
                        m = (i * 2 + kk) * 4 + r1_
                        value = got[m * rows:(m + 1) * rows]
                        acc[d] = acc[d] + value
            if p == 0:
                arrivals(g + 1)
        return carry

    def clear(d, carry):
        acc[d] = jnp.zeros((rows, vocab_rows), jnp.float32)
        return carry

    lax.fori_loop(0, 128, clear, 0)
    lax.fori_loop(0, 8, group, 0)

    first_id = (ctx * 16 + tp) * vocab_rows
    ids = first_id + lax.broadcasted_iota(jnp.int32, (rows, vocab_rows), 1)

    def fold(v):
        total = v[:, :128]
        for i in range(1, vocab_rows // 128):
            total = total + v[:, i * 128:(i + 1) * 128]
        return total

    def tail(d, carry):
        capped = soft_cap * jnp.tanh(acc[d] * (1.0 / soft_cap))
        hit = ids == actions_ref[d]
        part_exp[d] = fold(jnp.exp(capped))
        part_hit[d] = fold(jnp.where(hit, capped, 0.0))
        return carry

    lax.fori_loop(0, 128, tail, 0)
    ones = jnp.ones((8, 128), jnp.float32)
    for c in range(8):
        for row, part in ((0, part_exp), (1, part_hit)):
            got = lax.dot_general(
                ones, part[pl.ds(c * 16, 16)].reshape(16 * rows, 128), (((1,), (1,)), ((), ())),
                preferred_element_type=jnp.float32, precision=lax.Precision.HIGHEST,
            )
            st1[c, row * 8:(row + 1) * 8, :] = got
    def stage1(off):
        return send(st1.at[(ctx + off) % 8], r1.at[off], sa.at[off], va.at[off], c_peer(off))

    def stage2(off):
        return send(st2, r2.at[off], sb.at[off], vb.at[off], t_peer(off))

    for off in range(1, 8):
        stage1(off).start()
    total = st1[ctx]
    for off in range(1, 8):
        stage1(off).wait_recv()
        total = total + r1[off]
    st2[...] = total
    for off in range(1, 16):
        stage2(off).start()
    for off in range(1, 16):
        stage2(off).wait_recv()
        total = total + r2[off]
    out_ref[...] = total[8:] - jnp.log(total[:8])

    for p in range(3):
        for step in (1, 2, 3):
            first(p, step).wait_send()
            second(p, step).wait_send()
        for q in range(4):
            third(p, q, 1).wait_send()
            third(p, q, 3).wait_send()
            passed(p, 3, q, 1).wait_send()
            for slab in range(4):
                across(p, slab, q).wait_send()
    for off in range(1, 8):
        stage1(off).wait_send()
    for off in range(1, 16):
        stage2(off).wait_send()


def vocab_stats(fin, table, actions):
    rows, depth = fin.shape
    width = depth // 3
    vocab_rows = table.shape[0]
    dma = pltpu.SemaphoreType.DMA
    return pl.pallas_call(
        vocab_kernel,
        out_shape=jax.ShapeDtypeStruct((8, 16 * rows), jnp.float32),
        in_specs=[
            pl.BlockSpec(memory_space=VMEM),
            pl.BlockSpec(memory_space=pl.ANY),
            pl.BlockSpec(memory_space=VMEM),
        ],
        out_specs=pl.BlockSpec(memory_space=VMEM),
        scratch_shapes=[
            VMEM((3, 4, 4, 2, 4, rows, width), jnp.bfloat16),
            VMEM((3, vocab_rows, width), jnp.bfloat16),
            VMEM((128, rows, vocab_rows), jnp.float32),
            VMEM((128, rows, 128), jnp.float32),
            VMEM((128, rows, 128), jnp.float32),
            VMEM((8, 16, 16 * rows), jnp.float32),
            VMEM((8, 16, 16 * rows), jnp.float32),
            VMEM((16, 16 * rows), jnp.float32),
            VMEM((16, 16, 16 * rows), jnp.float32),
            dma((3,)),
            dma((3, 3)), dma((3, 3)),
            dma((3, 4)), dma((3, 4)),
            dma((3, 4, 4)), dma((3, 4, 4)),
            dma((3, 4)), dma((3, 4)),
            dma((3, 4, 4)), dma((3, 4, 4)),
            dma((8,)), dma((8,)),
            dma((16,)), dma((16,)),
        ],
        compiler_params=pltpu.CompilerParams(
            collective_id=2, has_side_effects=True, vmem_limit_bytes=60 * 2**20
        ),
        name="vocab_stats",
    )(fin, table, actions.reshape(128, rows, 1))


A_COLS = 512


def layer_kernel(
    send_slot, keep_from, row_of, slot_of,
    residual_ref, stored_ref, cos_ref, sin_ref, start_ref,
    in_gain, q_gain, k_gain, post_gain, final_gain, out_ref,
    out_a, out_b, in_a, in_b, held_a, held_b, cols, proj, kv, query, mixed, wout,
    half_out, half_in, part_out, part_in, summed,
    xa_s, xa_r, xb_s, xb_r,
    ya_s, ya_r, za_s, za_r, fa_s, fa_r,
    yb_s, yb_r, zb_s, zb_r, fb_s, fb_r,
    h_s, h_r, c_s, c_r, p_s, p_r,
):
    ctx = lax.axis_index("ctx")
    tp = lax.axis_index("tp")
    core = tp % 2
    chip = tp // 2
    y_hi, z = ctx // 4, ctx % 4
    n_blk = stored_ref.shape[0]
    blk_rows = stored_ref.shape[1]
    tokens, depth = residual_ref.shape
    head = q_gain.shape[1]

    def send(src, dst, send_sem, recv_sem, peer):
        return pltpu.make_async_remote_copy(
            src_ref=src, dst_ref=dst, send_sem=send_sem, recv_sem=recv_sem,
            device_id=peer, device_id_type=MESH,
        )

    t_peer = lambda off: (ctx, (tp + off) % 16)
    z_peer = lambda step: (y_hi * 4 + (z + step) % 4, tp)
    y_peer = ((ctx + 4) % 8, tp)

    def swap(out, got, ss, rs, off):
        return send(out.at[(tp + off) % 16], got.at[tp], ss.at[off], rs.at[off], t_peer(off))

    def stage(t, carry):
        block = stored_ref[send_slot[t]]
        out_a[t] = block[:, :A_COLS]
        out_b[t] = block[:, A_COLS:]
        return carry

    lax.fori_loop(0, 16, stage, 0)
    greet([((ctx + o) % 8, tp) for o in range(1, 8)] + [t_peer(o) for o in range(1, 16)])

    def start_a(off, carry):
        swap(out_a, in_a, xa_s, xa_r, off).start()
        return carry

    lax.fori_loop(1, 16, start_a, 0)
    in_a[tp] = out_a[tp]
    in_b[tp] = out_b[tp]

    step_rows = 32

    def norm_rows(i, carry):
        at = pl.ds(pl.multiple_of(i * step_rows, step_rows), step_rows)
        x = residual_ref[at].astype(jnp.float32)
        scale = lax.rsqrt(jnp.mean(x * x, axis=-1, keepdims=True) + epsilon)
        n = (x * scale * in_gain[...]).astype(jnp.bfloat16)
        for r in range(depth // blk_rows):
            cols[r, at, :blk_rows] = n[:, r * blk_rows:(r + 1) * blk_rows]
        return carry

    lax.fori_loop(0, tokens // step_rows, norm_rows, 0)
    proj[...] = jnp.zeros_like(proj)

    class Gather:
        def __init__(self, held, got, ys, yr, zs, zr, fs, fr):
            self.held, self.got = held, got
            self.ys, self.yr, self.zs, self.zr, self.fs, self.fr = ys, yr, zs, zr, fs, fr

        def y(self, k):
            return send(self.held.at[0, 0, k], self.held.at[1, 0, k], self.ys.at[k], self.yr.at[k], y_peer)

        def z(self, yy, step, k):
            i = 0 if step == 1 else 1
            return send(
                self.held.at[yy, 0, k], self.held.at[yy, (4 - step) % 4, k],
                self.zs.at[yy, i, k], self.zr.at[yy, i, k], z_peer(step),
            )

        def f(self, yy, step, k):
            return send(
                self.held.at[yy, 3 if step == 1 else 1, k], self.held.at[yy, 2, k],
                self.fs.at[yy, k], self.fr.at[yy, k], z_peer(step),
            )

        def own(self, k):
            self.held[0, 0, k] = self.got[keep_from[k]]
            self.y(k).start()
            self.z(0, 1, k).start()
            self.z(0, 3, k).start()

        def partner(self, k):
            self.y(k).wait_recv()
            self.z(1, 1, k).start()
            self.z(1, 3, k).start()

        def side(self, yy, k):
            right = k < 4 - yy
            self.z(yy, 1, k).wait_recv()

            @pl.when(right)
            def _():
                self.f(yy, 1, k).start()

            self.z(yy, 3, k).wait_recv()

            @pl.when(jnp.logical_not(right))
            def _():
                self.f(yy, 3, k).start()

        def far(self, yy, k):
            self.f(yy, 1, k).wait_recv()

        def sent(self, k):
            self.y(k).wait_send()
            for yy in range(2):
                self.z(yy, 1, k).wait_send()
                self.z(yy, 3, k).wait_send()
                self.f(yy, 1, k).wait_send()

    ga = Gather(held_a, in_a, ya_s, ya_r, za_s, za_r, fa_s, fa_r)
    gb = Gather(held_b, in_b, yb_s, yb_r, zb_s, zb_r, fb_s, fb_r)

    def term(yy, zz, k):
        c = (y_hi + yy) % 2 * 4 + (z + zz) % 4
        r = row_of[c * n_blk + k]
        proj[...] += jnp.dot(
            cols[r, :, :blk_rows], held_a[yy, zz, k], preferred_element_type=jnp.float32
        )

    def each_block(body):
        def run(k, carry):
            body(k)
            return carry

        lax.fori_loop(0, n_blk, run, 0)

    def wait_a(off, carry):
        swap(out_a, in_a, xa_s, xa_r, off).wait_recv()
        return carry

    lax.fori_loop(1, 16, wait_a, 0)
    each_block(ga.own)

    def start_b(off, carry):
        swap(out_b, in_b, xb_s, xb_r, off).start()
        return carry

    lax.fori_loop(1, 16, start_b, 0)

    def one(k):
        ga.partner(k)
        term(0, 0, k)

    def two(k):
        ga.side(0, k)
        term(0, 3, k)
        term(0, 1, k)

    def three(k):
        ga.side(1, k)
        term(1, 0, k)
        term(1, 3, k)
        term(1, 1, k)

    def four(yy):
        def run(k):
            ga.far(yy, k)
            term(yy, 2, k)

        return run

    each_block(one)
    each_block(two)
    each_block(three)

    def wait_b(off, carry):
        swap(out_b, in_b, xb_s, xb_r, off).wait_recv()
        return carry

    lax.fori_loop(1, 16, wait_b, 0)
    each_block(gb.own)
    each_block(four(0))
    each_block(gb.partner)
    each_block(four(1))

    def heads(at, gain):
        e = proj[:, pl.ds(at * head, head)]
        scale = lax.rsqrt(jnp.mean(e * e, axis=-1, keepdims=True) + epsilon)
        e = e * scale * gain[...]
        return (e * cos_ref[...] + pltpu.roll(e, head // 2, 1) * sin_ref[...]).astype(jnp.bfloat16)

    reach = kv.shape[0] - 1
    kv[reach, :, :head] = heads(2, k_gain)
    kv[reach, :, head:] = proj[:, 3 * head:].astype(jnp.bfloat16)

    def halo(step):
        return send(
            kv.at[reach], kv.at[reach - step], h_s.at[step - 1], h_r.at[step - 1],
            ((ctx + step) % 8, tp),
        )

    for step in range(1, reach + 1):
        @pl.when(ctx + step < 8)
        def _():
            halo(step).start()

        @pl.when(ctx < step)
        def _():
            kv[reach - step] = jnp.zeros(kv.shape[1:], kv.dtype)

    for h in range(2):
        query[h] = heads(h, q_gain)
    for yy in range(2):
        each_block(lambda k: gb.side(yy, k))
    for step in range(1, reach + 1):
        @pl.when(ctx >= step)
        def _():
            halo(step).wait_recv()

    span = (reach + 1) * tokens
    key_rows = kv[:, :, :head].reshape(span, head)
    value_rows = kv[:, :, head:].reshape(span, head)
    q_ids = ctx * tokens + lax.broadcasted_iota(jnp.int32, (tokens, span), 0)
    k_ids = (ctx - reach) * tokens + lax.broadcasted_iota(jnp.int32, (tokens, span), 1)
    visible = (k_ids <= q_ids) & (q_ids - k_ids < WINDOW) & (k_ids >= start_ref[...])
    for h in range(2):
        scores = lax.dot_general(
            query[h], key_rows, (((1,), (1,)), ((), ())), preferred_element_type=jnp.float32
        ) * QUERY_SCALAR ** (-0.5)
        probs = jnp.where(visible, jnp.exp(scores), 0.0)
        probs = (probs / jnp.sum(probs, axis=1, keepdims=True)).astype(jnp.bfloat16)
        got = jnp.dot(probs, value_rows, preferred_element_type=jnp.float32).astype(jnp.bfloat16)
        mixed[:, :, :, h * head:(h + 1) * head] = got.reshape(8, 2, tokens // 16, head)

    for yy in range(2):
        each_block(lambda k: gb.far(yy, k))

    def order(r, carry):
        wout[r] = held_b.reshape(8 * n_blk, blk_rows, 2 * head)[slot_of[r]]
        return carry

    lax.fori_loop(0, depth // blk_rows, order, 0)

    share = tokens // 16
    per = wout.shape[0] // half_out.shape[0]
    piece = per * blk_rows
    other = (tp // 2) * 2 + (1 - core)

    def product(which, n):
        rows = mixed[:, which].reshape(8 * share, 2 * head)
        block = wout[pl.ds(n * per, per)].reshape(piece, 2 * head)
        return lax.dot_general(
            rows, block, (((1,), (1,)), ((), ())), preferred_element_type=jnp.float32
        ).reshape(8, share, piece)

    def between(n):
        return send(half_out.at[n], half_in.at[n], c_s.at[n], c_r.at[n], (ctx, other))

    def to_chip(n, off):
        there = (chip + off) % 8
        return send(
            part_out.at[n, there], part_in.at[n, off], p_s.at[n, off], p_r.at[n, off],
            (ctx, there * 2 + core),
        )

    n_pieces = half_out.shape[0]

    def give(n, carry):
        half_out[n] = product(1 - core, n).astype(jnp.bfloat16)
        between(n).start()
        return carry

    def take(n, carry):
        mine = product(core, n)
        between(n).wait_recv()
        part_out[n] = (mine + half_in[n].astype(jnp.float32)).astype(jnp.bfloat16)
        for off in range(1, 8):
            to_chip(n, off).start()
        return carry

    lax.fori_loop(0, n_pieces, give, 0)
    lax.fori_loop(0, n_pieces, take, 0)
    for n in range(n_pieces):
        total = part_out[n, chip].astype(jnp.float32)
        for off in range(1, 8):
            to_chip(n, off).wait_recv()
            total = total + part_in[n, off].astype(jnp.float32)
        summed[:, n * piece:(n + 1) * piece] = total

    def rms(values, gain):
        return values * lax.rsqrt(jnp.mean(values * values, axis=-1, keepdims=True) + epsilon) * gain[...]

    mine = residual_ref[pl.ds(pl.multiple_of(tp * share, share), share)].astype(jnp.float32)
    hidden = mine + rms(summed[...], post_gain)
    out_ref[...] = rms(hidden, final_gain).astype(jnp.bfloat16)

    def swapped(off, carry):
        swap(out_a, in_a, xa_s, xa_r, off).wait_send()
        swap(out_b, in_b, xb_s, xb_r, off).wait_send()
        return carry

    lax.fori_loop(1, 16, swapped, 0)
    each_block(ga.sent)
    each_block(gb.sent)
    for step in range(1, reach + 1):
        @pl.when(ctx + step < 8)
        def _():
            halo(step).wait_send()

    def parts_sent(n, carry):
        between(n).wait_send()
        for off in range(1, 8):
            to_chip(n, off).wait_send()
        return carry

    lax.fori_loop(0, n_pieces, parts_sent, 0)


def layer(
    send_slot, keep_from, row_of, slot_of, residual, stored, cosine, sine, seg_start,
    in_gain, q_gain, k_gain, post_gain, final_gain,
):
    tokens, depth = residual.shape
    n_blk, blk_rows, width = stored.shape
    head = q_gain.shape[0]
    share = tokens // 16
    bf16 = jnp.bfloat16
    n_rows = depth // blk_rows
    n_pieces = 7
    piece = depth // n_pieces
    reach = WINDOW // tokens
    dma = pltpu.SemaphoreType.DMA
    b_cols = width - A_COLS
    smem = pl.BlockSpec(memory_space=pltpu.SMEM)
    vmem = pl.BlockSpec(memory_space=VMEM)
    gather_sems = [dma((n_blk,))] * 2 + [dma((2, 2, n_blk))] * 2 + [dma((2, n_blk))] * 2
    return pl.pallas_call(
        layer_kernel,
        out_shape=jax.ShapeDtypeStruct((share, depth), bf16),
        in_specs=[smem] * 4 + [vmem] * 10,
        out_specs=vmem,
        scratch_shapes=[
            VMEM((16, blk_rows, A_COLS), bf16),
            VMEM((16, blk_rows, b_cols), bf16),
            VMEM((16, blk_rows, A_COLS), bf16),
            VMEM((16, blk_rows, b_cols), bf16),
            VMEM((2, 4, n_blk, blk_rows, A_COLS), bf16),
            VMEM((2, 4, n_blk, blk_rows, b_cols), bf16),
            VMEM((n_rows, tokens, 128), bf16),
            VMEM((tokens, A_COLS), jnp.float32),
            VMEM((reach + 1, tokens, 2 * head), bf16),
            VMEM((2, tokens, head), bf16),
            VMEM((8, 2, share, 2 * head), bf16),
            VMEM((n_rows, blk_rows, b_cols), bf16),
            VMEM((n_pieces, 8, share, piece), bf16),
            VMEM((n_pieces, 8, share, piece), bf16),
            VMEM((n_pieces, 8, share, piece), bf16),
            VMEM((n_pieces, 8, share, piece), bf16),
            VMEM((share, depth), jnp.float32),
        ]
        + [dma((16,))] * 4
        + gather_sems * 2
        + [dma((reach,))] * 2
        + [dma((n_pieces,))] * 2
        + [dma((n_pieces, 8))] * 2,
        compiler_params=pltpu.CompilerParams(
            collective_id=1, has_side_effects=True, vmem_limit_bytes=60 * 2**20
        ),
        name="layer",
    )(
        send_slot, keep_from, row_of, slot_of, residual, stored, cosine, sine, seg_start[:, None],
        in_gain[None], q_gain[None], k_gain[None], post_gain[None], final_gain[None],
    )


def rope_tables(position, head):
    half_size = head // 2
    frequency = rope_base ** (-2.0 * jnp.arange(half_size, dtype=jnp.float32) / head)
    angle_rows = position.astype(jnp.float32)[:, None] * frequency[None, :]
    cosine, sine = jnp.cos(angle_rows), jnp.sin(angle_rows)
    return (
        jnp.concatenate([cosine, cosine], axis=-1),
        jnp.concatenate([-sine, sine], axis=-1),
    )


def block_tables(block_list, ctx_index, tp_index, ctx_count, tp_count, blocks_dev):
    rows_per_reader = blocks_dev * ctx_count
    grid = block_list.reshape(ctx_count, tp_count, blocks_dev)
    readers = grid // rows_per_reader
    my_readers = lax.dynamic_slice(
        readers, (ctx_index, tp_index, 0), (1, 1, blocks_dev)
    ).reshape(-1)
    slots = jnp.arange(blocks_dev, dtype=jnp.int32)
    sources = jnp.arange(tp_count, dtype=jnp.int32)
    send_slot = jnp.sum(jnp.where(my_readers[None, :] == sources[:, None], slots[None, :], 0), axis=1)
    hit = readers == tp_index
    present = jnp.any(hit, axis=2)
    row_index = jnp.sum(jnp.where(hit, grid % rows_per_reader, 0), axis=2)
    before = sources[None, :] < sources[:, None]
    rank = jnp.sum((present[:, None, :] & before[None]).astype(jnp.int32), axis=2)
    chosen = (rank[:, None, :] == slots[None, :, None]) & present[:, None, :]
    row_of = jnp.sum(jnp.where(chosen, row_index[:, None, :], 0), axis=2)
    keep_all = jnp.sum(jnp.where(chosen, sources[None, None, :], 0), axis=2)
    keep_from = lax.dynamic_index_in_dim(keep_all, ctx_index, 0, False)
    ids = jnp.arange(ctx_count, dtype=jnp.int32)
    side = (ids // 4 + ctx_index // 4) % 2
    slot = (side * 4 + (ids + 4 - ctx_index % 4) % 4)[:, None] * blocks_dev + slots[None, :]
    rows = jnp.arange(rows_per_reader, dtype=jnp.int32)
    slot_of = jnp.sum(jnp.where(row_of.reshape(1, -1) == rows[:, None], slot.reshape(1, -1), 0), axis=1)
    return send_slot, keep_from, row_of.reshape(-1), slot_of


def shards(
    residual,
    stored_blocks,
    block_list,
    lengths,
    in_gain,
    q_gain,
    k_gain,
    post_gain,
    final_gain,
    vocab_table,
    actions,
    old_logprob,
):
    ctx_count = lax.axis_size("ctx")
    tp_count = lax.axis_size("tp")
    ctx_index = lax.axis_index("ctx")
    tp_index = lax.axis_index("tp")
    row_count = residual.shape[0]
    share_rows = row_count // tp_count
    tables = block_tables(
        block_list, ctx_index, tp_index, ctx_count, tp_count, stored_blocks.shape[0]
    )
    seq_starts = jnp.cumsum(lengths) - lengths
    query_ids = ctx_index * row_count + jnp.arange(row_count, dtype=jnp.int32)
    seg_start = jnp.max(
        jnp.where(seq_starts[None, :] <= query_ids[:, None], seq_starts[None, :], 0), axis=1
    )
    cosine, sine = rope_tables(query_ids - seg_start, HEAD_DIM)
    final = layer(
        *tables, residual, stored_blocks, cosine, sine, seg_start,
        in_gain, q_gain, k_gain, post_gain, final_gain,
    )
    all_rows = vocab_stats(final, vocab_table, actions)
    ref_logprob = lax.dynamic_slice_in_dim(all_rows[0], tp_index * share_rows, share_rows, 0)
    return (ref_logprob, old_logprob - ref_logprob)


def solution(mesh):
    return jax.shard_map(
        shards,
        mesh=mesh,
        in_specs=(
            P("ctx", None),
            P(("ctx", "tp"), None, None),
            P(),
            P(),
            P(),
            P(),
            P(),
            P(),
            P(),
            P(("ctx", "tp"), None),
            P(),
            P(("ctx", "tp")),
        ),
        out_specs=(P(("ctx", "tp")), P(("ctx", "tp"))),
        check_vma=False,
    )
```

```python
import jax
import jax.numpy as jnp
from jax import lax
from jax.experimental import pallas as pl
from jax.experimental.pallas import tpu as pltpu
from jax.sharding import PartitionSpec as P

HEADS = 32
KV_HEADS = 16
HEAD_DIM = 128
WINDOW = 1024
QUERY_SCALAR = 168


epsilon = 1e-06
soft_cap = 30.0
rope_base = 10000.0
MESH = pl.DeviceIdType.MESH
VMEM = pltpu.VMEM
A2_REL = (0, 1, 3, 2)


def coords():
    c = lax.axis_index("ctx")
    t = lax.axis_index("tp")
    return t // 4, (c // 4) * 2 + (t // 2) % 2, c % 4, t % 2


def device_of(x, y, z, k):
    x, y, z, k = x % 4, y % 4, z % 4, k % 2
    return ((y // 2) * 4 + z, x * 4 + (y % 2) * 2 + k)


def axis_of(part, place):
    return (part + place) % 3


def shifted(axis, steps):
    where = list(coords())
    where[axis] = where[axis] + steps
    return device_of(*where)


def sibling():
    x, y, z, k = coords()
    return device_of(x, y, z, k + 1)


def greet(peers):
    barrier = pltpu.get_barrier_semaphore()
    for peer in peers:
        pl.semaphore_signal(barrier, inc=1, device_id=peer, device_id_type=MESH)
    pl.semaphore_wait(barrier, len(peers))


def vocab_kernel(
    fin_ref, table_ref, actions_ref, out_ref,
    buf, table, acc, part_exp, part_hit, column, st1, r1, st2, r2,
    table_sem, s1, v1, s2, v2, s3, v3, sf, vf, sk, vk, sa, va, sb, vb,
):
    ctx = lax.axis_index("ctx")
    tp = lax.axis_index("tp")
    core = tp % 2
    own = coords()[:3]
    width = fin_ref.shape[1] // 3
    rows = fin_ref.shape[0]
    vocab_rows = table.shape[1]

    def table_copy(p):
        return pltpu.make_async_copy(
            table_ref.at[:, pl.ds(p * width, width)], table.at[p], table_sem.at[p]
        )

    for p in range(3):
        table_copy(p).start()
    for p in range(3):
        buf[p, 0, 0, core, 0] = fin_ref[:, pl.ds(p * width, width)]
    x, y, z, k = coords()
    c_peer = lambda off: ((ctx + off) % 8, tp)
    t_peer = lambda off: (ctx, (tp + off) % 16)
    far_y = device_of(x, y - 1 + 2 * (y % 2), z, k)
    greet([c_peer(o) for o in range(1, 8)] + [t_peer(o) for o in range(1, 16)] + [far_y])

    def send(src, dst, send_sem, recv_sem, peer):
        return pltpu.make_async_remote_copy(
            src_ref=src, dst_ref=dst, send_sem=send_sem, recv_sem=recv_sem,
            device_id=peer, device_id_type=MESH,
        )

    def first(p, step):
        return send(
            buf.at[p, 0, 0, core, 0], buf.at[p, 0, 0, core, 4 - step],
            s1.at[p, step - 1], v1.at[p, step - 1], shifted(axis_of(p, 0), step),
        )

    def second(p, step):
        slot = A2_REL.index(4 - step)
        return send(
            buf.at[p, 0, 0, core], buf.at[p, 0, slot, core],
            s2.at[p, slot], v2.at[p, slot], shifted(axis_of(p, 1), step),
        )

    def third(p, q, step):
        return send(
            buf.at[p, 0, q, core], buf.at[p, 4 - step, q, core],
            s3.at[p, 4 - step, q], v3.at[p, 4 - step, q], shifted(axis_of(p, 2), step),
        )

    def passed(p, slab, q, step):
        return send(
            buf.at[p, slab, q, core], buf.at[p, 2, q, core],
            sf.at[p, q], vf.at[p, q], shifted(axis_of(p, 2), step),
        )

    def across(p, slab, q):
        return send(
            buf.at[p, slab, q, core], buf.at[p, slab, q, core],
            sk.at[p, slab, q], vk.at[p, slab, q], sibling(),
        )

    for p in range(3):
        for step in (1, 3, 2):
            first(p, step).start()
    for p in range(3):
        for step in (1, 3, 2):
            first(p, step).wait_recv()
        for step in (3, 1, 2):
            second(p, step).start()
    for p in range(3):
        for step in (1, 3):
            third(p, 0, step).start()
        across(p, 0, 0).start()

    def own_chunk(p, q):
        second(p, 4 - A2_REL[q]).wait_recv()
        for step in (1, 3):
            third(p, q, step).start()
        across(p, 0, q).start()

    for p in range(3):
        own_chunk(p, 1)

    def slab_of(g, i):
        return jnp.where(g < 2, 0, jnp.where(g > 5, 2, 3 - 2 * i))

    def row_of(g, i):
        return jnp.where(g < 2, g * 2 + i, jnp.where(g > 5, (g - 6) * 2 + i, g - 2))

    def arrivals(g):
        @pl.when(g == 1)
        def _():
            for q in (2, 3):
                for p in range(3):
                    own_chunk(p, q)

        @pl.when((g > 1) & (g < 6))
        def _():
            q = g - 2
            for p in range(3):
                third(p, q, 1).wait_recv()

                @pl.when(q % 2 == 0)
                def _():
                    passed(p, 3, q, 1).start()

                across(p, 3, q).start()
                third(p, q, 3).wait_recv()

                @pl.when(q % 2 == 1)
                def _():
                    passed(p, 1, q, 3).start()

                across(p, 1, q).start()

        @pl.when((g > 5) & (g < 8))
        def _():
            for i in range(2):
                q = (g - 6) * 2 + i
                for p in range(3):
                    passed(p, 3, q, 1).wait_recv()
                    across(p, 2, q).start()

    def place(axis_values, k):
        x, y, z = axis_values
        return ((y // 2) * 4 + z) * 16 + x * 4 + (y % 2) * 2 + k

    first_id = (ctx * 16 + tp) * vocab_rows
    ids = first_id + lax.broadcasted_iota(jnp.int32, (rows, vocab_rows), 1)

    def fold(v):
        total = v[:, :128]
        for i in range(1, vocab_rows // 128):
            total = total + v[:, i * 128:(i + 1) * 128]
        return total

    def tail(rel):
        at = place([(own[i] + rel[i]) % 4 for i in range(3)], 0)
        for kk in range(2):
            capped = soft_cap * jnp.tanh(acc[at + kk] * (1.0 / soft_cap))
            hit = ids == column[at + kk]
            part_exp[at + kk] = fold(jnp.exp(capped))
            part_hit[at + kk] = fold(jnp.where(hit, capped, 0.0))

    def near(digit):
        return digit + digit // 2

    def early_tail(i, carry):
        for j in range(3):
            tail((near(i // 3), near(i % 3), near(j)))
        return carry

    def late_x(i, carry):
        for j in range(4):
            tail((2, i, j))
        return carry

    def late_y(i, carry):
        for j in range(4):
            tail((near(i), 2, j))
        return carry

    def late_z(i, carry):
        for j in range(3):
            tail((near(i), near(j), 2))
        return carry

    def group(g, carry):
        slabs, lines = [slab_of(g, i) for i in range(2)], [row_of(g, i) for i in range(2)]
        for p in range(3):
            for i in range(2):
                across(p, slabs[i], lines[i]).wait_recv()

            @pl.when(g == 0)
            def _():
                table_copy(p).wait()

            lhs = jnp.concatenate(
                [buf[p, slabs[i], lines[i]].reshape(8 * rows, width) for i in range(2)], axis=0
            )
            got = lax.dot_general(
                lhs, table[p], (((1,), (1,)), ((), ())), preferred_element_type=jnp.float32
            )
            a1, a2, a3 = (axis_of(p, i) for i in range(3))
            for i in range(2):
                rel2 = jnp.where(lines[i] < 2, lines[i], 5 - lines[i])
                for kk in range(2):
                    for r1_ in range(4):
                        at = [None] * 3
                        at[a1] = (own[a1] + r1_) % 4
                        at[a2] = (own[a2] + rel2) % 4
                        at[a3] = (own[a3] + slabs[i]) % 4
                        d = place(at, kk)
                        m = (i * 2 + kk) * 4 + r1_
                        value = got[m * rows:(m + 1) * rows]
                        acc[d] = acc[d] + value
            if p == 0:
                @pl.when(g == 6)
                def _():
                    lax.fori_loop(0, 9, early_tail, 0)

                arrivals(g + 1)
        return carry

    def clear(d, carry):
        acc[d] = jnp.zeros((rows, vocab_rows), jnp.float32)
        return carry

    lax.fori_loop(0, 128, clear, 0)
    lanes = lax.broadcasted_iota(jnp.int32, (128, 128), 1)
    diagonal = lax.broadcasted_iota(jnp.int32, (128, 128), 0) == lanes

    def turn(j, carry):
        line = jnp.broadcast_to(actions_ref[pl.ds(j, 1)].astype(jnp.float32), (128, 128))
        turned = jnp.sum(jnp.where(diagonal, line, 0.0), axis=1, keepdims=True)
        column[pl.ds(j * 8, 8)] = turned.astype(jnp.int32).reshape(8, rows, 1)
        return carry

    lax.fori_loop(0, actions_ref.shape[0], turn, 0)
    lax.fori_loop(0, 8, group, 0)

    lax.fori_loop(0, 4, late_x, 0)
    lax.fori_loop(0, 3, late_y, 0)
    lax.fori_loop(0, 3, late_z, 0)
    ones = jnp.ones((8, 128), jnp.float32)
    for c in range(8):
        sums = [
            lax.dot_general(
                ones, part[pl.ds(c * 16, 16)].reshape(16 * rows, 128), (((1,), (1,)), ((), ())),
                preferred_element_type=jnp.float32, precision=lax.Precision.HIGHEST,
            )
            for part in (part_exp, part_hit)
        ]
        st1[c] = jnp.concatenate(
            [v[:1, i * 128:(i + 1) * 128] for v in (sums + sums) for i in range(2)], axis=0
        )

    def stage1(off):
        return send(st1.at[(ctx + off) % 8], r1.at[off], sa.at[off], va.at[off], c_peer(off))

    def stage2(off):
        return send(st2, r2.at[off], sb.at[off], vb.at[off], t_peer(off))

    for off in range(1, 8):
        stage1(off).start()
    total = st1[ctx]
    for off in range(1, 8):
        stage1(off).wait_recv()
        total = total + r1[off]
    st2[...] = total
    for off in range(1, 16):
        stage2(off).start()
    for off in range(1, 16):
        stage2(off).wait_recv()
        total = total + r2[off]
    out_ref[...] = total[2:4] - jnp.log(total[:2])

    for p in range(3):
        for step in (1, 2, 3):
            first(p, step).wait_send()
            second(p, step).wait_send()
        for q in range(4):
            third(p, q, 1).wait_send()
            third(p, q, 3).wait_send()
            passed(p, 3, q, 1).wait_send()
            for slab in range(4):
                across(p, slab, q).wait_send()
    for off in range(1, 8):
        stage1(off).wait_send()
    for off in range(1, 16):
        stage2(off).wait_send()


def vocab_stats(fin, table, actions):
    rows, depth = fin.shape
    width = depth // 3
    vocab_rows = table.shape[0]
    dma = pltpu.SemaphoreType.DMA
    return pl.pallas_call(
        vocab_kernel,
        out_shape=jax.ShapeDtypeStruct((2, 128), jnp.float32),
        in_specs=[
            pl.BlockSpec(memory_space=VMEM),
            pl.BlockSpec(memory_space=pl.ANY),
            pl.BlockSpec(memory_space=VMEM),
        ],
        out_specs=pl.BlockSpec(memory_space=VMEM),
        scratch_shapes=[
            VMEM((3, 4, 4, 2, 4, rows, width), jnp.bfloat16),
            VMEM((3, vocab_rows, width), jnp.bfloat16),
            VMEM((128, rows, vocab_rows), jnp.float32),
            VMEM((128, rows, 128), jnp.float32),
            VMEM((128, rows, 128), jnp.float32),
            VMEM((128, rows, 1), jnp.int32),
            VMEM((8, 8, 128), jnp.float32),
            VMEM((8, 8, 128), jnp.float32),
            VMEM((8, 128), jnp.float32),
            VMEM((16, 8, 128), jnp.float32),
            dma((3,)),
            dma((3, 3)), dma((3, 3)),
            dma((3, 4)), dma((3, 4)),
            dma((3, 4, 4)), dma((3, 4, 4)),
            dma((3, 4)), dma((3, 4)),
            dma((3, 4, 4)), dma((3, 4, 4)),
            dma((8,)), dma((8,)),
            dma((16,)), dma((16,)),
        ],
        compiler_params=pltpu.CompilerParams(
            collective_id=2, has_side_effects=True, vmem_limit_bytes=60 * 2**20
        ),
        name="vocab_stats",
    )(fin, table, actions.reshape(-1, 128))


A_COLS = 512


def layer_kernel(
    send_slot, keep_from, row_of, slot_of,
    lengths, residual_ref, stored_ref, frequency, in_lines, post_lines, final_lines, q_gain, k_gain, out_ref,
    in_gain, post_gain, final_gain, cos_ref, sin_ref,
    out_a, out_b, in_a, in_b, held_a, held_b, cols, proj, kv, query, mixed, wout,
    half_out, half_in, part_out, part_in, summed,
    xa_s, xa_r, xb_s, xb_r,
    ya_s, ya_r, za_s, za_r, fa_s, fa_r,
    yb_s, yb_r, zb_s, zb_r, fb_s, fb_r,
    h_s, h_r, c_s, c_r, p_s, p_r,
):
    ctx = lax.axis_index("ctx")
    tp = lax.axis_index("tp")
    core = tp % 2
    chip = tp // 2
    y_hi, z = ctx // 4, ctx % 4
    n_blk = stored_ref.shape[0]
    blk_rows = stored_ref.shape[1]
    tokens, depth = residual_ref.shape
    head = q_gain.shape[1]

    def send(src, dst, send_sem, recv_sem, peer):
        return pltpu.make_async_remote_copy(
            src_ref=src, dst_ref=dst, send_sem=send_sem, recv_sem=recv_sem,
            device_id=peer, device_id_type=MESH,
        )

    t_peer = lambda off: (ctx, (tp + off) % 16)
    z_peer = lambda step: (y_hi * 4 + (z + step) % 4, tp)
    y_peer = ((ctx + 4) % 8, tp)

    def swap(out, got, ss, rs, off):
        return send(out.at[(tp + off) % 16], got.at[tp], ss.at[off], rs.at[off], t_peer(off))

    def stage(t, carry):
        block = stored_ref[send_slot[t]]
        out_a[t] = block[:, :A_COLS]
        out_b[t] = block[:, A_COLS:]
        return carry

    lax.fori_loop(0, 16, stage, 0)
    greet([((ctx + o) % 8, tp) for o in range(1, 8)] + [t_peer(o) for o in range(1, 16)])

    def start_a(off, carry):
        swap(out_a, in_a, xa_s, xa_r, off).start()
        return carry

    lax.fori_loop(1, 16, start_a, 0)
    for gain, lines in ((in_gain, in_lines), (post_gain, post_lines), (final_gain, final_lines)):
        for i in range(lines.shape[0]):
            gain[:, i * 128:(i + 1) * 128] = lines[i:i + 1]
    in_a[tp] = out_a[tp]
    in_b[tp] = out_b[tp]

    step_rows = 32

    def norm_rows(i, carry):
        at = pl.ds(pl.multiple_of(i * step_rows, step_rows), step_rows)
        x = residual_ref[at].astype(jnp.float32)
        scale = lax.rsqrt(jnp.mean(x * x, axis=-1, keepdims=True) + epsilon)
        n = (x * scale * in_gain[...]).astype(jnp.bfloat16)
        for r in range(depth // blk_rows):
            cols[r, at, :blk_rows] = n[:, r * blk_rows:(r + 1) * blk_rows]
        return carry

    lax.fori_loop(0, tokens // step_rows, norm_rows, 0)
    proj[...] = jnp.zeros_like(proj)
    row_ids = ctx * tokens + lax.broadcasted_iota(jnp.int32, (tokens, 1), 0)
    seg_start = jnp.zeros_like(row_ids)
    begin = jnp.int32(0)
    for i in range(lengths.shape[0]):
        seg_start = jnp.maximum(seg_start, jnp.where(begin <= row_ids, begin, 0))
        begin = begin + lengths[i]
    angle = (row_ids - seg_start).astype(jnp.float32) * frequency[...]
    low = lax.broadcasted_iota(jnp.int32, angle.shape, 1) < head // 2
    cos_ref[...] = jnp.cos(angle)
    sin_ref[...] = jnp.where(low, -jnp.sin(angle), jnp.sin(angle))

    class Gather:
        def __init__(self, held, got, ys, yr, zs, zr, fs, fr):
            self.held, self.got = held, got
            self.ys, self.yr, self.zs, self.zr, self.fs, self.fr = ys, yr, zs, zr, fs, fr

        def y(self, k):
            return send(self.held.at[0, 0, k], self.held.at[1, 0, k], self.ys.at[k], self.yr.at[k], y_peer)

        def z(self, yy, step, k):
            i = 0 if step == 1 else 1
            return send(
                self.held.at[yy, 0, k], self.held.at[yy, (4 - step) % 4, k],
                self.zs.at[yy, i, k], self.zr.at[yy, i, k], z_peer(step),
            )

        def f(self, yy, step, k):
            return send(
                self.held.at[yy, 3 if step == 1 else 1, k], self.held.at[yy, 2, k],
                self.fs.at[yy, k], self.fr.at[yy, k], z_peer(step),
            )

        def own(self, k):
            self.held[0, 0, k] = self.got[keep_from[k]]
            self.y(k).start()
            self.z(0, 1, k).start()
            self.z(0, 3, k).start()

        def partner(self, k):
            self.y(k).wait_recv()
            self.z(1, 1, k).start()
            self.z(1, 3, k).start()

        def side(self, yy, k):
            right = k < 4 - yy
            self.z(yy, 1, k).wait_recv()

            @pl.when(right)
            def _():
                self.f(yy, 1, k).start()

            self.z(yy, 3, k).wait_recv()

            @pl.when(jnp.logical_not(right))
            def _():
                self.f(yy, 3, k).start()

        def far(self, yy, k):
            self.f(yy, 1, k).wait_recv()

        def sent(self, k):
            self.y(k).wait_send()
            for yy in range(2):
                self.z(yy, 1, k).wait_send()
                self.z(yy, 3, k).wait_send()
                self.f(yy, 1, k).wait_send()

    ga = Gather(held_a, in_a, ya_s, ya_r, za_s, za_r, fa_s, fa_r)
    gb = Gather(held_b, in_b, yb_s, yb_r, zb_s, zb_r, fb_s, fb_r)

    def term(yy, zz, k):
        c = (y_hi + yy) % 2 * 4 + (z + zz) % 4
        r = row_of[c * n_blk + k]
        proj[...] += jnp.dot(
            cols[r, :, :blk_rows], held_a[yy, zz, k], preferred_element_type=jnp.float32
        )

    def each_block(body):
        def run(k, carry):
            body(k)
            return carry

        lax.fori_loop(0, n_blk, run, 0)

    def wait_a(off, carry):
        swap(out_a, in_a, xa_s, xa_r, off).wait_recv()
        return carry

    lax.fori_loop(1, 16, wait_a, 0)
    each_block(ga.own)

    def start_b(off, carry):
        swap(out_b, in_b, xb_s, xb_r, off).start()
        return carry

    lax.fori_loop(1, 16, start_b, 0)

    def one(k):
        ga.partner(k)
        term(0, 0, k)

    def two(k):
        ga.side(0, k)
        term(0, 3, k)
        term(0, 1, k)

    def three(k):
        ga.side(1, k)
        term(1, 0, k)
        term(1, 3, k)
        term(1, 1, k)

    def four(yy):
        def run(k):
            ga.far(yy, k)
            term(yy, 2, k)

        return run

    each_block(one)
    each_block(two)
    each_block(three)

    def wait_b(off, carry):
        swap(out_b, in_b, xb_s, xb_r, off).wait_recv()
        return carry

    lax.fori_loop(1, 16, wait_b, 0)
    each_block(gb.own)
    each_block(four(0))
    each_block(gb.partner)
    each_block(four(1))

    def heads(at, gain):
        e = proj[:, pl.ds(at * head, head)]
        scale = lax.rsqrt(jnp.mean(e * e, axis=-1, keepdims=True) + epsilon)
        e = e * scale * gain[...]
        return (e * cos_ref[...] + pltpu.roll(e, head // 2, 1) * sin_ref[...]).astype(jnp.bfloat16)

    reach = kv.shape[0] - 1
    kv[reach, :, :head] = heads(2, k_gain)
    kv[reach, :, head:] = proj[:, 3 * head:].astype(jnp.bfloat16)

    def halo(step):
        return send(
            kv.at[reach], kv.at[reach - step], h_s.at[step - 1], h_r.at[step - 1],
            ((ctx + step) % 8, tp),
        )

    for step in range(1, reach + 1):
        @pl.when(ctx + step < 8)
        def _():
            halo(step).start()

        @pl.when(ctx < step)
        def _():
            kv[reach - step] = jnp.zeros(kv.shape[1:], kv.dtype)

    for h in range(2):
        query[h] = heads(h, q_gain)
    for yy in range(2):
        each_block(lambda k: gb.side(yy, k))
    for step in range(1, reach + 1):
        @pl.when(ctx >= step)
        def _():
            halo(step).wait_recv()

    span = (reach + 1) * tokens
    key_rows = kv[:, :, :head].reshape(span, head)
    value_rows = kv[:, :, head:].reshape(span, head)
    q_ids = ctx * tokens + lax.broadcasted_iota(jnp.int32, (tokens, span), 0)
    k_ids = (ctx - reach) * tokens + lax.broadcasted_iota(jnp.int32, (tokens, span), 1)
    visible = (k_ids <= q_ids) & (q_ids - k_ids < WINDOW) & (k_ids >= seg_start)
    for h in range(2):
        scores = lax.dot_general(
            query[h], key_rows, (((1,), (1,)), ((), ())), preferred_element_type=jnp.float32
        ) * QUERY_SCALAR ** (-0.5)
        probs = jnp.where(visible, jnp.exp(scores), 0.0)
        probs = (probs / jnp.sum(probs, axis=1, keepdims=True)).astype(jnp.bfloat16)
        got = jnp.dot(probs, value_rows, preferred_element_type=jnp.float32).astype(jnp.bfloat16)
        mixed[:, :, :, h * head:(h + 1) * head] = got.reshape(8, 2, tokens // 16, head)

    for yy in range(2):
        each_block(lambda k: gb.far(yy, k))

    def order(r, carry):
        wout[r] = held_b.reshape(8 * n_blk, blk_rows, 2 * head)[slot_of[r]]
        return carry

    lax.fori_loop(0, depth // blk_rows, order, 0)

    share = tokens // 16
    per = wout.shape[0] // half_out.shape[0]
    piece = per * blk_rows
    other = (tp // 2) * 2 + (1 - core)

    def product(which, n):
        rows = mixed[:, which].reshape(8 * share, 2 * head)
        block = wout[pl.ds(n * per, per)].reshape(piece, 2 * head)
        return lax.dot_general(
            rows, block, (((1,), (1,)), ((), ())), preferred_element_type=jnp.float32
        ).reshape(8, share, piece)

    def between(n):
        return send(half_out.at[n], half_in.at[n], c_s.at[n], c_r.at[n], (ctx, other))

    def to_chip(n, off):
        there = (chip + off) % 8
        return send(
            part_out.at[n, there], part_in.at[n, off], p_s.at[n, off], p_r.at[n, off],
            (ctx, there * 2 + core),
        )

    n_pieces = half_out.shape[0]

    def give(n, carry):
        half_out[n] = product(1 - core, n).astype(jnp.bfloat16)
        between(n).start()
        return carry

    def take(n, carry):
        mine = product(core, n)
        between(n).wait_recv()
        part_out[n] = (mine + half_in[n].astype(jnp.float32)).astype(jnp.bfloat16)
        for off in range(1, 8):
            to_chip(n, off).start()
        return carry

    lax.fori_loop(0, n_pieces, give, 0)
    lax.fori_loop(0, n_pieces, take, 0)
    for n in range(n_pieces):
        total = part_out[n, chip].astype(jnp.float32)
        for off in range(1, 8):
            to_chip(n, off).wait_recv()
            total = total + part_in[n, off].astype(jnp.float32)
        summed[:, n * piece:(n + 1) * piece] = total

    def rms(values, gain):
        return values * lax.rsqrt(jnp.mean(values * values, axis=-1, keepdims=True) + epsilon) * gain[...]

    mine = residual_ref[pl.ds(pl.multiple_of(tp * share, share), share)].astype(jnp.float32)
    hidden = mine + rms(summed[...], post_gain)
    out_ref[...] = rms(hidden, final_gain).astype(jnp.bfloat16)

    def swapped(off, carry):
        swap(out_a, in_a, xa_s, xa_r, off).wait_send()
        swap(out_b, in_b, xb_s, xb_r, off).wait_send()
        return carry

    lax.fori_loop(1, 16, swapped, 0)
    each_block(ga.sent)
    each_block(gb.sent)
    for step in range(1, reach + 1):
        @pl.when(ctx + step < 8)
        def _():
            halo(step).wait_send()

    def parts_sent(n, carry):
        between(n).wait_send()
        for off in range(1, 8):
            to_chip(n, off).wait_send()
        return carry

    lax.fori_loop(0, n_pieces, parts_sent, 0)


def layer(
    send_slot, keep_from, row_of, slot_of, lengths, residual, stored, frequency,
    in_gain, q_gain, k_gain, post_gain, final_gain,
):
    tokens, depth = residual.shape
    n_blk, blk_rows, width = stored.shape
    head = q_gain.shape[0]
    share = tokens // 16
    bf16 = jnp.bfloat16
    n_rows = depth // blk_rows
    n_pieces = 7
    piece = depth // n_pieces
    reach = WINDOW // tokens
    dma = pltpu.SemaphoreType.DMA
    b_cols = width - A_COLS
    smem = pl.BlockSpec(memory_space=pltpu.SMEM)
    vmem = pl.BlockSpec(memory_space=VMEM)
    gather_sems = [dma((n_blk,))] * 2 + [dma((2, 2, n_blk))] * 2 + [dma((2, n_blk))] * 2
    return pl.pallas_call(
        layer_kernel,
        out_shape=jax.ShapeDtypeStruct((share, depth), bf16),
        in_specs=[smem] * 5 + [vmem] * 8,
        out_specs=vmem,
        scratch_shapes=[VMEM((1, depth), jnp.float32)] * 3
        + [VMEM((tokens, head), jnp.float32)] * 2
        + [
            VMEM((16, blk_rows, A_COLS), bf16),
            VMEM((16, blk_rows, b_cols), bf16),
            VMEM((16, blk_rows, A_COLS), bf16),
            VMEM((16, blk_rows, b_cols), bf16),
            VMEM((2, 4, n_blk, blk_rows, A_COLS), bf16),
            VMEM((2, 4, n_blk, blk_rows, b_cols), bf16),
            VMEM((n_rows, tokens, 128), bf16),
            VMEM((tokens, A_COLS), jnp.float32),
            VMEM((reach + 1, tokens, 2 * head), bf16),
            VMEM((2, tokens, head), bf16),
            VMEM((8, 2, share, 2 * head), bf16),
            VMEM((n_rows, blk_rows, b_cols), bf16),
            VMEM((n_pieces, 8, share, piece), bf16),
            VMEM((n_pieces, 8, share, piece), bf16),
            VMEM((n_pieces, 8, share, piece), bf16),
            VMEM((n_pieces, 8, share, piece), bf16),
            VMEM((share, depth), jnp.float32),
        ]
        + [dma((16,))] * 4
        + gather_sems * 2
        + [dma((reach,))] * 2
        + [dma((n_pieces,))] * 2
        + [dma((n_pieces, 8))] * 2,
        compiler_params=pltpu.CompilerParams(
            collective_id=1, has_side_effects=True, vmem_limit_bytes=60 * 2**20
        ),
        name="layer",
    )(
        send_slot, keep_from, row_of, slot_of, lengths, residual, stored, frequency,
        in_gain.reshape(-1, 128), post_gain.reshape(-1, 128), final_gain.reshape(-1, 128),
        q_gain[None], k_gain[None],
    )


def rope_frequency(head):
    half_size = head // 2
    frequency = rope_base ** (-2.0 * jnp.arange(half_size, dtype=jnp.float32) / head)
    return jnp.concatenate([frequency, frequency])[None]


def block_tables(block_list, ctx_index, tp_index, ctx_count, tp_count, blocks_dev):
    rows_per_reader = blocks_dev * ctx_count
    grid = block_list.reshape(ctx_count, tp_count, blocks_dev)
    readers = (grid * 1171) >> 16
    my_readers = lax.dynamic_slice(
        readers, (ctx_index, tp_index, 0), (1, 1, blocks_dev)
    ).reshape(-1)
    slots = jnp.arange(blocks_dev, dtype=jnp.int32)
    sources = jnp.arange(tp_count, dtype=jnp.int32)
    send_slot = jnp.sum(jnp.where(my_readers[None, :] == sources[:, None], slots[None, :], 0), axis=1)
    hit = readers == tp_index
    present = jnp.any(hit, axis=2)
    row_index = jnp.sum(jnp.where(hit, grid - readers * rows_per_reader, 0), axis=2)
    before = sources[None, :] < sources[:, None]
    rank = jnp.sum((present[:, None, :] & before[None]).astype(jnp.int32), axis=2)
    chosen = (rank[:, None, :] == slots[None, :, None]) & present[:, None, :]
    row_of = jnp.sum(jnp.where(chosen, row_index[:, None, :], 0), axis=2)
    keep_all = jnp.sum(jnp.where(chosen, sources[None, None, :], 0), axis=2)
    keep_from = lax.dynamic_index_in_dim(keep_all, ctx_index, 0, False)
    ids = jnp.arange(ctx_count, dtype=jnp.int32)
    side = (ids // 4 + ctx_index // 4) % 2
    slot = (side * 4 + (ids + 4 - ctx_index % 4) % 4)[:, None] * blocks_dev + slots[None, :]
    rows = jnp.arange(rows_per_reader, dtype=jnp.int32)
    slot_of = jnp.sum(jnp.where(row_of.reshape(1, -1) == rows[:, None], slot.reshape(1, -1), 0), axis=1)
    return send_slot, keep_from, row_of.reshape(-1), slot_of


def shards(
    residual,
    stored_blocks,
    block_list,
    lengths,
    in_gain,
    q_gain,
    k_gain,
    post_gain,
    final_gain,
    vocab_table,
    actions,
    old_logprob,
):
    ctx_count = lax.axis_size("ctx")
    tp_count = lax.axis_size("tp")
    ctx_index = lax.axis_index("ctx")
    tp_index = lax.axis_index("tp")
    row_count = residual.shape[0]
    share_rows = row_count // tp_count
    tables = block_tables(
        block_list, ctx_index, tp_index, ctx_count, tp_count, stored_blocks.shape[0]
    )
    final = layer(
        *tables, lengths, residual, stored_blocks, rope_frequency(HEAD_DIM),
        in_gain, q_gain, k_gain, post_gain, final_gain,
    )
    all_rows = vocab_stats(final, vocab_table, actions)
    ref_logprob = lax.dynamic_slice_in_dim(all_rows.reshape(-1), tp_index * share_rows, share_rows, 0)
    return (ref_logprob, old_logprob - ref_logprob)


def solution(mesh):
    return jax.shard_map(
        shards,
        mesh=mesh,
        in_specs=(
            P("ctx", None),
            P(("ctx", "tp"), None, None),
            P(),
            P(),
            P(),
            P(),
            P(),
            P(),
            P(),
            P(("ctx", "tp"), None),
            P(),
            P(("ctx", "tp")),
        ),
        out_specs=(P(("ctx", "tp")), P(("ctx", "tp"))),
        check_vma=False,
    )
```

```python
import jax
import jax.numpy as jnp
from jax import lax
from jax.experimental import pallas as pl
from jax.experimental.pallas import tpu as pltpu
from jax.sharding import PartitionSpec as P

HEADS = 32
KV_HEADS = 16
HEAD_DIM = 128
WINDOW = 1024
QUERY_SCALAR = 168


epsilon = 1e-06
soft_cap = 30.0
rope_base = 10000.0
MESH = pl.DeviceIdType.MESH
VMEM = pltpu.VMEM
A2_REL = (0, 1, 3, 2)


def coords():
    c = lax.axis_index("ctx")
    t = lax.axis_index("tp")
    return t // 4, (c // 4) * 2 + (t // 2) % 2, c % 4, t % 2


def device_of(x, y, z, k):
    x, y, z, k = x % 4, y % 4, z % 4, k % 2
    return ((y // 2) * 4 + z, x * 4 + (y % 2) * 2 + k)


def axis_of(part, place):
    return (part + place) % 3


def shifted(axis, steps):
    where = list(coords())
    where[axis] = where[axis] + steps
    return device_of(*where)


def sibling():
    x, y, z, k = coords()
    return device_of(x, y, z, k + 1)


def greet(peers, meanwhile=None):
    barrier = pltpu.get_barrier_semaphore()
    for peer in peers:
        pl.semaphore_signal(barrier, inc=1, device_id=peer, device_id_type=MESH)
    if meanwhile is not None:
        meanwhile()
    pl.semaphore_wait(barrier, len(peers))


def vocab_kernel(
    fin_ref, table_ref, actions_ref, out_ref,
    buf, table, acc, part_exp, part_hit, column, st1, r1, st2, r2,
    table_sem, s1, v1, s2, v2, s3, v3, sf, vf, sk, vk, sa, va, sb, vb,
):
    ctx = lax.axis_index("ctx")
    tp = lax.axis_index("tp")
    core = tp % 2
    own = coords()[:3]
    width = fin_ref.shape[1] // 3
    rows = fin_ref.shape[0]
    vocab_rows = table.shape[1]

    def table_copy(p):
        return pltpu.make_async_copy(
            table_ref.at[:, pl.ds(p * width, width)], table.at[p], table_sem.at[p]
        )

    for p in range(3):
        table_copy(p).start()
    for p in range(3):
        buf[p, 0, 0, core, 0] = fin_ref[:, pl.ds(p * width, width)]
    x, y, z, k = coords()
    c_peer = lambda off: ((ctx + off) % 8, tp)
    t_peer = lambda off: (ctx, (tp + off) % 16)
    far_y = device_of(x, y - 1 + 2 * (y % 2), z, k)
    greet([c_peer(o) for o in range(1, 8)] + [t_peer(o) for o in range(1, 16)] + [far_y])

    def send(src, dst, send_sem, recv_sem, peer):
        return pltpu.make_async_remote_copy(
            src_ref=src, dst_ref=dst, send_sem=send_sem, recv_sem=recv_sem,
            device_id=peer, device_id_type=MESH,
        )

    def first(p, step):
        return send(
            buf.at[p, 0, 0, core, 0], buf.at[p, 0, 0, core, 4 - step],
            s1.at[p, step - 1], v1.at[p, step - 1], shifted(axis_of(p, 0), step),
        )

    def second(p, step):
        slot = A2_REL.index(4 - step)
        return send(
            buf.at[p, 0, 0, core], buf.at[p, 0, slot, core],
            s2.at[p, slot], v2.at[p, slot], shifted(axis_of(p, 1), step),
        )

    def third(p, q, step):
        return send(
            buf.at[p, 0, q, core], buf.at[p, 4 - step, q, core],
            s3.at[p, 4 - step, q], v3.at[p, 4 - step, q], shifted(axis_of(p, 2), step),
        )

    def passed(p, slab, q, step):
        return send(
            buf.at[p, slab, q, core], buf.at[p, 2, q, core],
            sf.at[p, q], vf.at[p, q], shifted(axis_of(p, 2), step),
        )

    def across(p, slab, q):
        return send(
            buf.at[p, slab, q, core], buf.at[p, slab, q, core],
            sk.at[p, slab, q], vk.at[p, slab, q], sibling(),
        )

    for p in range(3):
        for step in (1, 3, 2):
            first(p, step).start()
    for p in range(3):
        for step in (1, 3, 2):
            first(p, step).wait_recv()
        for step in (3, 1, 2):
            second(p, step).start()
    for p in range(3):
        for step in (1, 3):
            third(p, 0, step).start()
        across(p, 0, 0).start()

    def own_chunk(p, q):
        second(p, 4 - A2_REL[q]).wait_recv()
        for step in (1, 3):
            third(p, q, step).start()
        across(p, 0, q).start()

    for p in range(3):
        own_chunk(p, 1)

    def slab_of(g, i):
        return jnp.where(g < 2, 0, jnp.where(g > 5, 2, 3 - 2 * i))

    def row_of(g, i):
        return jnp.where(g < 2, g * 2 + i, jnp.where(g > 5, (g - 6) * 2 + i, g - 2))

    def arrivals(g):
        @pl.when(g == 1)
        def _():
            for q in (2, 3):
                for p in range(3):
                    own_chunk(p, q)

        @pl.when((g > 1) & (g < 6))
        def _():
            q = g - 2
            for p in range(3):
                third(p, q, 1).wait_recv()

                @pl.when(q % 2 == 0)
                def _():
                    passed(p, 3, q, 1).start()

                across(p, 3, q).start()
                third(p, q, 3).wait_recv()

                @pl.when(q % 2 == 1)
                def _():
                    passed(p, 1, q, 3).start()

                across(p, 1, q).start()

        @pl.when((g > 5) & (g < 8))
        def _():
            for i in range(2):
                q = (g - 6) * 2 + i
                for p in range(3):
                    passed(p, 3, q, 1).wait_recv()
                    across(p, 2, q).start()

    def place(axis_values, k):
        x, y, z = axis_values
        return ((y // 2) * 4 + z) * 16 + x * 4 + (y % 2) * 2 + k

    first_id = (ctx * 16 + tp) * vocab_rows
    ids = first_id + lax.broadcasted_iota(jnp.int32, (rows, vocab_rows), 1)

    def fold(v):
        total = v[:, :128]
        for i in range(1, vocab_rows // 128):
            total = total + v[:, i * 128:(i + 1) * 128]
        return total

    def tail(rel):
        at = place([(own[i] + rel[i]) % 4 for i in range(3)], 0)
        for kk in range(2):
            capped = soft_cap * jnp.tanh(acc[at + kk] * (1.0 / soft_cap))
            hit = ids == column[at + kk]
            part_exp[at + kk] = fold(jnp.exp(capped))
            part_hit[at + kk] = fold(jnp.where(hit, capped, 0.0))

    def near(digit):
        return digit + digit // 2

    def early_tail(i, carry):
        for j in range(3):
            tail((near(i // 3), near(i % 3), near(j)))
        return carry

    def late_x(i, carry):
        for j in range(4):
            tail((2, i, j))
        return carry

    def late_y(i, carry):
        for j in range(4):
            tail((near(i), 2, j))
        return carry

    def late_z(i, carry):
        for j in range(3):
            tail((near(i), near(j), 2))
        return carry

    def group(g, carry):
        slabs, lines = [slab_of(g, i) for i in range(2)], [row_of(g, i) for i in range(2)]
        for p in range(3):
            for i in range(2):
                across(p, slabs[i], lines[i]).wait_recv()

            @pl.when(g == 0)
            def _():
                table_copy(p).wait()

            lhs = jnp.concatenate(
                [buf[p, slabs[i], lines[i]].reshape(8 * rows, width) for i in range(2)], axis=0
            )
            got = lax.dot_general(
                lhs, table[p], (((1,), (1,)), ((), ())), preferred_element_type=jnp.float32
            )
            a1, a2, a3 = (axis_of(p, i) for i in range(3))
            for i in range(2):
                rel2 = jnp.where(lines[i] < 2, lines[i], 5 - lines[i])
                for kk in range(2):
                    for r1_ in range(4):
                        at = [None] * 3
                        at[a1] = (own[a1] + r1_) % 4
                        at[a2] = (own[a2] + rel2) % 4
                        at[a3] = (own[a3] + slabs[i]) % 4
                        d = place(at, kk)
                        m = (i * 2 + kk) * 4 + r1_
                        value = got[m * rows:(m + 1) * rows]
                        acc[d] = acc[d] + value
            if p == 0:
                @pl.when(g == 6)
                def _():
                    lax.fori_loop(0, 9, early_tail, 0)

                arrivals(g + 1)
        return carry

    def clear(d, carry):
        acc[d] = jnp.zeros((rows, vocab_rows), jnp.float32)
        return carry

    lax.fori_loop(0, 128, clear, 0)
    lanes = lax.broadcasted_iota(jnp.int32, (128, 128), 1)
    diagonal = lax.broadcasted_iota(jnp.int32, (128, 128), 0) == lanes

    def turn(j, carry):
        line = jnp.broadcast_to(actions_ref[pl.ds(j, 1)].astype(jnp.float32), (128, 128))
        turned = jnp.sum(jnp.where(diagonal, line, 0.0), axis=1, keepdims=True)
        column[pl.ds(j * 8, 8)] = turned.astype(jnp.int32).reshape(8, rows, 1)
        return carry

    lax.fori_loop(0, actions_ref.shape[0], turn, 0)
    lax.fori_loop(0, 8, group, 0)

    lax.fori_loop(0, 4, late_x, 0)
    lax.fori_loop(0, 3, late_y, 0)
    lax.fori_loop(0, 3, late_z, 0)
    ones = jnp.ones((8, 128), jnp.float32)
    for c in range(8):
        sums = [
            lax.dot_general(
                ones, part[pl.ds(c * 16, 16)].reshape(16 * rows, 128), (((1,), (1,)), ((), ())),
                preferred_element_type=jnp.float32, precision=lax.Precision.HIGHEST,
            )
            for part in (part_exp, part_hit)
        ]
        st1[c] = jnp.concatenate(
            [v[:1, i * 128:(i + 1) * 128] for v in (sums + sums) for i in range(2)], axis=0
        )

    def stage1(off):
        return send(st1.at[(ctx + off) % 8], r1.at[off], sa.at[off], va.at[off], c_peer(off))

    def stage2(off):
        return send(st2, r2.at[off], sb.at[off], vb.at[off], t_peer(off))

    for off in range(1, 8):
        stage1(off).start()
    total = st1[ctx]
    for off in range(1, 8):
        stage1(off).wait_recv()
        total = total + r1[off]
    st2[...] = total
    for off in range(1, 16):
        stage2(off).start()
    for off in range(1, 16):
        stage2(off).wait_recv()
        total = total + r2[off]
    out_ref[...] = total[2:4] - jnp.log(total[:2])

    for p in range(3):
        for step in (1, 2, 3):
            first(p, step).wait_send()
            second(p, step).wait_send()
        for q in range(4):
            third(p, q, 1).wait_send()
            third(p, q, 3).wait_send()
            passed(p, 3, q, 1).wait_send()
            for slab in range(4):
                across(p, slab, q).wait_send()
    for off in range(1, 8):
        stage1(off).wait_send()
    for off in range(1, 16):
        stage2(off).wait_send()


def vocab_stats(fin, table, actions):
    rows, depth = fin.shape
    width = depth // 3
    vocab_rows = table.shape[0]
    dma = pltpu.SemaphoreType.DMA
    return pl.pallas_call(
        vocab_kernel,
        out_shape=jax.ShapeDtypeStruct((2, 128), jnp.float32),
        in_specs=[
            pl.BlockSpec(memory_space=VMEM),
            pl.BlockSpec(memory_space=pl.ANY),
            pl.BlockSpec(memory_space=VMEM),
        ],
        out_specs=pl.BlockSpec(memory_space=VMEM),
        scratch_shapes=[
            VMEM((3, 4, 4, 2, 4, rows, width), jnp.bfloat16),
            VMEM((3, vocab_rows, width), jnp.bfloat16),
            VMEM((128, rows, vocab_rows), jnp.float32),
            VMEM((128, rows, 128), jnp.float32),
            VMEM((128, rows, 128), jnp.float32),
            VMEM((128, rows, 1), jnp.int32),
            VMEM((8, 8, 128), jnp.float32),
            VMEM((8, 8, 128), jnp.float32),
            VMEM((8, 128), jnp.float32),
            VMEM((16, 8, 128), jnp.float32),
            dma((3,)),
            dma((3, 3)), dma((3, 3)),
            dma((3, 4)), dma((3, 4)),
            dma((3, 4, 4)), dma((3, 4, 4)),
            dma((3, 4)), dma((3, 4)),
            dma((3, 4, 4)), dma((3, 4, 4)),
            dma((8,)), dma((8,)),
            dma((16,)), dma((16,)),
        ],
        compiler_params=pltpu.CompilerParams(
            collective_id=2, has_side_effects=True, vmem_limit_bytes=60 * 2**20
        ),
        name="vocab_stats",
    )(fin, table, actions.reshape(-1, 128))


CHUNK_AT = (1, 0, 2)
Z_FIRST = (0, 0, 0)


def layer_kernel(
    send_slot, keep_from, row_of, slot_of,
    lengths, residual_hbm, stored_hbm, frequency, in_lines, post_lines, final_lines, q_gain, k_gain, out_ref,
    in_gain, post_gain, final_gain, cos_ref, sin_ref,
    residual_ref, stored_ref, out, got_0, got_1, got_2, held, cols, proj, kv, query, mixed, wout,
    half_out, half_in, part_out, part_in, summed,
    load_sem, x_s, x_r, y_s, y_r, z_s, z_r, f_s, f_r,
    h_s, h_r, c_s, c_r, p_s, p_r,
):
    ctx = lax.axis_index("ctx")
    tp = lax.axis_index("tp")
    core = tp % 2
    chip = tp // 2
    y_hi, z = ctx // 4, ctx % 4
    n_blk = stored_ref.shape[0]
    blk_rows = stored_ref.shape[1]
    tokens, depth = residual_ref.shape
    head = q_gain.shape[1]

    def send(src, dst, send_sem, recv_sem, peer):
        return pltpu.make_async_remote_copy(
            src_ref=src, dst_ref=dst, send_sem=send_sem, recv_sem=recv_sem,
            device_id=peer, device_id_type=MESH,
        )

    t_peer = lambda off: (ctx, (tp + off) % 16)
    z_peer = lambda step: (y_hi * 4 + (z + step) % 4, tp)
    y_peer = ((ctx + 4) % 8, tp)

    got = (got_0, got_1, got_2)

    def swap(i, off):
        return send(
            out.at[i, (tp + off) % 16], got[i].at[tp], x_s.at[i, off], x_r.at[i, off], t_peer(off)
        )

    stored_copy = pltpu.make_async_copy(stored_hbm, stored_ref, load_sem.at[0])
    residual_copy = pltpu.make_async_copy(residual_hbm, residual_ref, load_sem.at[1])
    stored_copy.start()
    residual_copy.start()
    chunk = out.shape[3]

    def stage(t, carry):
        block = stored_ref[send_slot[t]]
        for i, at in enumerate(CHUNK_AT):
            out[i, t] = block[:, at * chunk:(at + 1) * chunk]
        return carry

    def stage_all():
        stored_copy.wait()
        lax.fori_loop(0, 16, stage, 0)

    greet(
        [((ctx + o) % 8, tp) for o in range(1, 8)] + [t_peer(o) for o in range(1, 16)], stage_all
    )

    def start_swap(off, carry):
        swap(0, off).start()
        return carry

    lax.fori_loop(1, 16, start_swap, 0)
    residual_copy.wait()
    for gain, lines in ((in_gain, in_lines), (post_gain, post_lines), (final_gain, final_lines)):
        for i in range(lines.shape[0]):
            gain[:, i * 128:(i + 1) * 128] = lines[i:i + 1]
    for i in range(3):
        got[i][tp] = out[i, tp]

    step_rows = 32

    def norm_rows(i, carry):
        at = pl.ds(pl.multiple_of(i * step_rows, step_rows), step_rows)
        x = residual_ref[at].astype(jnp.float32)
        scale = lax.rsqrt(jnp.mean(x * x, axis=-1, keepdims=True) + epsilon)
        n = (x * scale * in_gain[...]).astype(jnp.bfloat16)
        for r in range(depth // blk_rows):
            cols[r, at, :blk_rows] = n[:, r * blk_rows:(r + 1) * blk_rows]
        return carry

    lax.fori_loop(0, tokens // step_rows, norm_rows, 0)
    proj[...] = jnp.zeros_like(proj)
    row_ids = ctx * tokens + lax.broadcasted_iota(jnp.int32, (tokens, 1), 0)
    seg_start = jnp.zeros_like(row_ids)
    begin = jnp.int32(0)
    for i in range(lengths.shape[0]):
        seg_start = jnp.maximum(seg_start, jnp.where(begin <= row_ids, begin, 0))
        begin = begin + lengths[i]
    angle = (row_ids - seg_start).astype(jnp.float32) * frequency[...]
    low = lax.broadcasted_iota(jnp.int32, angle.shape, 1) < head // 2
    cos_ref[...] = jnp.cos(angle)
    sin_ref[...] = jnp.where(low, -jnp.sin(angle), jnp.sin(angle))

    def early(i):
        return n_blk - Z_FIRST[i]

    def y_copy(i, zz, k):
        return send(
            held.at[i, 0, zz, k], held.at[i, 1, zz, k], y_s.at[i, zz, k], y_r.at[i, zz, k], y_peer
        )

    def z_copy(i, yy, step, k):
        j = 0 if step == 1 else 1
        return send(
            held.at[i, yy, 0, k], held.at[i, yy, 4 - step, k],
            z_s.at[i, yy, j, k], z_r.at[i, yy, j, k], z_peer(step),
        )

    def f_copy(i, yy, step, k):
        return send(
            held.at[i, yy, 3 if step == 1 else 1, k], held.at[i, yy, 2, k],
            f_s.at[i, yy, k], f_r.at[i, yy, k], z_peer(step),
        )

    def blocks(body, low=0, high=None):
        def run(k, carry):
            body(k)
            return carry

        lax.fori_loop(low, n_blk if high is None else high, run, 0)

    def own(i):
        def wait(off, carry):
            swap(i, off).wait_recv()
            return carry

        def body(k):
            held[i, 0, 0, k] = got[i][keep_from[k]]
            y_copy(i, 0, k).start()
            z_copy(i, 0, 1, k).start()
            z_copy(i, 0, 3, k).start()
            if i < 2:
                swap(i + 1, 2 * k + 1).start()
                swap(i + 1, 2 * k + 2).start()

        lax.fori_loop(1, 16, wait, 0)
        blocks(body)
        if i < 2:
            swap(i + 1, 15).start()

    def partner(i):
        def body(k):
            y_copy(i, 0, k).wait_recv()

            @pl.when(k < early(i))
            def _():
                z_copy(i, 1, 1, k).start()
                z_copy(i, 1, 3, k).start()

            term(i, 0, 0, k)
            term(i, 1, 0, k)

        blocks(body)

    def side(i, yy):
        turn = 4 if yy == 0 else early(i) // 2

        def body(k):
            z_copy(i, yy, 1, k).wait_recv()

            @pl.when(k < turn)
            def _():
                f_copy(i, yy, 1, k).start()

            z_copy(i, yy, 3, k).wait_recv()

            @pl.when(k >= turn)
            def _():
                f_copy(i, yy, 3, k).start()

            if yy == 0:
                @pl.when(k >= early(i))
                def _():
                    y_copy(i, 3, k).start()
                    y_copy(i, 1, k).start()

            term(i, yy, 3, k)
            term(i, yy, 1, k)

        def across(k):
            y_copy(i, 3, k).wait_recv()
            y_copy(i, 1, k).wait_recv()
            term(i, 1, 3, k)
            term(i, 1, 1, k)

        if yy == 0:
            blocks(body)
        else:
            blocks(body, 0, early(i))
            blocks(across, early(i))

    def far(i, yy):
        def body(k):
            f_copy(i, yy, 1, k).wait_recv()
            if yy == 0:
                @pl.when(k >= early(i))
                def _():
                    y_copy(i, 2, k).start()
            term(i, yy, 2, k)

        def across(k):
            y_copy(i, 2, k).wait_recv()
            term(i, 1, 2, k)

        if yy == 0:
            blocks(body)
        else:
            blocks(body, 0, early(i))
            blocks(across, early(i))

    def term(i, yy, zz, k):
        if CHUNK_AT[i] < 2:
            c = (y_hi + yy) % 2 * 4 + (z + zz) % 4
            at = CHUNK_AT[i] * chunk
            proj[:, at:at + chunk] += jnp.dot(
                cols[row_of[c * n_blk + k], :, :blk_rows], held[i, yy, zz, k],
                preferred_element_type=jnp.float32,
            )

    own(0)
    partner(0)
    own(1)
    side(0, 0)
    partner(1)
    side(0, 1)
    far(0, 0)
    side(1, 0)
    far(0, 1)

    def heads(at, gain):
        e = proj[:, pl.ds(at * head, head)]
        scale = lax.rsqrt(jnp.mean(e * e, axis=-1, keepdims=True) + epsilon)
        e = e * scale * gain[...]
        return (e * cos_ref[...] + pltpu.roll(e, head // 2, 1) * sin_ref[...]).astype(jnp.bfloat16)

    reach = kv.shape[0] - 1
    kv[reach, :, :head] = heads(2, k_gain)
    kv[reach, :, head:] = proj[:, 3 * head:].astype(jnp.bfloat16)

    def halo(step):
        return send(
            kv.at[reach], kv.at[reach - step], h_s.at[step - 1], h_r.at[step - 1],
            ((ctx + step) % 8, tp),
        )

    for step in range(1, reach + 1):
        @pl.when(ctx + step < 8)
        def _():
            halo(step).start()

        @pl.when(ctx < step)
        def _():
            kv[reach - step] = jnp.zeros(kv.shape[1:], kv.dtype)

    side(1, 1)
    own(2)
    far(1, 0)
    partner(2)
    far(1, 1)
    for h in range(2):
        query[h] = heads(h, q_gain)
    side(2, 0)
    side(2, 1)
    for step in range(1, reach + 1):
        @pl.when(ctx >= step)
        def _():
            halo(step).wait_recv()

    span = (reach + 1) * tokens
    key_rows = kv[:, :, :head].reshape(span, head)
    value_rows = kv[:, :, head:].reshape(span, head)
    q_ids = ctx * tokens + lax.broadcasted_iota(jnp.int32, (tokens, span), 0)
    k_ids = (ctx - reach) * tokens + lax.broadcasted_iota(jnp.int32, (tokens, span), 1)
    visible = (k_ids <= q_ids) & (q_ids - k_ids < WINDOW) & (k_ids >= seg_start)
    for h in range(2):
        scores = lax.dot_general(
            query[h], key_rows, (((1,), (1,)), ((), ())), preferred_element_type=jnp.float32
        ) * QUERY_SCALAR ** (-0.5)
        probs = jnp.where(visible, jnp.exp(scores), 0.0)
        probs = (probs / jnp.sum(probs, axis=1, keepdims=True)).astype(jnp.bfloat16)
        heard = jnp.dot(probs, value_rows, preferred_element_type=jnp.float32).astype(jnp.bfloat16)
        mixed[:, :, :, h * head:(h + 1) * head] = heard.reshape(8, 2, tokens // 16, head)

    far(2, 0)
    far(2, 1)

    def order(r, carry):
        wout[r] = held.at[2].reshape(8 * n_blk, blk_rows, chunk)[slot_of[r]]
        return carry

    lax.fori_loop(0, depth // blk_rows, order, 0)

    share = tokens // 16
    per = wout.shape[0] // half_out.shape[0]
    piece = per * blk_rows
    other = (tp // 2) * 2 + (1 - core)

    def product(which, n):
        rows = mixed[:, which].reshape(8 * share, 2 * head)
        block = wout[pl.ds(n * per, per)].reshape(piece, 2 * head)
        return lax.dot_general(
            rows, block, (((1,), (1,)), ((), ())), preferred_element_type=jnp.float32
        ).reshape(8, share, piece)

    def between(n):
        return send(half_out.at[n], half_in.at[n], c_s.at[n], c_r.at[n], (ctx, other))

    def to_chip(n, off):
        there = (chip + off) % 8
        return send(
            part_out.at[n, there], part_in.at[n, off], p_s.at[n, off], p_r.at[n, off],
            (ctx, there * 2 + core),
        )

    n_pieces = half_out.shape[0]

    def give(n, carry):
        half_out[n] = product(1 - core, n).astype(jnp.bfloat16)
        between(n).start()
        return carry

    def take(n, carry):
        mine = product(core, n)
        between(n).wait_recv()
        part_out[n] = (mine + half_in[n].astype(jnp.float32)).astype(jnp.bfloat16)
        for off in range(1, 8):
            to_chip(n, off).start()
        return carry

    lax.fori_loop(0, n_pieces, give, 0)
    lax.fori_loop(0, n_pieces, take, 0)
    for n in range(n_pieces):
        total = part_out[n, chip].astype(jnp.float32)
        for off in range(1, 8):
            to_chip(n, off).wait_recv()
            total = total + part_in[n, off].astype(jnp.float32)
        summed[:, n * piece:(n + 1) * piece] = total

    def rms(values, gain):
        return values * lax.rsqrt(jnp.mean(values * values, axis=-1, keepdims=True) + epsilon) * gain[...]

    mine = residual_ref[pl.ds(pl.multiple_of(tp * share, share), share)].astype(jnp.float32)
    hidden = mine + rms(summed[...], post_gain)
    out_ref[...] = rms(hidden, final_gain).astype(jnp.bfloat16)

    def swapped(off, carry):
        for i in range(3):
            swap(i, off).wait_send()
        return carry

    lax.fori_loop(1, 16, swapped, 0)
    for i in range(3):
        def sent(k):
            y_copy(i, 0, k).wait_send()
            z_copy(i, 0, 1, k).wait_send()
            z_copy(i, 0, 3, k).wait_send()
            f_copy(i, 0, 1, k).wait_send()

        def sent_z(k):
            z_copy(i, 1, 1, k).wait_send()
            z_copy(i, 1, 3, k).wait_send()
            f_copy(i, 1, 1, k).wait_send()

        def sent_y(k):
            for zz in range(1, 4):
                y_copy(i, zz, k).wait_send()

        blocks(sent)
        blocks(sent_z, 0, early(i))
        blocks(sent_y, early(i))
    for step in range(1, reach + 1):
        @pl.when(ctx + step < 8)
        def _():
            halo(step).wait_send()

    def parts_sent(n, carry):
        between(n).wait_send()
        for off in range(1, 8):
            to_chip(n, off).wait_send()
        return carry

    lax.fori_loop(0, n_pieces, parts_sent, 0)


def layer(
    send_slot, keep_from, row_of, slot_of, lengths, residual, stored, frequency,
    in_gain, q_gain, k_gain, post_gain, final_gain,
):
    tokens, depth = residual.shape
    n_blk, blk_rows, width = stored.shape
    head = q_gain.shape[0]
    share = tokens // 16
    bf16 = jnp.bfloat16
    n_rows = depth // blk_rows
    n_pieces = 7
    piece = depth // n_pieces
    reach = WINDOW // tokens
    dma = pltpu.SemaphoreType.DMA
    chunk = width // 3
    smem = pl.BlockSpec(memory_space=pltpu.SMEM)
    vmem = pl.BlockSpec(memory_space=VMEM)
    return pl.pallas_call(
        layer_kernel,
        out_shape=jax.ShapeDtypeStruct((share, depth), bf16),
        in_specs=[smem] * 5 + [pl.BlockSpec(memory_space=pl.ANY)] * 2 + [vmem] * 6,
        out_specs=vmem,
        scratch_shapes=[VMEM((1, depth), jnp.float32)] * 3
        + [VMEM((tokens, head), jnp.float32)] * 2
        + [
            VMEM((tokens, depth), bf16),
            VMEM((n_blk, blk_rows, width), bf16),
            VMEM((3, 16, blk_rows, chunk), bf16),
            VMEM((16, blk_rows, chunk), bf16),
            VMEM((16, blk_rows, chunk), bf16),
            VMEM((16, blk_rows, chunk), bf16),
            VMEM((3, 2, 4, n_blk, blk_rows, chunk), bf16),
            VMEM((n_rows, tokens, 128), bf16),
            VMEM((tokens, 2 * chunk), jnp.float32),
            VMEM((reach + 1, tokens, 2 * head), bf16),
            VMEM((2, tokens, head), bf16),
            VMEM((8, 2, share, 2 * head), bf16),
            VMEM((n_rows, blk_rows, chunk), bf16),
            VMEM((n_pieces, 8, share, piece), bf16),
            VMEM((n_pieces, 8, share, piece), bf16),
            VMEM((n_pieces, 8, share, piece), bf16),
            VMEM((n_pieces, 8, share, piece), bf16),
            VMEM((share, depth), jnp.float32),
        ]
        + [dma((2,))]
        + [dma((3, 16))] * 2
        + [dma((3, 4, n_blk))] * 2
        + [dma((3, 2, 2, n_blk))] * 2
        + [dma((3, 2, n_blk))] * 2
        + [dma((reach,))] * 2
        + [dma((n_pieces,))] * 2
        + [dma((n_pieces, 8))] * 2,
        compiler_params=pltpu.CompilerParams(
            collective_id=1, has_side_effects=True, vmem_limit_bytes=60 * 2**20
        ),
        name="layer",
    )(
        send_slot, keep_from, row_of, slot_of, lengths, residual, stored, frequency,
        in_gain.reshape(-1, 128), post_gain.reshape(-1, 128), final_gain.reshape(-1, 128),
        q_gain[None], k_gain[None],
    )


def rope_frequency(head):
    half_size = head // 2
    frequency = rope_base ** (-2.0 * jnp.arange(half_size, dtype=jnp.float32) / head)
    return jnp.concatenate([frequency, frequency])[None]


def block_tables(block_list, ctx_index, tp_index, ctx_count, tp_count, blocks_dev):
    rows_per_reader = blocks_dev * ctx_count
    grid = block_list.reshape(ctx_count, tp_count, blocks_dev)
    readers = (grid * 1171) >> 16
    my_readers = lax.dynamic_slice(
        readers, (ctx_index, tp_index, 0), (1, 1, blocks_dev)
    ).reshape(-1)
    slots = jnp.arange(blocks_dev, dtype=jnp.int32)
    sources = jnp.arange(tp_count, dtype=jnp.int32)
    send_slot = jnp.sum(jnp.where(my_readers[None, :] == sources[:, None], slots[None, :], 0), axis=1)
    hit = readers == tp_index
    present = jnp.any(hit, axis=2)
    row_index = jnp.sum(jnp.where(hit, grid - readers * rows_per_reader, 0), axis=2)
    before = sources[None, :] < sources[:, None]
    rank = jnp.sum((present[:, None, :] & before[None]).astype(jnp.int32), axis=2)
    chosen = (rank[:, None, :] == slots[None, :, None]) & present[:, None, :]
    row_of = jnp.sum(jnp.where(chosen, row_index[:, None, :], 0), axis=2)
    keep_all = jnp.sum(jnp.where(chosen, sources[None, None, :], 0), axis=2)
    keep_from = lax.dynamic_index_in_dim(keep_all, ctx_index, 0, False)
    ids = jnp.arange(ctx_count, dtype=jnp.int32)
    side = (ids // 4 + ctx_index // 4) % 2
    slot = (side * 4 + (ids + 4 - ctx_index % 4) % 4)[:, None] * blocks_dev + slots[None, :]
    rows = jnp.arange(rows_per_reader, dtype=jnp.int32)
    slot_of = jnp.sum(jnp.where(row_of.reshape(1, -1) == rows[:, None], slot.reshape(1, -1), 0), axis=1)
    return send_slot, keep_from, row_of.reshape(-1), slot_of


def shards(
    residual,
    stored_blocks,
    block_list,
    lengths,
    in_gain,
    q_gain,
    k_gain,
    post_gain,
    final_gain,
    vocab_table,
    actions,
    old_logprob,
):
    ctx_count = lax.axis_size("ctx")
    tp_count = lax.axis_size("tp")
    ctx_index = lax.axis_index("ctx")
    tp_index = lax.axis_index("tp")
    row_count = residual.shape[0]
    share_rows = row_count // tp_count
    tables = block_tables(
        block_list, ctx_index, tp_index, ctx_count, tp_count, stored_blocks.shape[0]
    )
    final = layer(
        *tables, lengths, residual, stored_blocks, rope_frequency(HEAD_DIM),
        in_gain, q_gain, k_gain, post_gain, final_gain,
    )
    all_rows = vocab_stats(final, vocab_table, actions)
    ref_logprob = lax.dynamic_slice_in_dim(all_rows.reshape(-1), tp_index * share_rows, share_rows, 0)
    return (ref_logprob, old_logprob - ref_logprob)


def solution(mesh):
    return jax.shard_map(
        shards,
        mesh=mesh,
        in_specs=(
            P("ctx", None),
            P(("ctx", "tp"), None, None),
            P(),
            P(),
            P(),
            P(),
            P(),
            P(),
            P(),
            P(("ctx", "tp"), None),
            P(),
            P(("ctx", "tp")),
        ),
        out_specs=(P(("ctx", "tp")), P(("ctx", "tp"))),
        check_vma=False,
    )
```

```python
import functools

import jax
import jax.numpy as jnp
import numpy as np
from jax import lax
from jax.experimental import pallas as pl
from jax.experimental.pallas import tpu as pltpu
from jax.sharding import PartitionSpec as P

HEADS = 32
KV_HEADS = 16
HEAD_DIM = 128
WINDOW = 1024
QUERY_SCALAR = 168


epsilon = 1e-06
soft_cap = 30.0
rope_base = 10000.0
MESH = pl.DeviceIdType.MESH
VMEM = pltpu.VMEM
A2_REL = (0, 1, 3, 2)


def coords():
    c = lax.axis_index("ctx")
    t = lax.axis_index("tp")
    return t // 4, (c // 4) * 2 + (t // 2) % 2, c % 4, t % 2


def device_of(x, y, z, k):
    x, y, z, k = x % 4, y % 4, z % 4, k % 2
    return ((y // 2) * 4 + z, x * 4 + (y % 2) * 2 + k)


def axis_of(part, place):
    return (part + place) % 3


def shifted(axis, steps):
    where = list(coords())
    where[axis] = where[axis] + steps
    return device_of(*where)


def sibling():
    x, y, z, k = coords()
    return device_of(x, y, z, k + 1)


def greet(peers, meanwhile=None):
    barrier = pltpu.get_barrier_semaphore()
    for peer in peers:
        pl.semaphore_signal(barrier, inc=1, device_id=peer, device_id_type=MESH)
    if meanwhile is not None:
        meanwhile()
    pl.semaphore_wait(barrier, len(peers))


def vocab_part(
    fin_ref, table_ref, actions_ref, out_ref, buf, r1, r2,
    table_sem, s1, v1, s2, v2, s3, v3, sf, vf, sk, vk, sa, va, sb, vb,
    table, acc, part_exp, part_hit, column, st1, st2,
):
    ctx = lax.axis_index("ctx")
    tp = lax.axis_index("tp")
    core = tp % 2
    own = coords()[:3]
    width = fin_ref.shape[1] // 3
    rows = fin_ref.shape[0]
    vocab_rows = table.shape[1]

    def table_copy(p):
        return pltpu.make_async_copy(
            table_ref.at[:, pl.ds(p * width, width)], table.at[p], table_sem.at[p]
        )

    for p in range(3):
        table_copy(p).start()
    for p in range(3):
        buf[p, 0, 0, core, 0] = fin_ref[:, pl.ds(p * width, width)]
    c_peer = lambda off: ((ctx + off) % 8, tp)
    t_peer = lambda off: (ctx, (tp + off) % 16)

    def send(src, dst, send_sem, recv_sem, peer):
        return pltpu.make_async_remote_copy(
            src_ref=src, dst_ref=dst, send_sem=send_sem, recv_sem=recv_sem,
            device_id=peer, device_id_type=MESH,
        )

    def first(p, step):
        return send(
            buf.at[p, 0, 0, core, 0], buf.at[p, 0, 0, core, 4 - step],
            s1.at[p, step - 1], v1.at[p, step - 1], shifted(axis_of(p, 0), step),
        )

    def second(p, step):
        slot = A2_REL.index(4 - step)
        return send(
            buf.at[p, 0, 0, core], buf.at[p, 0, slot, core],
            s2.at[p, slot], v2.at[p, slot], shifted(axis_of(p, 1), step),
        )

    def third(p, q, step):
        return send(
            buf.at[p, 0, q, core], buf.at[p, 4 - step, q, core],
            s3.at[p, 4 - step, q], v3.at[p, 4 - step, q], shifted(axis_of(p, 2), step),
        )

    def passed(p, slab, q, step):
        return send(
            buf.at[p, slab, q, core], buf.at[p, 2, q, core],
            sf.at[p, q], vf.at[p, q], shifted(axis_of(p, 2), step),
        )

    def across(p, slab, q):
        return send(
            buf.at[p, slab, q, core], buf.at[p, slab, q, core],
            sk.at[p, slab, q], vk.at[p, slab, q], sibling(),
        )

    for p in range(3):
        for step in (1, 3, 2):
            first(p, step).start()
    for p in range(3):
        for step in (1, 3, 2):
            first(p, step).wait_recv()
        for step in (3, 1, 2):
            second(p, step).start()
    for p in range(3):
        for step in (1, 3):
            third(p, 0, step).start()
        across(p, 0, 0).start()

    def own_chunk(p, q):
        second(p, 4 - A2_REL[q]).wait_recv()
        for step in (1, 3):
            third(p, q, step).start()
        across(p, 0, q).start()

    for p in range(3):
        own_chunk(p, 1)

    def slab_of(g, i):
        return jnp.where(g < 2, 0, jnp.where(g > 5, 2, 3 - 2 * i))

    def row_of(g, i):
        return jnp.where(g < 2, g * 2 + i, jnp.where(g > 5, (g - 6) * 2 + i, g - 2))

    def arrivals(g):
        @pl.when(g == 1)
        def _():
            for q in (2, 3):
                for p in range(3):
                    own_chunk(p, q)

        @pl.when((g > 1) & (g < 6))
        def _():
            q = g - 2
            for p in range(3):
                third(p, q, 1).wait_recv()

                @pl.when(q % 2 == 0)
                def _():
                    passed(p, 3, q, 1).start()

                across(p, 3, q).start()
                third(p, q, 3).wait_recv()

                @pl.when(q % 2 == 1)
                def _():
                    passed(p, 1, q, 3).start()

                across(p, 1, q).start()

        @pl.when((g > 5) & (g < 8))
        def _():
            for i in range(2):
                q = (g - 6) * 2 + i
                for p in range(3):
                    passed(p, 3, q, 1).wait_recv()
                    across(p, 2, q).start()

    def place(axis_values, k):
        x, y, z = axis_values
        return ((y // 2) * 4 + z) * 16 + x * 4 + (y % 2) * 2 + k

    first_id = (ctx * 16 + tp) * vocab_rows
    ids = first_id + lax.broadcasted_iota(jnp.int32, (rows, vocab_rows), 1)

    def fold(v):
        total = v[:, :128]
        for i in range(1, vocab_rows // 128):
            total = total + v[:, i * 128:(i + 1) * 128]
        return total

    def tail(rel):
        at = place([(own[i] + rel[i]) % 4 for i in range(3)], 0)
        for kk in range(2):
            capped = soft_cap * jnp.tanh(acc[at + kk] * (1.0 / soft_cap))
            hit = ids == column[at + kk]
            part_exp[at + kk] = fold(jnp.exp(capped))
            part_hit[at + kk] = fold(jnp.where(hit, capped, 0.0))

    def near(digit):
        return digit + digit // 2

    def early_tail(i, carry):
        for j in range(3):
            tail((near(i // 3), near(i % 3), near(j)))
        return carry

    def late_x(i, carry):
        for j in range(4):
            tail((2, i, j))
        return carry

    def late_y(i, carry):
        for j in range(4):
            tail((near(i), 2, j))
        return carry

    def late_z(i, carry):
        for j in range(3):
            tail((near(i), near(j), 2))
        return carry

    def group(g, carry):
        slabs, lines = [slab_of(g, i) for i in range(2)], [row_of(g, i) for i in range(2)]
        for p in range(3):
            for i in range(2):
                across(p, slabs[i], lines[i]).wait_recv()

            @pl.when(g == 0)
            def _():
                table_copy(p).wait()

            lhs = jnp.concatenate(
                [buf[p, slabs[i], lines[i]].reshape(8 * rows, width) for i in range(2)], axis=0
            )
            got = lax.dot_general(
                lhs, table[p], (((1,), (1,)), ((), ())), preferred_element_type=jnp.float32
            )
            a1, a2, a3 = (axis_of(p, i) for i in range(3))
            for i in range(2):
                rel2 = jnp.where(lines[i] < 2, lines[i], 5 - lines[i])
                for kk in range(2):
                    for r1_ in range(4):
                        at = [None] * 3
                        at[a1] = (own[a1] + r1_) % 4
                        at[a2] = (own[a2] + rel2) % 4
                        at[a3] = (own[a3] + slabs[i]) % 4
                        d = place(at, kk)
                        m = (i * 2 + kk) * 4 + r1_
                        value = got[m * rows:(m + 1) * rows]
                        acc[d] = acc[d] + value
            if p == 0:
                @pl.when(g == 6)
                def _():
                    lax.fori_loop(0, 9, early_tail, 0)

                arrivals(g + 1)
        return carry

    def clear(d, carry):
        acc[d] = jnp.zeros((rows, vocab_rows), jnp.float32)
        return carry

    lax.fori_loop(0, 128, clear, 0)
    lanes = lax.broadcasted_iota(jnp.int32, (128, 128), 1)
    diagonal = lax.broadcasted_iota(jnp.int32, (128, 128), 0) == lanes

    def turn(j, carry):
        line = jnp.broadcast_to(actions_ref[pl.ds(j, 1)].astype(jnp.float32), (128, 128))
        turned = jnp.sum(jnp.where(diagonal, line, 0.0), axis=1, keepdims=True)
        column[pl.ds(j * 8, 8)] = turned.astype(jnp.int32).reshape(8, rows, 1)
        return carry

    lax.fori_loop(0, actions_ref.shape[0], turn, 0)
    lax.fori_loop(0, 8, group, 0)

    lax.fori_loop(0, 4, late_x, 0)
    lax.fori_loop(0, 3, late_y, 0)
    lax.fori_loop(0, 3, late_z, 0)
    ones = jnp.ones((8, 128), jnp.float32)
    for c in range(8):
        sums = [
            lax.dot_general(
                ones, part[pl.ds(c * 16, 16)].reshape(16 * rows, 128), (((1,), (1,)), ((), ())),
                preferred_element_type=jnp.float32, precision=lax.Precision.HIGHEST,
            )
            for part in (part_exp, part_hit)
        ]
        st1[c] = jnp.concatenate(
            [v[:1, i * 128:(i + 1) * 128] for v in (sums + sums) for i in range(2)], axis=0
        )

    def stage1(off):
        return send(st1.at[(ctx + off) % 8], r1.at[off], sa.at[off], va.at[off], c_peer(off))

    def stage2(off):
        return send(st2, r2.at[off], sb.at[off], vb.at[off], t_peer(off))

    for off in range(1, 8):
        stage1(off).start()
    total = st1[ctx]
    for off in range(1, 8):
        stage1(off).wait_recv()
        total = total + r1[off]
    st2[...] = total
    for off in range(1, 16):
        stage2(off).start()
    for off in range(1, 16):
        stage2(off).wait_recv()
        total = total + r2[off]
    out_ref[...] = total[2:4] - jnp.log(total[:2])

    for p in range(3):
        for step in (1, 2, 3):
            first(p, step).wait_send()
            second(p, step).wait_send()
        for q in range(4):
            third(p, q, 1).wait_send()
            third(p, q, 3).wait_send()
            passed(p, 3, q, 1).wait_send()
            for slab in range(4):
                across(p, slab, q).wait_send()
    for off in range(1, 8):
        stage1(off).wait_send()
    for off in range(1, 16):
        stage2(off).wait_send()


CHUNK_AT = (1, 0, 2)
Z_FIRST = (0, 0, 2)


def layer_part(
    send_slot, keep_from, row_of, slot_of,
    lengths, residual_hbm, stored_hbm, frequency, in_lines, post_lines, final_lines, q_gain, k_gain, out_ref,
    got_0, got_1, got_2, held, kv, half_in, part_in,
    load_sem, x_s, x_r, y_s, y_r, z_s, z_r, f_s, f_r, h_s, h_r, c_s, c_r, p_s, p_r,
    in_gain, post_gain, final_gain, cos_ref, sin_ref, residual_ref, stored_ref, out, cols, proj,
    query, mixed, wout, half_out, part_out, summed,
):
    ctx = lax.axis_index("ctx")
    tp = lax.axis_index("tp")
    core = tp % 2
    chip = tp // 2
    y_hi, z = ctx // 4, ctx % 4
    n_blk = stored_ref.shape[0]
    blk_rows = stored_ref.shape[1]
    tokens, depth = residual_ref.shape
    head = q_gain.shape[1]

    def send(src, dst, send_sem, recv_sem, peer):
        return pltpu.make_async_remote_copy(
            src_ref=src, dst_ref=dst, send_sem=send_sem, recv_sem=recv_sem,
            device_id=peer, device_id_type=MESH,
        )

    t_peer = lambda off: (ctx, (tp + off) % 16)
    z_peer = lambda step: (y_hi * 4 + (z + step) % 4, tp)
    y_peer = ((ctx + 4) % 8, tp)

    got = (got_0, got_1, got_2)

    def swap(i, off):
        return send(
            out.at[i, (tp + off) % 16], got[i].at[tp], x_s.at[i, off], x_r.at[i, off], t_peer(off)
        )

    stored_copy = pltpu.make_async_copy(stored_hbm, stored_ref, load_sem.at[0])
    residual_copy = pltpu.make_async_copy(residual_hbm, residual_ref, load_sem.at[1])
    stored_copy.start()
    residual_copy.start()
    chunk = out.shape[3]

    def stage(t, carry):
        block = stored_ref[send_slot[t]]
        for i, at in enumerate(CHUNK_AT):
            out[i, t] = block[:, at * chunk:(at + 1) * chunk]
        return carry

    def stage_all():
        stored_copy.wait()
        lax.fori_loop(0, 16, stage, 0)

    x_at, y_at, z_at, k_at = coords()
    far_y = device_of(x_at, y_at - 1 + 2 * (y_at % 2), z_at, k_at)
    greet(
        [((ctx + o) % 8, tp) for o in range(1, 8)] + [t_peer(o) for o in range(1, 16)] + [far_y],
        stage_all,
    )

    def start_swap(off, carry):
        swap(0, off).start()
        return carry

    lax.fori_loop(1, 16, start_swap, 0)
    residual_copy.wait()
    for gain, lines in ((in_gain, in_lines), (post_gain, post_lines), (final_gain, final_lines)):
        for i in range(lines.shape[0]):
            gain[:, i * 128:(i + 1) * 128] = lines[i:i + 1]
    for i in range(3):
        got[i][tp] = out[i, tp]

    step_rows = 32

    def norm_rows(i, carry):
        at = pl.ds(pl.multiple_of(i * step_rows, step_rows), step_rows)
        x = residual_ref[at].astype(jnp.float32)
        scale = lax.rsqrt(jnp.mean(x * x, axis=-1, keepdims=True) + epsilon)
        n = (x * scale * in_gain[...]).astype(jnp.bfloat16)
        for r in range(depth // blk_rows):
            cols[r, at, :blk_rows] = n[:, r * blk_rows:(r + 1) * blk_rows]
        return carry

    lax.fori_loop(0, tokens // step_rows, norm_rows, 0)
    proj[...] = jnp.zeros_like(proj)
    row_ids = ctx * tokens + lax.broadcasted_iota(jnp.int32, (tokens, 1), 0)
    seg_start = jnp.zeros_like(row_ids)
    begin = jnp.int32(0)
    for i in range(lengths.shape[0]):
        seg_start = jnp.maximum(seg_start, jnp.where(begin <= row_ids, begin, 0))
        begin = begin + lengths[i]
    angle = (row_ids - seg_start).astype(jnp.float32) * frequency[...]
    low = lax.broadcasted_iota(jnp.int32, angle.shape, 1) < head // 2
    cos_ref[...] = jnp.cos(angle)
    sin_ref[...] = jnp.where(low, -jnp.sin(angle), jnp.sin(angle))

    def early(i):
        return n_blk - Z_FIRST[i]

    def y_copy(i, zz, k):
        return send(
            held.at[i, 0, zz, k], held.at[i, 1, zz, k], y_s.at[i, zz, k], y_r.at[i, zz, k], y_peer
        )

    def z_copy(i, yy, step, k):
        j = 0 if step == 1 else 1
        return send(
            held.at[i, yy, 0, k], held.at[i, yy, 4 - step, k],
            z_s.at[i, yy, j, k], z_r.at[i, yy, j, k], z_peer(step),
        )

    def f_copy(i, yy, step, k):
        return send(
            held.at[i, yy, 3 if step == 1 else 1, k], held.at[i, yy, 2, k],
            f_s.at[i, yy, k], f_r.at[i, yy, k], z_peer(step),
        )

    def blocks(body, low=0, high=None):
        def run(k, carry):
            body(k)
            return carry

        lax.fori_loop(low, n_blk if high is None else high, run, 0)

    def own(i):
        def wait(off, carry):
            swap(i, off).wait_recv()
            return carry

        def body(k):
            held[i, 0, 0, k] = got[i][keep_from[k]]
            y_copy(i, 0, k).start()
            z_copy(i, 0, 1, k).start()
            z_copy(i, 0, 3, k).start()
            if i < 2:
                swap(i + 1, 2 * k + 1).start()
                swap(i + 1, 2 * k + 2).start()

        lax.fori_loop(1, 16, wait, 0)
        blocks(body)
        if i < 2:
            swap(i + 1, 15).start()

    def partner(i):
        def body(k):
            y_copy(i, 0, k).wait_recv()

            @pl.when(k < early(i))
            def _():
                z_copy(i, 1, 1, k).start()
                z_copy(i, 1, 3, k).start()

            term(i, 0, 0, k)
            term(i, 1, 0, k)

        blocks(body)

    def side(i, yy):
        turn = 4 if yy == 0 else early(i) // 2

        def body(k):
            z_copy(i, yy, 1, k).wait_recv()

            @pl.when(k < turn)
            def _():
                f_copy(i, yy, 1, k).start()

            z_copy(i, yy, 3, k).wait_recv()

            @pl.when(k >= turn)
            def _():
                f_copy(i, yy, 3, k).start()

            if yy == 0:
                @pl.when(k >= early(i))
                def _():
                    y_copy(i, 3, k).start()
                    y_copy(i, 1, k).start()

            term(i, yy, 3, k)
            term(i, yy, 1, k)

        def across(k):
            y_copy(i, 3, k).wait_recv()
            y_copy(i, 1, k).wait_recv()
            term(i, 1, 3, k)
            term(i, 1, 1, k)

        if yy == 0:
            blocks(body)
        else:
            blocks(body, 0, early(i))
            blocks(across, early(i))

    def far(i, yy):
        def body(k):
            f_copy(i, yy, 1, k).wait_recv()
            if yy == 0:
                @pl.when(k >= early(i))
                def _():
                    y_copy(i, 2, k).start()
            term(i, yy, 2, k)

        def across(k):
            y_copy(i, 2, k).wait_recv()
            term(i, 1, 2, k)

        if yy == 0:
            blocks(body)
        else:
            blocks(body, 0, early(i))
            blocks(across, early(i))

    def term(i, yy, zz, k):
        if CHUNK_AT[i] < 2:
            c = (y_hi + yy) % 2 * 4 + (z + zz) % 4
            at = CHUNK_AT[i] * chunk
            proj[:, at:at + chunk] += jnp.dot(
                cols[row_of[c * n_blk + k], :, :blk_rows], held[i, yy, zz, k],
                preferred_element_type=jnp.float32,
            )

    own(0)
    partner(0)
    own(1)
    side(0, 0)
    partner(1)
    side(0, 1)
    far(0, 0)
    side(1, 0)
    far(0, 1)

    def heads(at, gain):
        e = proj[:, pl.ds(at * head, head)]
        scale = lax.rsqrt(jnp.mean(e * e, axis=-1, keepdims=True) + epsilon)
        e = e * scale * gain[...]
        return (e * cos_ref[...] + pltpu.roll(e, head // 2, 1) * sin_ref[...]).astype(jnp.bfloat16)

    reach = kv.shape[0] - 1
    kv[reach, :, :head] = heads(2, k_gain)
    kv[reach, :, head:] = proj[:, 3 * head:].astype(jnp.bfloat16)

    def halo(step):
        return send(
            kv.at[reach], kv.at[reach - step], h_s.at[step - 1], h_r.at[step - 1],
            ((ctx + step) % 8, tp),
        )

    for step in range(1, reach + 1):
        @pl.when(ctx + step < 8)
        def _():
            halo(step).start()

        @pl.when(ctx < step)
        def _():
            kv[reach - step] = jnp.zeros(kv.shape[1:], kv.dtype)

    side(1, 1)
    own(2)
    far(1, 0)
    partner(2)
    far(1, 1)
    for h in range(2):
        query[h] = heads(h, q_gain)
    side(2, 0)
    side(2, 1)
    for step in range(1, reach + 1):
        @pl.when(ctx >= step)
        def _():
            halo(step).wait_recv()

    span = (reach + 1) * tokens
    key_rows = kv[:, :, :head].reshape(span, head)
    value_rows = kv[:, :, head:].reshape(span, head)
    q_ids = ctx * tokens + lax.broadcasted_iota(jnp.int32, (tokens, span), 0)
    k_ids = (ctx - reach) * tokens + lax.broadcasted_iota(jnp.int32, (tokens, span), 1)
    visible = (k_ids <= q_ids) & (q_ids - k_ids < WINDOW) & (k_ids >= seg_start)
    for h in range(2):
        scores = lax.dot_general(
            query[h], key_rows, (((1,), (1,)), ((), ())), preferred_element_type=jnp.float32
        ) * QUERY_SCALAR ** (-0.5)
        probs = jnp.where(visible, jnp.exp(scores), 0.0)
        probs = (probs / jnp.sum(probs, axis=1, keepdims=True)).astype(jnp.bfloat16)
        heard = jnp.dot(probs, value_rows, preferred_element_type=jnp.float32).astype(jnp.bfloat16)
        mixed[:, :, :, h * head:(h + 1) * head] = heard.reshape(8, 2, tokens // 16, head)

    far(2, 0)
    far(2, 1)

    def order(r, carry):
        wout[r] = held.at[2].reshape(8 * n_blk, blk_rows, chunk)[slot_of[r]]
        return carry

    lax.fori_loop(0, depth // blk_rows, order, 0)

    share = tokens // 16
    per = wout.shape[0] // half_out.shape[0]
    piece = per * blk_rows
    other = (tp // 2) * 2 + (1 - core)

    def product(which, n):
        rows = mixed[:, which].reshape(8 * share, 2 * head)
        block = wout[pl.ds(n * per, per)].reshape(piece, 2 * head)
        return lax.dot_general(
            rows, block, (((1,), (1,)), ((), ())), preferred_element_type=jnp.float32
        ).reshape(8, share, piece)

    def between(n):
        return send(half_out.at[n], half_in.at[n], c_s.at[n], c_r.at[n], (ctx, other))

    def to_chip(n, off):
        there = (chip + off) % 8
        return send(
            part_out.at[n, there], part_in.at[n, off], p_s.at[n, off], p_r.at[n, off],
            (ctx, there * 2 + core),
        )

    n_pieces = half_out.shape[0]

    def give(n, carry):
        half_out[n] = product(1 - core, n).astype(jnp.bfloat16)
        between(n).start()
        return carry

    def take(n, carry):
        mine = product(core, n)
        between(n).wait_recv()
        part_out[n] = (mine + half_in[n].astype(jnp.float32)).astype(jnp.bfloat16)
        for off in range(1, 8):
            to_chip(n, off).start()
        return carry

    lax.fori_loop(0, n_pieces, give, 0)
    lax.fori_loop(0, n_pieces, take, 0)
    def swapped(off, carry):
        for i in range(3):
            swap(i, off).wait_send()
        return carry

    lax.fori_loop(1, 16, swapped, 0)
    for i in range(3):
        def sent(k):
            y_copy(i, 0, k).wait_send()
            z_copy(i, 0, 1, k).wait_send()
            z_copy(i, 0, 3, k).wait_send()
            f_copy(i, 0, 1, k).wait_send()

        def sent_z(k):
            z_copy(i, 1, 1, k).wait_send()
            z_copy(i, 1, 3, k).wait_send()
            f_copy(i, 1, 1, k).wait_send()

        def sent_y(k):
            for zz in range(1, 4):
                y_copy(i, zz, k).wait_send()

        blocks(sent)
        blocks(sent_z, 0, early(i))
        blocks(sent_y, early(i))
    for step in range(1, reach + 1):
        @pl.when(ctx + step < 8)
        def _():
            halo(step).wait_send()

    def halves_sent(n, carry):
        between(n).wait_send()
        return carry

    lax.fori_loop(0, n_pieces, halves_sent, 0)
    for n in range(n_pieces):
        total = part_out[n, chip].astype(jnp.float32)
        for off in range(1, 8):
            to_chip(n, off).wait_recv()
            total = total + part_in[n, off].astype(jnp.float32)
        summed[:, n * piece:(n + 1) * piece] = total

    def rms(values, gain):
        return values * lax.rsqrt(jnp.mean(values * values, axis=-1, keepdims=True) + epsilon) * gain[...]

    mine = residual_ref[pl.ds(pl.multiple_of(tp * share, share), share)].astype(jnp.float32)
    hidden = mine + rms(summed[...], post_gain)
    out_ref[...] = rms(hidden, final_gain).astype(jnp.bfloat16)

    def parts_sent(n, carry):
        for off in range(1, 8):
            to_chip(n, off).wait_send()
        return carry

    lax.fori_loop(0, n_pieces, parts_sent, 0)


def whole_kernel(counts, *refs):
    n_tables, n_layer, n_layer_own, n_vocab_own = counts
    tables, refs = refs[:n_tables], refs[n_tables:]
    (lengths, residual, stored, frequency, in_lines, post_lines, final_lines, q_gain, k_gain,
     table, actions, out_ref, fin), refs = refs[:13], refs[13:]
    layer_refs, vocab_refs = refs[:n_layer], refs[n_layer:]
    pl.run_scoped(
        lambda *own: layer_part(
            *tables, lengths, residual, stored, frequency, in_lines, post_lines, final_lines,
            q_gain, k_gain, fin, *layer_refs, *own,
        ),
        *n_layer_own,
    )
    pl.run_scoped(
        lambda *own: vocab_part(fin, table, actions, out_ref, *vocab_refs, *own), *n_vocab_own
    )


def whole(
    tables, lengths, residual, stored, frequency, in_gain, q_gain, k_gain, post_gain, final_gain,
    vocab_table, actions,
):
    tokens, depth = residual.shape
    n_blk, blk_rows, width = stored.shape
    vocab_rows = vocab_table.shape[0]
    head = q_gain.shape[0]
    share = tokens // 16
    bf16, f32 = jnp.bfloat16, jnp.float32
    n_rows = depth // blk_rows
    n_pieces = 7
    piece = depth // n_pieces
    reach = WINDOW // tokens
    chunk = width // 3
    third = depth // 3
    dma = pltpu.SemaphoreType.DMA
    smem = pl.BlockSpec(memory_space=pltpu.SMEM)
    vmem = pl.BlockSpec(memory_space=VMEM)
    far = pl.BlockSpec(memory_space=pl.ANY)
    layer_refs = [
        VMEM((16, blk_rows, chunk), bf16),
        VMEM((16, blk_rows, chunk), bf16),
        VMEM((16, blk_rows, chunk), bf16),
        VMEM((3, 2, 4, n_blk, blk_rows, chunk), bf16),
        VMEM((reach + 1, tokens, 2 * head), bf16),
        VMEM((n_pieces, 8, share, piece), bf16),
        VMEM((n_pieces, 8, share, piece), bf16),
        dma((2,)),
        dma((3, 16)), dma((3, 16)),
        dma((3, 4, n_blk)), dma((3, 4, n_blk)),
        dma((3, 2, 2, n_blk)), dma((3, 2, 2, n_blk)),
        dma((3, 2, n_blk)), dma((3, 2, n_blk)),
        dma((reach,)), dma((reach,)),
        dma((n_pieces,)), dma((n_pieces,)),
        dma((n_pieces, 8)), dma((n_pieces, 8)),
    ]
    layer_own = [
        VMEM((1, depth), f32),
        VMEM((1, depth), f32),
        VMEM((1, depth), f32),
        VMEM((tokens, head), f32),
        VMEM((tokens, head), f32),
        VMEM((tokens, depth), bf16),
        VMEM((n_blk, blk_rows, width), bf16),
        VMEM((3, 16, blk_rows, chunk), bf16),
        VMEM((n_rows, tokens, 128), bf16),
        VMEM((tokens, 2 * chunk), f32),
        VMEM((2, tokens, head), bf16),
        VMEM((8, 2, share, 2 * head), bf16),
        VMEM((n_rows, blk_rows, chunk), bf16),
        VMEM((n_pieces, 8, share, piece), bf16),
        VMEM((n_pieces, 8, share, piece), bf16),
        VMEM((share, depth), f32),
    ]
    vocab_refs = [
        VMEM((3, 4, 4, 2, 4, share, third), bf16),
        VMEM((8, 8, 128), f32),
        VMEM((16, 8, 128), f32),
        dma((3,)),
        dma((3, 3)), dma((3, 3)),
        dma((3, 4)), dma((3, 4)),
        dma((3, 4, 4)), dma((3, 4, 4)),
        dma((3, 4)), dma((3, 4)),
        dma((3, 4, 4)), dma((3, 4, 4)),
        dma((8,)), dma((8,)),
        dma((16,)), dma((16,)),
    ]
    vocab_own = [
        VMEM((3, vocab_rows, third), bf16),
        VMEM((128, share, vocab_rows), f32),
        VMEM((128, share, 128), f32),
        VMEM((128, share, 128), f32),
        VMEM((128, share, 1), jnp.int32),
        VMEM((8, 8, 128), f32),
        VMEM((8, 128), f32),
    ]
    counts = (len(tables), len(layer_refs), layer_own, vocab_own)
    return pl.pallas_call(
        functools.partial(whole_kernel, counts),
        out_shape=jax.ShapeDtypeStruct((2, 128), f32),
        in_specs=[smem] * 5 + [far] * 2 + [vmem] * 6 + [far, vmem],
        out_specs=vmem,
        scratch_shapes=[VMEM((share, depth), bf16)] + layer_refs + vocab_refs,
        compiler_params=pltpu.CompilerParams(
            collective_id=1, has_side_effects=True, vmem_limit_bytes=63 * 2**20
        ),
        name="whole",
    )(
        *tables, lengths, residual, stored, frequency,
        in_gain.reshape(-1, 128), post_gain.reshape(-1, 128), final_gain.reshape(-1, 128),
        q_gain[None], k_gain[None], vocab_table, actions.reshape(-1, 128),
    )


def rope_frequency(head):
    half_size = head // 2
    frequency = rope_base ** (-2.0 * np.arange(half_size, dtype=np.float64) / head)
    return jnp.asarray(np.concatenate([frequency, frequency])[None].astype(np.float32))


def block_tables(block_list, ctx_index, tp_index, ctx_count, tp_count, blocks_dev):
    rows_per_reader = blocks_dev * ctx_count
    grid = block_list.reshape(ctx_count, tp_count, blocks_dev)
    readers = (grid * 1171) >> 16
    my_readers = lax.dynamic_slice(
        readers, (ctx_index, tp_index, 0), (1, 1, blocks_dev)
    ).reshape(-1)
    slots = jnp.arange(blocks_dev, dtype=jnp.int32)
    sources = jnp.arange(tp_count, dtype=jnp.int32)
    send_slot = jnp.sum(jnp.where(my_readers[None, :] == sources[:, None], slots[None, :], 0), axis=1)
    hit = readers == tp_index
    present = jnp.any(hit, axis=2)
    row_index = jnp.sum(jnp.where(hit, grid - readers * rows_per_reader, 0), axis=2)
    before = sources[None, :] < sources[:, None]
    rank = jnp.sum((present[:, None, :] & before[None]).astype(jnp.int32), axis=2)
    chosen = (rank[:, None, :] == slots[None, :, None]) & present[:, None, :]
    row_of = jnp.sum(jnp.where(chosen, row_index[:, None, :], 0), axis=2)
    keep_all = jnp.sum(jnp.where(chosen, sources[None, None, :], 0), axis=2)
    keep_from = lax.dynamic_index_in_dim(keep_all, ctx_index, 0, False)
    ids = jnp.arange(ctx_count, dtype=jnp.int32)
    side = (ids // 4 + ctx_index // 4) % 2
    slot = (side * 4 + (ids + 4 - ctx_index % 4) % 4)[:, None] * blocks_dev + slots[None, :]
    rows = jnp.arange(rows_per_reader, dtype=jnp.int32)
    slot_of = jnp.sum(jnp.where(row_of.reshape(1, -1) == rows[:, None], slot.reshape(1, -1), 0), axis=1)
    return send_slot, keep_from, row_of.reshape(-1), slot_of


def shards(
    residual,
    stored_blocks,
    block_list,
    lengths,
    in_gain,
    q_gain,
    k_gain,
    post_gain,
    final_gain,
    vocab_table,
    actions,
    old_logprob,
):
    ctx_count = lax.axis_size("ctx")
    tp_count = lax.axis_size("tp")
    ctx_index = lax.axis_index("ctx")
    tp_index = lax.axis_index("tp")
    row_count = residual.shape[0]
    share_rows = row_count // tp_count
    tables = block_tables(
        block_list, ctx_index, tp_index, ctx_count, tp_count, stored_blocks.shape[0]
    )
    all_rows = whole(
        tables, lengths, residual, stored_blocks, rope_frequency(HEAD_DIM),
        in_gain, q_gain, k_gain, post_gain, final_gain, vocab_table, actions,
    )
    ref_logprob = lax.dynamic_slice_in_dim(all_rows.reshape(-1), tp_index * share_rows, share_rows, 0)
    return (ref_logprob, old_logprob - ref_logprob)


def solution(mesh):
    return jax.shard_map(
        shards,
        mesh=mesh,
        in_specs=(
            P("ctx", None),
            P(("ctx", "tp"), None, None),
            P(),
            P(),
            P(),
            P(),
            P(),
            P(),
            P(),
            P(("ctx", "tp"), None),
            P(),
            P(("ctx", "tp")),
        ),
        out_specs=(P(("ctx", "tp")), P(("ctx", "tp"))),
        check_vma=False,
    )
```

```python
import functools

import jax
import jax.numpy as jnp
import numpy as np
from jax import lax
from jax.experimental import pallas as pl
from jax.experimental.pallas import tpu as pltpu
from jax.sharding import PartitionSpec as P

HEADS = 32
KV_HEADS = 16
HEAD_DIM = 128
WINDOW = 1024
QUERY_SCALAR = 168


epsilon = 1e-06
soft_cap = 30.0
rope_base = 10000.0
MESH = pl.DeviceIdType.MESH
VMEM = pltpu.VMEM
A2_REL = (0, 1, 3, 2)


def coords():
    c = lax.axis_index("ctx")
    t = lax.axis_index("tp")
    return t // 4, (c // 4) * 2 + (t // 2) % 2, c % 4, t % 2


def device_of(x, y, z, k):
    x, y, z, k = x % 4, y % 4, z % 4, k % 2
    return ((y // 2) * 4 + z, x * 4 + (y % 2) * 2 + k)


def axis_of(part, place):
    return (part + place) % 3


def shifted(axis, steps):
    where = list(coords())
    where[axis] = where[axis] + steps
    return device_of(*where)


def sibling():
    x, y, z, k = coords()
    return device_of(x, y, z, k + 1)


def greet(peers, meanwhile=None):
    barrier = pltpu.get_barrier_semaphore()
    for peer in peers:
        pl.semaphore_signal(barrier, inc=1, device_id=peer, device_id_type=MESH)
    if meanwhile is not None:
        meanwhile()
    pl.semaphore_wait(barrier, len(peers))


def vocab_part(
    fin_ref, table_ref, actions_ref, out_ref, buf, r1, r2,
    table_sem, s1, v1, s2, v2, s3, v3, sf, vf, sk, vk, sa, va, sb, vb,
    table, acc, part_exp, part_hit, column, st1, st2,
):
    ctx = lax.axis_index("ctx")
    tp = lax.axis_index("tp")
    core = tp % 2
    own = coords()[:3]
    width = fin_ref.shape[1] // 3
    rows = fin_ref.shape[0]
    vocab_rows = table.shape[1]

    def table_copy(p):
        return pltpu.make_async_copy(
            table_ref.at[:, pl.ds(p * width, width)], table.at[p], table_sem.at[p]
        )

    for p in range(3):
        table_copy(p).start()
    for p in range(3):
        buf[p, 0, 0, core, 0] = fin_ref[:, pl.ds(p * width, width)]
    c_peer = lambda off: ((ctx + off) % 8, tp)
    t_peer = lambda off: (ctx, (tp + off) % 16)

    def send(src, dst, send_sem, recv_sem, peer):
        return pltpu.make_async_remote_copy(
            src_ref=src, dst_ref=dst, send_sem=send_sem, recv_sem=recv_sem,
            device_id=peer, device_id_type=MESH,
        )

    def first(p, step):
        return send(
            buf.at[p, 0, 0, core, 0], buf.at[p, 0, 0, core, 4 - step],
            s1.at[p, step - 1], v1.at[p, step - 1], shifted(axis_of(p, 0), step),
        )

    def second(p, step):
        slot = A2_REL.index(4 - step)
        return send(
            buf.at[p, 0, 0, core], buf.at[p, 0, slot, core],
            s2.at[p, slot], v2.at[p, slot], shifted(axis_of(p, 1), step),
        )

    def third(p, q, step):
        return send(
            buf.at[p, 0, q, core], buf.at[p, 4 - step, q, core],
            s3.at[p, 4 - step, q], v3.at[p, 4 - step, q], shifted(axis_of(p, 2), step),
        )

    def passed(p, slab, q, step):
        return send(
            buf.at[p, slab, q, core], buf.at[p, 2, q, core],
            sf.at[p, q], vf.at[p, q], shifted(axis_of(p, 2), step),
        )

    def across(p, slab, q):
        return send(
            buf.at[p, slab, q, core], buf.at[p, slab, q, core],
            sk.at[p, slab, q], vk.at[p, slab, q], sibling(),
        )

    for step in (1, 3, 2):
        for p in range(3):
            first(p, step).start()

    def clear(d, carry):
        acc[d] = jnp.zeros((rows, vocab_rows), jnp.float32)
        return carry

    lax.fori_loop(0, 128, clear, 0)
    lanes = lax.broadcasted_iota(jnp.int32, (128, 128), 1)
    diagonal = lax.broadcasted_iota(jnp.int32, (128, 128), 0) == lanes

    def turn(j, carry):
        line = jnp.broadcast_to(actions_ref[pl.ds(j, 1)].astype(jnp.float32), (128, 128))
        turned = jnp.sum(jnp.where(diagonal, line, 0.0), axis=1, keepdims=True)
        column[pl.ds(j * 8, 8)] = turned.astype(jnp.int32).reshape(8, rows, 1)
        return carry

    lax.fori_loop(0, actions_ref.shape[0], turn, 0)

    for p in range(3):
        for step in (1, 3, 2):
            first(p, step).wait_recv()
    for step in (3, 1, 2):
        for p in range(3):
            second(p, step).start()
    for p in range(3):
        for step in (1, 3):
            third(p, 0, step).start()
        across(p, 0, 0).start()

    def own_chunk(p, q):
        second(p, 4 - A2_REL[q]).wait_recv()
        for step in (1, 3):
            third(p, q, step).start()
        across(p, 0, q).start()

    for p in range(3):
        own_chunk(p, 1)

    def slab_of(g, i):
        return jnp.where(g < 2, 0, jnp.where(g > 5, 2, 3 - 2 * i))

    def row_of(g, i):
        return jnp.where(g < 2, g * 2 + i, jnp.where(g > 5, (g - 6) * 2 + i, g - 2))

    def arrivals(g):
        @pl.when(g == 1)
        def _():
            for q in (2, 3):
                for p in range(3):
                    own_chunk(p, q)

        @pl.when((g > 1) & (g < 6))
        def _():
            q = g - 2
            for p in range(3):
                third(p, q, 1).wait_recv()

                @pl.when(q % 2 == 0)
                def _():
                    passed(p, 3, q, 1).start()

                across(p, 3, q).start()
                third(p, q, 3).wait_recv()

                @pl.when(q % 2 == 1)
                def _():
                    passed(p, 1, q, 3).start()

                across(p, 1, q).start()

        @pl.when((g > 5) & (g < 8))
        def _():
            for i in range(2):
                q = (g - 6) * 2 + i
                for p in range(3):
                    passed(p, 3, q, 1).wait_recv()
                    across(p, 2, q).start()

    def place(axis_values, k):
        x, y, z = axis_values
        return ((y // 2) * 4 + z) * 16 + x * 4 + (y % 2) * 2 + k

    first_id = (ctx * 16 + tp) * vocab_rows
    ids = first_id + lax.broadcasted_iota(jnp.int32, (rows, vocab_rows), 1)

    def fold(v):
        total = v[:, :128]
        for i in range(1, vocab_rows // 128):
            total = total + v[:, i * 128:(i + 1) * 128]
        return total

    def tail(rel):
        at = place([(own[i] + rel[i]) % 4 for i in range(3)], 0)
        for kk in range(2):
            capped = soft_cap * jnp.tanh(acc[at + kk] * (1.0 / soft_cap))
            hit = ids == column[at + kk]
            part_exp[at + kk] = fold(jnp.exp(capped))
            part_hit[at + kk] = fold(jnp.where(hit, capped, 0.0))

    def near(digit):
        return digit + digit // 2

    def early_tail(i, carry):
        for j in range(3):
            tail((near(i // 3), near(i % 3), near(j)))
        return carry

    def middle_tail(i, carry):
        for j in range(3):
            tail((2, near(j), i))
            tail((i, 2, near(j)))
            tail((near(j), i, 2))
        return carry

    def late_tail(i, carry):
        for j in range(4):
            tail((2, j, 2 + i))
        tail((2, 2, i))
        tail((i, 2, 2))
        for j in range(2):
            tail((3, 2, 2 * i + j))
        return carry

    def group(g, carry):
        @pl.when(g == 7)
        def _():
            lax.fori_loop(0, 2, middle_tail, 0)

        slabs, lines = [slab_of(g, i) for i in range(2)], [row_of(g, i) for i in range(2)]
        for p in range(3):
            for i in range(2):
                across(p, slabs[i], lines[i]).wait_recv()

            @pl.when(g == 0)
            def _():
                table_copy(p).wait()

            lhs = jnp.concatenate(
                [buf[p, slabs[i], lines[i]].reshape(8 * rows, width) for i in range(2)], axis=0
            )
            got = lax.dot_general(
                lhs, table[p], (((1,), (1,)), ((), ())), preferred_element_type=jnp.float32
            )
            a1, a2, a3 = (axis_of(p, i) for i in range(3))
            for i in range(2):
                rel2 = jnp.where(lines[i] < 2, lines[i], 5 - lines[i])
                for kk in range(2):
                    for r1_ in range(4):
                        at = [None] * 3
                        at[a1] = (own[a1] + r1_) % 4
                        at[a2] = (own[a2] + rel2) % 4
                        at[a3] = (own[a3] + slabs[i]) % 4
                        d = place(at, kk)
                        m = (i * 2 + kk) * 4 + r1_
                        value = got[m * rows:(m + 1) * rows]
                        acc[d] = acc[d] + value
            if p == 0:
                @pl.when(g == 6)
                def _():
                    lax.fori_loop(0, 9, early_tail, 0)

                arrivals(g + 1)
        return carry

    lax.fori_loop(0, 8, group, 0)

    lax.fori_loop(0, 2, late_tail, 0)
    for j in range(3):
        tail((near(j), 3, 2))
    ones = jnp.ones((8, 128), jnp.float32)
    for c in range(8):
        sums = [
            lax.dot_general(
                ones, part[pl.ds(c * 16, 16)].reshape(16 * rows, 128), (((1,), (1,)), ((), ())),
                preferred_element_type=jnp.float32, precision=lax.Precision.HIGHEST,
            )
            for part in (part_exp, part_hit)
        ]
        st1[c] = jnp.concatenate(
            [v[:1, i * 128:(i + 1) * 128] for v in (sums + sums) for i in range(2)], axis=0
        )

    def stage1(off):
        return send(st1.at[(ctx + off) % 8], r1.at[off], sa.at[off], va.at[off], c_peer(off))

    def stage2(off):
        return send(st2, r2.at[off], sb.at[off], vb.at[off], t_peer(off))

    for off in range(1, 8):
        stage1(off).start()
    total = st1[ctx]
    for off in range(1, 8):
        stage1(off).wait_recv()
        total = total + r1[off]
    st2[...] = total
    for off in range(1, 16):
        stage2(off).start()
    for off in range(1, 16):
        stage2(off).wait_recv()
        total = total + r2[off]
    out_ref[...] = total[2:4] - jnp.log(total[:2])

    for p in range(3):
        for step in (1, 2, 3):
            first(p, step).wait_send()
            second(p, step).wait_send()
        for q in range(4):
            third(p, q, 1).wait_send()
            third(p, q, 3).wait_send()
            passed(p, 3, q, 1).wait_send()
            for slab in range(4):
                across(p, slab, q).wait_send()
    for off in range(1, 8):
        stage1(off).wait_send()
    for off in range(1, 16):
        stage2(off).wait_send()


CHUNK_AT = (1, 0, 2)
Z_FIRST = (0, 0, 2)


def layer_part(
    send_slot, keep_from, row_of, slot_of,
    lengths, residual_hbm, stored_hbm, frequency, in_lines, post_lines, final_lines, q_gain, k_gain, out_ref,
    got_0, got_1, got_2, held, kv, half_in, part_in,
    load_sem, x_s, x_r, y_s, y_r, z_s, z_r, f_s, f_r, h_s, h_r, c_s, c_r, p_s, p_r,
    in_gain, post_gain, final_gain, cos_ref, sin_ref, residual_ref, stored_ref, out, cols, proj,
    query, mixed, wout, half_out, part_out, summed,
):
    ctx = lax.axis_index("ctx")
    tp = lax.axis_index("tp")
    core = tp % 2
    chip = tp // 2
    y_hi, z = ctx // 4, ctx % 4
    n_blk = stored_ref.shape[0]
    blk_rows = stored_ref.shape[1]
    tokens, depth = residual_ref.shape
    head = q_gain.shape[1]

    def send(src, dst, send_sem, recv_sem, peer):
        return pltpu.make_async_remote_copy(
            src_ref=src, dst_ref=dst, send_sem=send_sem, recv_sem=recv_sem,
            device_id=peer, device_id_type=MESH,
        )

    t_peer = lambda off: (ctx, (tp + off) % 16)
    z_peer = lambda step: (y_hi * 4 + (z + step) % 4, tp)
    y_peer = ((ctx + 4) % 8, tp)

    got = (got_0, got_1, got_2)

    def swap(i, off):
        return send(
            out.at[i, (tp + off) % 16], got[i].at[tp], x_s.at[i, off], x_r.at[i, off], t_peer(off)
        )

    stored_copy = pltpu.make_async_copy(stored_hbm, stored_ref, load_sem.at[0])
    residual_copy = pltpu.make_async_copy(residual_hbm, residual_ref, load_sem.at[1])
    stored_copy.start()
    residual_copy.start()
    chunk = out.shape[3]

    def stage(t, carry):
        block = stored_ref[send_slot[t]]
        for i, at in enumerate(CHUNK_AT):
            out[i, t] = block[:, at * chunk:(at + 1) * chunk]
        return carry

    def stage_all():
        stored_copy.wait()
        lax.fori_loop(0, 16, stage, 0)

    x_at, y_at, z_at, k_at = coords()
    far_y = device_of(x_at, y_at - 1 + 2 * (y_at % 2), z_at, k_at)
    greet(
        [((ctx + o) % 8, tp) for o in range(1, 8)] + [t_peer(o) for o in range(1, 16)] + [far_y],
        stage_all,
    )

    def start_swap(off, carry):
        swap(0, off).start()
        return carry

    lax.fori_loop(1, 16, start_swap, 0)
    residual_copy.wait()
    for gain, lines in ((in_gain, in_lines), (post_gain, post_lines), (final_gain, final_lines)):
        for i in range(lines.shape[0]):
            gain[:, i * 128:(i + 1) * 128] = lines[i:i + 1]
    for i in range(3):
        got[i][tp] = out[i, tp]

    step_rows = 32

    def norm_rows(i, carry):
        at = pl.ds(pl.multiple_of(i * step_rows, step_rows), step_rows)
        x = residual_ref[at].astype(jnp.float32)
        scale = lax.rsqrt(jnp.mean(x * x, axis=-1, keepdims=True) + epsilon)
        n = (x * scale * in_gain[...]).astype(jnp.bfloat16)
        for r in range(depth // blk_rows):
            cols[r, at, :blk_rows] = n[:, r * blk_rows:(r + 1) * blk_rows]
        return carry

    lax.fori_loop(0, tokens // step_rows, norm_rows, 0)
    proj[...] = jnp.zeros_like(proj)
    row_ids = ctx * tokens + lax.broadcasted_iota(jnp.int32, (tokens, 1), 0)
    seg_start = jnp.zeros_like(row_ids)
    begin = jnp.int32(0)
    for i in range(lengths.shape[0]):
        seg_start = jnp.maximum(seg_start, jnp.where(begin <= row_ids, begin, 0))
        begin = begin + lengths[i]
    angle = (row_ids - seg_start).astype(jnp.float32) * frequency[...]
    low = lax.broadcasted_iota(jnp.int32, angle.shape, 1) < head // 2
    cos_ref[...] = jnp.cos(angle)
    sin_ref[...] = jnp.where(low, -jnp.sin(angle), jnp.sin(angle))

    def early(i):
        return n_blk - Z_FIRST[i]

    def y_copy(i, zz, k):
        return send(
            held.at[i, 0, zz, k], held.at[i, 1, zz, k], y_s.at[i, zz, k], y_r.at[i, zz, k], y_peer
        )

    def z_copy(i, yy, step, k):
        j = 0 if step == 1 else 1
        return send(
            held.at[i, yy, 0, k], held.at[i, yy, 4 - step, k],
            z_s.at[i, yy, j, k], z_r.at[i, yy, j, k], z_peer(step),
        )

    def f_copy(i, yy, step, k):
        return send(
            held.at[i, yy, 3 if step == 1 else 1, k], held.at[i, yy, 2, k],
            f_s.at[i, yy, k], f_r.at[i, yy, k], z_peer(step),
        )

    def blocks(body, low=0, high=None):
        def run(k, carry):
            body(k)
            return carry

        lax.fori_loop(low, n_blk if high is None else high, run, 0)

    def own(i):
        def wait(off, carry):
            swap(i, off).wait_recv()
            return carry

        def body(k):
            held[i, 0, 0, k] = got[i][keep_from[k]]
            y_copy(i, 0, k).start()
            z_copy(i, 0, 1, k).start()
            z_copy(i, 0, 3, k).start()
            if i < 2:
                swap(i + 1, 2 * k + 1).start()
                swap(i + 1, 2 * k + 2).start()

        lax.fori_loop(1, 16, wait, 0)
        blocks(body)
        if i < 2:
            swap(i + 1, 15).start()

    def partner(i):
        def body(k):
            y_copy(i, 0, k).wait_recv()

            @pl.when(k < early(i))
            def _():
                z_copy(i, 1, 1, k).start()
                z_copy(i, 1, 3, k).start()

            term(i, 0, 0, k)
            term(i, 1, 0, k)

        blocks(body)

    def side(i, yy):
        half = 4 if yy == 0 else early(i) // 2

        def body(k):
            z_copy(i, yy, 1, k).wait_recv()

            @pl.when(k < half)
            def _():
                f_copy(i, yy, 1, k).start()

            z_copy(i, yy, 3, k).wait_recv()

            @pl.when(k >= half)
            def _():
                f_copy(i, yy, 3, k).start()

            if yy == 0:
                @pl.when(k >= early(i))
                def _():
                    y_copy(i, 3, k).start()
                    y_copy(i, 1, k).start()

            term(i, yy, 3, k)
            term(i, yy, 1, k)

        def across(k):
            y_copy(i, 3, k).wait_recv()
            y_copy(i, 1, k).wait_recv()
            term(i, 1, 3, k)
            term(i, 1, 1, k)

        if yy == 0:
            blocks(body)
        else:
            blocks(body, 0, early(i))
            blocks(across, early(i))

    def far(i, yy):
        def body(k):
            f_copy(i, yy, 1, k).wait_recv()
            if yy == 0:
                @pl.when(k >= early(i))
                def _():
                    y_copy(i, 2, k).start()
            term(i, yy, 2, k)

        def across(k):
            y_copy(i, 2, k).wait_recv()
            term(i, 1, 2, k)

        if yy == 0:
            blocks(body)
        else:
            blocks(body, 0, early(i))
            blocks(across, early(i))

    def term(i, yy, zz, k):
        if CHUNK_AT[i] < 2:
            c = (y_hi + yy) % 2 * 4 + (z + zz) % 4
            at = CHUNK_AT[i] * chunk
            proj[:, at:at + chunk] += jnp.dot(
                cols[row_of[c * n_blk + k], :, :blk_rows], held[i, yy, zz, k],
                preferred_element_type=jnp.float32,
            )

    own(0)
    partner(0)
    side(0, 0)
    own(1)
    side(0, 1)
    partner(1)
    far(0, 0)
    side(1, 0)
    far(0, 1)

    def heads(at, gain):
        e = proj[:, pl.ds(at * head, head)]
        scale = lax.rsqrt(jnp.mean(e * e, axis=-1, keepdims=True) + epsilon)
        e = e * scale * gain[...]
        return (e * cos_ref[...] + pltpu.roll(e, head // 2, 1) * sin_ref[...]).astype(jnp.bfloat16)

    reach = kv.shape[0] - 1
    kv[reach, :, :head] = heads(2, k_gain)
    kv[reach, :, head:] = proj[:, 3 * head:].astype(jnp.bfloat16)

    def halo(step):
        return send(
            kv.at[reach], kv.at[reach - step], h_s.at[step - 1], h_r.at[step - 1],
            ((ctx + step) % 8, tp),
        )

    for step in range(1, reach + 1):
        @pl.when(ctx + step < 8)
        def _():
            halo(step).start()

        @pl.when(ctx < step)
        def _():
            kv[reach - step] = jnp.zeros(kv.shape[1:], kv.dtype)

    side(1, 1)
    own(2)
    far(1, 0)
    partner(2)
    far(1, 1)
    for h in range(2):
        query[h] = heads(h, q_gain)
    side(2, 0)
    side(2, 1)
    for step in range(1, reach + 1):
        @pl.when(ctx >= step)
        def _():
            halo(step).wait_recv()

    span = (reach + 1) * tokens
    key_rows = kv[:, :, :head].reshape(span, head)
    value_rows = kv[:, :, head:].reshape(span, head)
    q_ids = ctx * tokens + lax.broadcasted_iota(jnp.int32, (tokens, span), 0)
    k_ids = (ctx - reach) * tokens + lax.broadcasted_iota(jnp.int32, (tokens, span), 1)
    visible = (k_ids <= q_ids) & (q_ids - k_ids < WINDOW) & (k_ids >= seg_start)
    for h in range(2):
        scores = lax.dot_general(
            query[h], key_rows, (((1,), (1,)), ((), ())), preferred_element_type=jnp.float32
        ) * QUERY_SCALAR ** (-0.5)
        probs = jnp.where(visible, jnp.exp(scores), 0.0)
        probs = (probs / jnp.sum(probs, axis=1, keepdims=True)).astype(jnp.bfloat16)
        heard = jnp.dot(probs, value_rows, preferred_element_type=jnp.float32).astype(jnp.bfloat16)
        mixed[:, :, :, h * head:(h + 1) * head] = heard.reshape(8, 2, tokens // 16, head)

    far(2, 0)
    far(2, 1)

    share = tokens // 16
    per = wout.shape[0] // half_out.shape[0]
    piece = per * blk_rows
    other = (tp // 2) * 2 + (1 - core)

    def product(which, n):
        rows = mixed[:, which].reshape(8 * share, 2 * head)
        block = wout[pl.ds(n * per, per)].reshape(piece, 2 * head)
        return lax.dot_general(
            rows, block, (((1,), (1,)), ((), ())), preferred_element_type=jnp.float32
        ).reshape(8, share, piece)

    def between(n):
        return send(half_out.at[n], half_in.at[n], c_s.at[n], c_r.at[n], (ctx, other))

    def to_chip(n, off):
        there = (chip + off) % 8
        return send(
            part_out.at[n, there], part_in.at[n, off], p_s.at[n, off], p_r.at[n, off],
            (ctx, there * 2 + core),
        )

    n_pieces = half_out.shape[0]

    def order(r, carry):
        wout[r] = held.at[2].reshape(8 * n_blk, blk_rows, chunk)[slot_of[r]]
        return carry

    def give(n):
        lax.fori_loop(n * per, (n + 1) * per, order, 0)
        half_out[n] = product(1 - core, n).astype(jnp.bfloat16)
        between(n).start()

    def take(n, carry):
        mine = product(core, n)
        between(n).wait_recv()
        part_out[n] = (mine + half_in[n].astype(jnp.float32)).astype(jnp.bfloat16)
        for off in (2, 6, 1, 4, 3, 7, 5):
            to_chip(n, off).start()

        @pl.when(n + 2 < n_pieces)
        def _():
            give(n + 2)

        return carry

    give(0)
    give(1)
    lax.fori_loop(0, n_pieces, take, 0)
    def swapped(off, carry):
        for i in range(3):
            swap(i, off).wait_send()
        return carry

    lax.fori_loop(1, 16, swapped, 0)
    for i in range(3):
        def sent(k):
            y_copy(i, 0, k).wait_send()
            z_copy(i, 0, 1, k).wait_send()
            z_copy(i, 0, 3, k).wait_send()
            f_copy(i, 0, 1, k).wait_send()

        def sent_z(k):
            z_copy(i, 1, 1, k).wait_send()
            z_copy(i, 1, 3, k).wait_send()
            f_copy(i, 1, 1, k).wait_send()

        def sent_y(k):
            for zz in range(1, 4):
                y_copy(i, zz, k).wait_send()

        blocks(sent)
        blocks(sent_z, 0, early(i))
        blocks(sent_y, early(i))
    for step in range(1, reach + 1):
        @pl.when(ctx + step < 8)
        def _():
            halo(step).wait_send()

    def halves_sent(n, carry):
        between(n).wait_send()
        return carry

    lax.fori_loop(0, n_pieces, halves_sent, 0)
    for n in range(n_pieces):
        total = part_out[n, chip].astype(jnp.float32)
        for off in range(1, 8):
            to_chip(n, off).wait_recv()
            total = total + part_in[n, off].astype(jnp.float32)
        summed[:, n * piece:(n + 1) * piece] = total

    def rms(values, gain):
        return values * lax.rsqrt(jnp.mean(values * values, axis=-1, keepdims=True) + epsilon) * gain[...]

    mine = residual_ref[pl.ds(pl.multiple_of(tp * share, share), share)].astype(jnp.float32)
    hidden = mine + rms(summed[...], post_gain)
    out_ref[...] = rms(hidden, final_gain).astype(jnp.bfloat16)

    def parts_sent(n, carry):
        for off in range(1, 8):
            to_chip(n, off).wait_send()
        return carry

    lax.fori_loop(0, n_pieces, parts_sent, 0)


def whole_kernel(counts, *refs):
    n_tables, n_layer, n_layer_own, n_vocab_own = counts
    tables, refs = refs[:n_tables], refs[n_tables:]
    (lengths, residual, stored, frequency, in_lines, post_lines, final_lines, q_gain, k_gain,
     table, actions, out_ref, fin), refs = refs[:13], refs[13:]
    layer_refs, vocab_refs = refs[:n_layer], refs[n_layer:]
    pl.run_scoped(
        lambda *own: layer_part(
            *tables, lengths, residual, stored, frequency, in_lines, post_lines, final_lines,
            q_gain, k_gain, fin, *layer_refs, *own,
        ),
        *n_layer_own,
    )
    pl.run_scoped(
        lambda *own: vocab_part(fin, table, actions, out_ref, *vocab_refs, *own), *n_vocab_own
    )


def whole(
    tables, lengths, residual, stored, frequency, in_gain, q_gain, k_gain, post_gain, final_gain,
    vocab_table, actions,
):
    tokens, depth = residual.shape
    n_blk, blk_rows, width = stored.shape
    vocab_rows = vocab_table.shape[0]
    head = q_gain.shape[0]
    share = tokens // 16
    bf16, f32 = jnp.bfloat16, jnp.float32
    n_rows = depth // blk_rows
    n_pieces = 7
    piece = depth // n_pieces
    reach = WINDOW // tokens
    chunk = width // 3
    third = depth // 3
    dma = pltpu.SemaphoreType.DMA
    smem = pl.BlockSpec(memory_space=pltpu.SMEM)
    vmem = pl.BlockSpec(memory_space=VMEM)
    far = pl.BlockSpec(memory_space=pl.ANY)
    layer_refs = [
        VMEM((16, blk_rows, chunk), bf16),
        VMEM((16, blk_rows, chunk), bf16),
        VMEM((16, blk_rows, chunk), bf16),
        VMEM((3, 2, 4, n_blk, blk_rows, chunk), bf16),
        VMEM((reach + 1, tokens, 2 * head), bf16),
        VMEM((n_pieces, 8, share, piece), bf16),
        VMEM((n_pieces, 8, share, piece), bf16),
        dma((2,)),
        dma((3, 16)), dma((3, 16)),
        dma((3, 4, n_blk)), dma((3, 4, n_blk)),
        dma((3, 2, 2, n_blk)), dma((3, 2, 2, n_blk)),
        dma((3, 2, n_blk)), dma((3, 2, n_blk)),
        dma((reach,)), dma((reach,)),
        dma((n_pieces,)), dma((n_pieces,)),
        dma((n_pieces, 8)), dma((n_pieces, 8)),
    ]
    layer_own = [
        VMEM((1, depth), f32),
        VMEM((1, depth), f32),
        VMEM((1, depth), f32),
        VMEM((tokens, head), f32),
        VMEM((tokens, head), f32),
        VMEM((tokens, depth), bf16),
        VMEM((n_blk, blk_rows, width), bf16),
        VMEM((3, 16, blk_rows, chunk), bf16),
        VMEM((n_rows, tokens, 128), bf16),
        VMEM((tokens, 2 * chunk), f32),
        VMEM((2, tokens, head), bf16),
        VMEM((8, 2, share, 2 * head), bf16),
        VMEM((n_rows, blk_rows, chunk), bf16),
        VMEM((n_pieces, 8, share, piece), bf16),
        VMEM((n_pieces, 8, share, piece), bf16),
        VMEM((share, depth), f32),
    ]
    vocab_refs = [
        VMEM((3, 4, 4, 2, 4, share, third), bf16),
        VMEM((8, 8, 128), f32),
        VMEM((16, 8, 128), f32),
        dma((3,)),
        dma((3, 3)), dma((3, 3)),
        dma((3, 4)), dma((3, 4)),
        dma((3, 4, 4)), dma((3, 4, 4)),
        dma((3, 4)), dma((3, 4)),
        dma((3, 4, 4)), dma((3, 4, 4)),
        dma((8,)), dma((8,)),
        dma((16,)), dma((16,)),
    ]
    vocab_own = [
        VMEM((3, vocab_rows, third), bf16),
        VMEM((128, share, vocab_rows), f32),
        VMEM((128, share, 128), f32),
        VMEM((128, share, 128), f32),
        VMEM((128, share, 1), jnp.int32),
        VMEM((8, 8, 128), f32),
        VMEM((8, 128), f32),
    ]
    counts = (len(tables), len(layer_refs), layer_own, vocab_own)
    return pl.pallas_call(
        functools.partial(whole_kernel, counts),
        out_shape=jax.ShapeDtypeStruct((2, 128), f32),
        in_specs=[smem] * 5 + [far] * 2 + [vmem] * 6 + [far, vmem],
        out_specs=vmem,
        scratch_shapes=[VMEM((share, depth), bf16)] + layer_refs + vocab_refs,
        compiler_params=pltpu.CompilerParams(
            collective_id=1, has_side_effects=True, vmem_limit_bytes=63 * 2**20
        ),
        name="whole",
    )(
        *tables, lengths, residual, stored, frequency,
        in_gain.reshape(-1, 128), post_gain.reshape(-1, 128), final_gain.reshape(-1, 128),
        q_gain[None], k_gain[None], vocab_table, actions.reshape(-1, 128),
    )


def rope_frequency(head):
    half_size = head // 2
    frequency = rope_base ** (-2.0 * np.arange(half_size, dtype=np.float64) / head)
    return jnp.asarray(np.concatenate([frequency, frequency])[None].astype(np.float32))


def block_tables(block_list, ctx_index, tp_index, ctx_count, tp_count, blocks_dev):
    rows_per_reader = blocks_dev * ctx_count
    grid = block_list.reshape(ctx_count, tp_count, blocks_dev)
    readers = (grid * 1171) >> 16
    my_readers = lax.dynamic_slice(
        readers, (ctx_index, tp_index, 0), (1, 1, blocks_dev)
    ).reshape(-1)
    slots = jnp.arange(blocks_dev, dtype=jnp.int32)
    sources = jnp.arange(tp_count, dtype=jnp.int32)
    send_slot = jnp.sum(jnp.where(my_readers[None, :] == sources[:, None], slots[None, :], 0), axis=1)
    hit = readers == tp_index
    present = jnp.any(hit, axis=2)
    row_index = jnp.sum(jnp.where(hit, grid - readers * rows_per_reader, 0), axis=2)
    before = sources[None, :] < sources[:, None]
    rank = jnp.sum((present[:, None, :] & before[None]).astype(jnp.int32), axis=2)
    chosen = (rank[:, None, :] == slots[None, :, None]) & present[:, None, :]
    row_of = jnp.sum(jnp.where(chosen, row_index[:, None, :], 0), axis=2)
    keep_all = jnp.sum(jnp.where(chosen, sources[None, None, :], 0), axis=2)
    keep_from = lax.dynamic_index_in_dim(keep_all, ctx_index, 0, False)
    ids = jnp.arange(ctx_count, dtype=jnp.int32)
    side = (ids // 4 + ctx_index // 4) % 2
    slot = (side * 4 + (ids + 4 - ctx_index % 4) % 4)[:, None] * blocks_dev + slots[None, :]
    rows = jnp.arange(rows_per_reader, dtype=jnp.int32)
    slot_of = jnp.sum(jnp.where(row_of.reshape(1, -1) == rows[:, None], slot.reshape(1, -1), 0), axis=1)
    return send_slot, keep_from, row_of.reshape(-1), slot_of


def shards(
    residual,
    stored_blocks,
    block_list,
    lengths,
    in_gain,
    q_gain,
    k_gain,
    post_gain,
    final_gain,
    vocab_table,
    actions,
    old_logprob,
):
    ctx_count = lax.axis_size("ctx")
    tp_count = lax.axis_size("tp")
    ctx_index = lax.axis_index("ctx")
    tp_index = lax.axis_index("tp")
    row_count = residual.shape[0]
    share_rows = row_count // tp_count
    tables = block_tables(
        block_list, ctx_index, tp_index, ctx_count, tp_count, stored_blocks.shape[0]
    )
    all_rows = whole(
        tables, lengths, residual, stored_blocks, rope_frequency(HEAD_DIM),
        in_gain, q_gain, k_gain, post_gain, final_gain, vocab_table, actions,
    )
    ref_logprob = lax.dynamic_slice_in_dim(all_rows.reshape(-1), tp_index * share_rows, share_rows, 0)
    return (ref_logprob, old_logprob - ref_logprob)


def solution(mesh):
    return jax.shard_map(
        shards,
        mesh=mesh,
        in_specs=(
            P("ctx", None),
            P(("ctx", "tp"), None, None),
            P(),
            P(),
            P(),
            P(),
            P(),
            P(),
            P(),
            P(("ctx", "tp"), None),
            P(),
            P(("ctx", "tp")),
        ),
        out_specs=(P(("ctx", "tp")), P(("ctx", "tp"))),
        check_vma=False,
    )
```

```python
import functools

import jax
import jax.numpy as jnp
import numpy as np
from jax import lax
from jax.experimental import pallas as pl
from jax.experimental.pallas import tpu as pltpu
from jax.sharding import PartitionSpec as P

HEADS = 32
KV_HEADS = 16
HEAD_DIM = 128
WINDOW = 1024
QUERY_SCALAR = 168


epsilon = 1e-06
soft_cap = 30.0
rope_base = 10000.0
MESH = pl.DeviceIdType.MESH
VMEM = pltpu.VMEM
A2_REL = (0, 1, 3, 2)


def coords():
    c = lax.axis_index("ctx")
    t = lax.axis_index("tp")
    return t // 4, (c // 4) * 2 + (t // 2) % 2, c % 4, t % 2


def device_of(x, y, z, k):
    x, y, z, k = x % 4, y % 4, z % 4, k % 2
    return ((y // 2) * 4 + z, x * 4 + (y % 2) * 2 + k)


def axis_of(part, place):
    return (part + place) % 3


def shifted(axis, steps):
    where = list(coords())
    where[axis] = where[axis] + steps
    return device_of(*where)


def sibling():
    x, y, z, k = coords()
    return device_of(x, y, z, k + 1)


def greet(peers, meanwhile=None):
    barrier = pltpu.get_barrier_semaphore()
    for peer in peers:
        pl.semaphore_signal(barrier, inc=1, device_id=peer, device_id_type=MESH)
    if meanwhile is not None:
        meanwhile()
    pl.semaphore_wait(barrier, len(peers))


def vocab_part(
    fin_ref, table_ref, actions_ref, out_ref, buf, r1, r2,
    table_sem, s1, v1, s2, v2, s3, v3, sf, vf, sk, vk, sa, va, sb, vb,
    table, acc, part_exp, part_hit, column, st1, st2,
):
    ctx = lax.axis_index("ctx")
    tp = lax.axis_index("tp")
    core = tp % 2
    own = coords()[:3]
    width = fin_ref.shape[1] // 3
    rows = fin_ref.shape[0]
    vocab_rows = table.shape[1]

    def table_copy(p):
        return pltpu.make_async_copy(
            table_ref.at[:, pl.ds(p * width, width)], table.at[p], table_sem.at[p]
        )

    for p in range(3):
        table_copy(p).start()
    for p in range(3):
        buf[p, 0, 0, core, 0] = fin_ref[:, pl.ds(p * width, width)]
    c_peer = lambda off: ((ctx + off) % 8, tp)
    t_peer = lambda off: (ctx, (tp + off) % 16)

    def send(src, dst, send_sem, recv_sem, peer):
        return pltpu.make_async_remote_copy(
            src_ref=src, dst_ref=dst, send_sem=send_sem, recv_sem=recv_sem,
            device_id=peer, device_id_type=MESH,
        )

    def first(p, step):
        return send(
            buf.at[p, 0, 0, core, 0], buf.at[p, 0, 0, core, 4 - step],
            s1.at[p, step - 1], v1.at[p, step - 1], shifted(axis_of(p, 0), step),
        )

    def second(p, step):
        slot = A2_REL.index(4 - step)
        return send(
            buf.at[p, 0, 0, core], buf.at[p, 0, slot, core],
            s2.at[p, slot], v2.at[p, slot], shifted(axis_of(p, 1), step),
        )

    def second_far(p, step):
        slot, low = (2, 0) if step == 1 else (1, 2)
        return send(
            buf.at[p, 0, slot, core, pl.ds(low, 2)], buf.at[p, 0, 3, core, pl.ds(low, 2)],
            s2.at[p, step % 3 * 3], v2.at[p, step % 3 * 3], shifted(axis_of(p, 1), step),
        )

    def third(p, q, step):
        return send(
            buf.at[p, 0, q, core], buf.at[p, 4 - step, q, core],
            s3.at[p, 4 - step, q], v3.at[p, 4 - step, q], shifted(axis_of(p, 2), step),
        )

    def passed(p, slab, q, step):
        return send(
            buf.at[p, slab, q, core], buf.at[p, 2, q, core],
            sf.at[p, q], vf.at[p, q], shifted(axis_of(p, 2), step),
        )

    def across(p, slab, q):
        return send(
            buf.at[p, slab, q, core], buf.at[p, slab, q, core],
            sk.at[p, slab, q], vk.at[p, slab, q], sibling(),
        )

    for step in (1, 3, 2):
        for p in range(3):
            first(p, step).start()

    def clear(d, carry):
        acc[d] = jnp.zeros((rows, vocab_rows), jnp.float32)
        return carry

    lax.fori_loop(0, 128, clear, 0)
    lanes = lax.broadcasted_iota(jnp.int32, (128, 128), 1)
    diagonal = lax.broadcasted_iota(jnp.int32, (128, 128), 0) == lanes

    def turn(j, carry):
        line = jnp.broadcast_to(actions_ref[pl.ds(j, 1)].astype(jnp.float32), (128, 128))
        turned = jnp.sum(jnp.where(diagonal, line, 0.0), axis=1, keepdims=True)
        column[pl.ds(j * 8, 8)] = turned.astype(jnp.int32).reshape(8, rows, 1)
        return carry

    lax.fori_loop(0, actions_ref.shape[0], turn, 0)

    for p in range(3):
        for step in (1, 3, 2):
            first(p, step).wait_recv()
    for step in (3, 1):
        for p in range(3):
            second(p, step).start()
    for p in range(3):
        for step in (1, 3):
            third(p, 0, step).start()
        across(p, 0, 0).start()

    def own_chunk(p, q):
        if q == 3:
            second_far(p, 1).wait_recv()
            second_far(p, 3).wait_recv()
        else:
            second(p, 4 - A2_REL[q]).wait_recv()
            second_far(p, 4 - A2_REL[q]).start()
        for step in (1, 3):
            third(p, q, step).start()
        across(p, 0, q).start()

    for q in (1, 2):
        for p in range(3):
            own_chunk(p, q)

    def slab_of(g, i):
        return jnp.where(g < 2, 0, jnp.where(g > 5, 2, 3 - 2 * i))

    def row_of(g, i):
        return jnp.where(g < 2, g * 2 + i, jnp.where(g > 5, (g - 6) * 2 + i, g - 2))

    def arrivals(g):
        @pl.when(g == 1)
        def _():
            for p in range(3):
                own_chunk(p, 3)

        @pl.when((g > 1) & (g < 6))
        def _():
            q = g - 2
            for p in range(3):
                third(p, q, 1).wait_recv()

                @pl.when(q % 2 == 0)
                def _():
                    passed(p, 3, q, 1).start()

                across(p, 3, q).start()
                third(p, q, 3).wait_recv()

                @pl.when(q % 2 == 1)
                def _():
                    passed(p, 1, q, 3).start()

                across(p, 1, q).start()

        @pl.when((g > 5) & (g < 8))
        def _():
            for i in range(2):
                q = (g - 6) * 2 + i
                for p in range(3):
                    passed(p, 3, q, 1).wait_recv()
                    across(p, 2, q).start()

    def place(axis_values, k):
        x, y, z = axis_values
        return ((y // 2) * 4 + z) * 16 + x * 4 + (y % 2) * 2 + k

    first_id = (ctx * 16 + tp) * vocab_rows
    ids = first_id + lax.broadcasted_iota(jnp.int32, (rows, vocab_rows), 1)

    def fold(v):
        total = v[:, :128]
        for i in range(1, vocab_rows // 128):
            total = total + v[:, i * 128:(i + 1) * 128]
        return total

    def tail(rel):
        at = place([(own[i] + rel[i]) % 4 for i in range(3)], 0)
        for kk in range(2):
            capped = soft_cap * jnp.tanh(acc[at + kk] * (1.0 / soft_cap))
            hit = ids == column[at + kk]
            part_exp[at + kk] = fold(jnp.exp(capped))
            part_hit[at + kk] = fold(jnp.where(hit, capped, 0.0))

    def near(digit):
        return digit + digit // 2

    def early_tail(i, carry):
        for j in range(3):
            tail((near(i // 3), near(i % 3), near(j)))
        return carry

    def middle_tail(i, carry):
        for j in range(3):
            tail((2, near(j), i))
            tail((i, 2, near(j)))
            tail((near(j), i, 2))
        return carry

    def late_tail(i, carry):
        for j in range(4):
            tail((2, j, 2 + i))
        tail((2, 2, i))
        tail((i, 2, 2))
        for j in range(2):
            tail((3, 2, 2 * i + j))
        return carry

    def group(g, carry):
        @pl.when(g == 7)
        def _():
            lax.fori_loop(0, 2, middle_tail, 0)

        slabs, lines = [slab_of(g, i) for i in range(2)], [row_of(g, i) for i in range(2)]
        for p in range(3):
            for i in range(2):
                across(p, slabs[i], lines[i]).wait_recv()

            @pl.when(g == 0)
            def _():
                table_copy(p).wait()

            lhs = jnp.concatenate(
                [buf[p, slabs[i], lines[i]].reshape(8 * rows, width) for i in range(2)], axis=0
            )
            got = lax.dot_general(
                lhs, table[p], (((1,), (1,)), ((), ())), preferred_element_type=jnp.float32
            )
            a1, a2, a3 = (axis_of(p, i) for i in range(3))
            for i in range(2):
                rel2 = jnp.where(lines[i] < 2, lines[i], 5 - lines[i])
                for kk in range(2):
                    for r1_ in range(4):
                        at = [None] * 3
                        at[a1] = (own[a1] + r1_) % 4
                        at[a2] = (own[a2] + rel2) % 4
                        at[a3] = (own[a3] + slabs[i]) % 4
                        d = place(at, kk)
                        m = (i * 2 + kk) * 4 + r1_
                        value = got[m * rows:(m + 1) * rows]
                        acc[d] = acc[d] + value
            if p == 0:
                @pl.when(g == 6)
                def _():
                    lax.fori_loop(0, 9, early_tail, 0)

                arrivals(g + 1)
        return carry

    lax.fori_loop(0, 8, group, 0)

    lax.fori_loop(0, 2, late_tail, 0)
    for j in range(3):
        tail((near(j), 3, 2))
    ones = jnp.ones((8, 128), jnp.float32)
    for c in range(8):
        sums = [
            lax.dot_general(
                ones, part[pl.ds(c * 16, 16)].reshape(16 * rows, 128), (((1,), (1,)), ((), ())),
                preferred_element_type=jnp.float32, precision=lax.Precision.HIGHEST,
            )
            for part in (part_exp, part_hit)
        ]
        st1[c] = jnp.concatenate(
            [v[:1, i * 128:(i + 1) * 128] for v in (sums + sums) for i in range(2)], axis=0
        )

    def stage1(off):
        return send(st1.at[(ctx + off) % 8], r1.at[off], sa.at[off], va.at[off], c_peer(off))

    def stage2(off):
        return send(st2, r2.at[off], sb.at[off], vb.at[off], t_peer(off))

    for off in range(1, 8):
        stage1(off).start()
    total = st1[ctx]
    for off in range(1, 8):
        stage1(off).wait_recv()
        total = total + r1[off]
    st2[...] = total
    for off in range(1, 16):
        stage2(off).start()
    for off in range(1, 16):
        stage2(off).wait_recv()
        total = total + r2[off]
    out_ref[...] = total[2:4] - jnp.log(total[:2])

    for p in range(3):
        for step in (1, 2, 3):
            first(p, step).wait_send()
        for step in (1, 3):
            second(p, step).wait_send()
            second_far(p, step).wait_send()
        for q in range(4):
            third(p, q, 1).wait_send()
            third(p, q, 3).wait_send()
            passed(p, 3, q, 1).wait_send()
            for slab in range(4):
                across(p, slab, q).wait_send()
    for off in range(1, 8):
        stage1(off).wait_send()
    for off in range(1, 16):
        stage2(off).wait_send()


CHUNK_AT = (1, 0, 2)
Z_FIRST = (0, 0, 2)


def layer_part(
    send_slot, keep_from, row_of, slot_of,
    lengths, residual_hbm, stored_hbm, frequency, in_lines, post_lines, final_lines, q_gain, k_gain, out_ref,
    got_0, got_1, got_2, held, kv, half_in, part_in,
    load_sem, x_s, x_r, y_s, y_r, z_s, z_r, f_s, f_r, h_s, h_r, c_s, c_r, p_s, p_r,
    in_gain, post_gain, final_gain, cos_ref, sin_ref, residual_ref, stored_ref, out, cols, proj,
    query, mixed, wout, half_out, part_out, summed,
):
    ctx = lax.axis_index("ctx")
    tp = lax.axis_index("tp")
    core = tp % 2
    chip = tp // 2
    y_hi, z = ctx // 4, ctx % 4
    n_blk = stored_ref.shape[0]
    blk_rows = stored_ref.shape[1]
    tokens, depth = residual_ref.shape
    head = q_gain.shape[1]

    def send(src, dst, send_sem, recv_sem, peer):
        return pltpu.make_async_remote_copy(
            src_ref=src, dst_ref=dst, send_sem=send_sem, recv_sem=recv_sem,
            device_id=peer, device_id_type=MESH,
        )

    t_peer = lambda off: (ctx, (tp + off) % 16)
    z_peer = lambda step: (y_hi * 4 + (z + step) % 4, tp)
    y_peer = ((ctx + 4) % 8, tp)

    got = (got_0, got_1, got_2)

    def swap(i, off):
        return send(
            out.at[i, (tp + off) % 16], got[i].at[tp], x_s.at[i, off], x_r.at[i, off], t_peer(off)
        )

    stored_copy = pltpu.make_async_copy(stored_hbm, stored_ref, load_sem.at[0])
    residual_copy = pltpu.make_async_copy(residual_hbm, residual_ref, load_sem.at[1])
    stored_copy.start()
    residual_copy.start()
    chunk = out.shape[3]

    def stage(t, carry):
        block = stored_ref[send_slot[t]]
        for i, at in enumerate(CHUNK_AT):
            out[i, t] = block[:, at * chunk:(at + 1) * chunk]
        return carry

    def stage_all():
        stored_copy.wait()
        lax.fori_loop(0, 16, stage, 0)

    x_at, y_at, z_at, k_at = coords()
    far_y = device_of(x_at, y_at - 1 + 2 * (y_at % 2), z_at, k_at)
    greet(
        [((ctx + o) % 8, tp) for o in range(1, 8)] + [t_peer(o) for o in range(1, 16)] + [far_y],
        stage_all,
    )

    def start_swap(off, carry):
        swap(0, off).start()
        return carry

    lax.fori_loop(1, 16, start_swap, 0)
    residual_copy.wait()
    for gain, lines in ((in_gain, in_lines), (post_gain, post_lines), (final_gain, final_lines)):
        for i in range(lines.shape[0]):
            gain[:, i * 128:(i + 1) * 128] = lines[i:i + 1]
    for i in range(3):
        got[i][tp] = out[i, tp]

    step_rows = 32

    def norm_rows(i, carry):
        at = pl.ds(pl.multiple_of(i * step_rows, step_rows), step_rows)
        x = residual_ref[at].astype(jnp.float32)
        scale = lax.rsqrt(jnp.mean(x * x, axis=-1, keepdims=True) + epsilon)
        n = (x * scale * in_gain[...]).astype(jnp.bfloat16)
        for r in range(depth // blk_rows):
            cols[r, at, :blk_rows] = n[:, r * blk_rows:(r + 1) * blk_rows]
        return carry

    lax.fori_loop(0, tokens // step_rows, norm_rows, 0)
    proj[...] = jnp.zeros_like(proj)
    row_ids = ctx * tokens + lax.broadcasted_iota(jnp.int32, (tokens, 1), 0)
    seg_start = jnp.zeros_like(row_ids)
    begin = jnp.int32(0)
    for i in range(lengths.shape[0]):
        seg_start = jnp.maximum(seg_start, jnp.where(begin <= row_ids, begin, 0))
        begin = begin + lengths[i]
    angle = (row_ids - seg_start).astype(jnp.float32) * frequency[...]
    low = lax.broadcasted_iota(jnp.int32, angle.shape, 1) < head // 2
    cos_ref[...] = jnp.cos(angle)
    sin_ref[...] = jnp.where(low, -jnp.sin(angle), jnp.sin(angle))

    def early(i):
        return n_blk - Z_FIRST[i]

    def y_copy(i, zz, k):
        return send(
            held.at[i, 0, zz, k], held.at[i, 1, zz, k], y_s.at[i, zz, k], y_r.at[i, zz, k], y_peer
        )

    def z_copy(i, yy, step, k):
        j = 0 if step == 1 else 1
        return send(
            held.at[i, yy, 0, k], held.at[i, yy, 4 - step, k],
            z_s.at[i, yy, j, k], z_r.at[i, yy, j, k], z_peer(step),
        )

    def f_copy(i, yy, step, k):
        return send(
            held.at[i, yy, 3 if step == 1 else 1, k], held.at[i, yy, 2, k],
            f_s.at[i, yy, k], f_r.at[i, yy, k], z_peer(step),
        )

    def blocks(body, low=0, high=None):
        def run(k, carry):
            body(k)
            return carry

        lax.fori_loop(low, n_blk if high is None else high, run, 0)

    def own(i):
        def wait(off, carry):
            swap(i, off).wait_recv()
            return carry

        def body(k):
            held[i, 0, 0, k] = got[i][keep_from[k]]
            y_copy(i, 0, k).start()
            z_copy(i, 0, 1, k).start()
            z_copy(i, 0, 3, k).start()
            if i < 2:
                swap(i + 1, 2 * k + 1).start()
                swap(i + 1, 2 * k + 2).start()

        lax.fori_loop(1, 16, wait, 0)
        blocks(body)
        if i < 2:
            swap(i + 1, 15).start()

    def partner(i):
        def body(k):
            y_copy(i, 0, k).wait_recv()

            @pl.when(k < early(i))
            def _():
                z_copy(i, 1, 1, k).start()
                z_copy(i, 1, 3, k).start()

            term(i, 0, 0, k)
            term(i, 1, 0, k)

        blocks(body)

    def side(i, yy):
        half = 4 if yy == 0 else early(i) // 2

        def body(k):
            z_copy(i, yy, 1, k).wait_recv()

            @pl.when(k < half)
            def _():
                f_copy(i, yy, 1, k).start()

            z_copy(i, yy, 3, k).wait_recv()

            @pl.when(k >= half)
            def _():
                f_copy(i, yy, 3, k).start()

            if yy == 0:
                @pl.when(k >= early(i))
                def _():
                    y_copy(i, 3, k).start()
                    y_copy(i, 1, k).start()

            term(i, yy, 3, k)
            term(i, yy, 1, k)

        def across(k):
            y_copy(i, 3, k).wait_recv()
            y_copy(i, 1, k).wait_recv()
            term(i, 1, 3, k)
            term(i, 1, 1, k)

        if yy == 0:
            blocks(body)
        else:
            blocks(body, 0, early(i))
            blocks(across, early(i))

    def far(i, yy):
        def body(k):
            f_copy(i, yy, 1, k).wait_recv()
            if yy == 0:
                @pl.when(k >= early(i))
                def _():
                    y_copy(i, 2, k).start()
            term(i, yy, 2, k)

        def across(k):
            y_copy(i, 2, k).wait_recv()
            term(i, 1, 2, k)

        if yy == 0:
            blocks(body)
        else:
            blocks(body, 0, early(i))
            blocks(across, early(i))

    def term(i, yy, zz, k):
        if CHUNK_AT[i] < 2:
            c = (y_hi + yy) % 2 * 4 + (z + zz) % 4
            at = CHUNK_AT[i] * chunk
            proj[:, at:at + chunk] += jnp.dot(
                cols[row_of[c * n_blk + k], :, :blk_rows], held[i, yy, zz, k],
                preferred_element_type=jnp.float32,
            )

    own(0)
    partner(0)
    side(0, 0)
    own(1)
    side(0, 1)
    partner(1)
    far(0, 0)
    side(1, 0)
    own(2)
    far(0, 1)

    def heads(at, gain):
        e = proj[:, pl.ds(at * head, head)]
        scale = lax.rsqrt(jnp.mean(e * e, axis=-1, keepdims=True) + epsilon)
        e = e * scale * gain[...]
        return (e * cos_ref[...] + pltpu.roll(e, head // 2, 1) * sin_ref[...]).astype(jnp.bfloat16)

    reach = kv.shape[0] - 1
    kv[reach, :, :head] = heads(2, k_gain)
    kv[reach, :, head:] = proj[:, 3 * head:].astype(jnp.bfloat16)

    def halo(step):
        return send(
            kv.at[reach], kv.at[reach - step], h_s.at[step - 1], h_r.at[step - 1],
            ((ctx + step) % 8, tp),
        )

    for step in range(1, reach + 1):
        @pl.when(ctx + step < 8)
        def _():
            halo(step).start()

        @pl.when(ctx < step)
        def _():
            kv[reach - step] = jnp.zeros(kv.shape[1:], kv.dtype)

    side(1, 1)
    partner(2)
    far(1, 0)
    far(1, 1)
    for h in range(2):
        query[h] = heads(h, q_gain)
    side(2, 0)
    side(2, 1)
    for step in range(1, reach + 1):
        @pl.when(ctx >= step)
        def _():
            halo(step).wait_recv()

    span = (reach + 1) * tokens
    key_rows = kv[:, :, :head].reshape(span, head)
    value_rows = kv[:, :, head:].reshape(span, head)
    q_ids = ctx * tokens + lax.broadcasted_iota(jnp.int32, (tokens, span), 0)
    k_ids = (ctx - reach) * tokens + lax.broadcasted_iota(jnp.int32, (tokens, span), 1)
    visible = (k_ids <= q_ids) & (q_ids - k_ids < WINDOW) & (k_ids >= seg_start)
    for h in range(2):
        scores = lax.dot_general(
            query[h], key_rows, (((1,), (1,)), ((), ())), preferred_element_type=jnp.float32
        ) * QUERY_SCALAR ** (-0.5)
        probs = jnp.where(visible, jnp.exp(scores), 0.0)
        probs = (probs / jnp.sum(probs, axis=1, keepdims=True)).astype(jnp.bfloat16)
        heard = jnp.dot(probs, value_rows, preferred_element_type=jnp.float32).astype(jnp.bfloat16)
        mixed[:, :, :, h * head:(h + 1) * head] = heard.reshape(8, 2, tokens // 16, head)

    far(2, 0)
    far(2, 1)

    share = tokens // 16
    per = wout.shape[0] // half_out.shape[0]
    piece = per * blk_rows
    other = (tp // 2) * 2 + (1 - core)

    def product(which, n):
        rows = mixed[:, which].reshape(8 * share, 2 * head)
        block = wout[pl.ds(n * per, per)].reshape(piece, 2 * head)
        return lax.dot_general(
            rows, block, (((1,), (1,)), ((), ())), preferred_element_type=jnp.float32
        ).reshape(8, share, piece)

    def between(n):
        return send(half_out.at[n], half_in.at[n], c_s.at[n], c_r.at[n], (ctx, other))

    def to_chip(n, off):
        there = (chip + off) % 8
        return send(
            part_out.at[n, there], part_in.at[n, off], p_s.at[n, off], p_r.at[n, off],
            (ctx, there * 2 + core),
        )

    n_pieces = half_out.shape[0]

    def order(r, carry):
        wout[r] = held.at[2].reshape(8 * n_blk, blk_rows, chunk)[slot_of[r]]
        return carry

    def give(n):
        lax.fori_loop(n * per, (n + 1) * per, order, 0)
        half_out[n] = product(1 - core, n).astype(jnp.bfloat16)
        between(n).start()

    def take(n, carry):
        mine = product(core, n)
        between(n).wait_recv()
        part_out[n] = (mine + half_in[n].astype(jnp.float32)).astype(jnp.bfloat16)
        for off in (2, 6, 1, 4, 3, 7, 5):
            to_chip(n, off).start()

        @pl.when(n + 2 < n_pieces)
        def _():
            give(n + 2)

        return carry

    give(0)
    give(1)
    lax.fori_loop(0, n_pieces, take, 0)
    def swapped(off, carry):
        for i in range(3):
            swap(i, off).wait_send()
        return carry

    lax.fori_loop(1, 16, swapped, 0)
    for i in range(3):
        def sent(k):
            y_copy(i, 0, k).wait_send()
            z_copy(i, 0, 1, k).wait_send()
            z_copy(i, 0, 3, k).wait_send()
            f_copy(i, 0, 1, k).wait_send()

        def sent_z(k):
            z_copy(i, 1, 1, k).wait_send()
            z_copy(i, 1, 3, k).wait_send()
            f_copy(i, 1, 1, k).wait_send()

        def sent_y(k):
            for zz in range(1, 4):
                y_copy(i, zz, k).wait_send()

        blocks(sent)
        blocks(sent_z, 0, early(i))
        blocks(sent_y, early(i))
    for step in range(1, reach + 1):
        @pl.when(ctx + step < 8)
        def _():
            halo(step).wait_send()

    def halves_sent(n, carry):
        between(n).wait_send()
        return carry

    lax.fori_loop(0, n_pieces, halves_sent, 0)
    for n in range(n_pieces):
        total = part_out[n, chip].astype(jnp.float32)
        for off in range(1, 8):
            to_chip(n, off).wait_recv()
            total = total + part_in[n, off].astype(jnp.float32)
        summed[:, n * piece:(n + 1) * piece] = total

    def rms(values, gain):
        return values * lax.rsqrt(jnp.mean(values * values, axis=-1, keepdims=True) + epsilon) * gain[...]

    mine = residual_ref[pl.ds(pl.multiple_of(tp * share, share), share)].astype(jnp.float32)
    hidden = mine + rms(summed[...], post_gain)
    out_ref[...] = rms(hidden, final_gain).astype(jnp.bfloat16)

    def parts_sent(n, carry):
        for off in range(1, 8):
            to_chip(n, off).wait_send()
        return carry

    lax.fori_loop(0, n_pieces, parts_sent, 0)


def whole_kernel(counts, *refs):
    n_tables, n_layer, n_layer_own, n_vocab_own = counts
    tables, refs = refs[:n_tables], refs[n_tables:]
    (lengths, residual, stored, frequency, in_lines, post_lines, final_lines, q_gain, k_gain,
     table, actions, out_ref, fin), refs = refs[:13], refs[13:]
    layer_refs, vocab_refs = refs[:n_layer], refs[n_layer:]
    pl.run_scoped(
        lambda *own: layer_part(
            *tables, lengths, residual, stored, frequency, in_lines, post_lines, final_lines,
            q_gain, k_gain, fin, *layer_refs, *own,
        ),
        *n_layer_own,
    )
    pl.run_scoped(
        lambda *own: vocab_part(fin, table, actions, out_ref, *vocab_refs, *own), *n_vocab_own
    )


def whole(
    tables, lengths, residual, stored, frequency, in_gain, q_gain, k_gain, post_gain, final_gain,
    vocab_table, actions,
):
    tokens, depth = residual.shape
    n_blk, blk_rows, width = stored.shape
    vocab_rows = vocab_table.shape[0]
    head = q_gain.shape[0]
    share = tokens // 16
    bf16, f32 = jnp.bfloat16, jnp.float32
    n_rows = depth // blk_rows
    n_pieces = 7
    piece = depth // n_pieces
    reach = WINDOW // tokens
    chunk = width // 3
    third = depth // 3
    dma = pltpu.SemaphoreType.DMA
    smem = pl.BlockSpec(memory_space=pltpu.SMEM)
    vmem = pl.BlockSpec(memory_space=VMEM)
    far = pl.BlockSpec(memory_space=pl.ANY)
    layer_refs = [
        VMEM((16, blk_rows, chunk), bf16),
        VMEM((16, blk_rows, chunk), bf16),
        VMEM((16, blk_rows, chunk), bf16),
        VMEM((3, 2, 4, n_blk, blk_rows, chunk), bf16),
        VMEM((reach + 1, tokens, 2 * head), bf16),
        VMEM((n_pieces, 8, share, piece), bf16),
        VMEM((n_pieces, 8, share, piece), bf16),
        dma((2,)),
        dma((3, 16)), dma((3, 16)),
        dma((3, 4, n_blk)), dma((3, 4, n_blk)),
        dma((3, 2, 2, n_blk)), dma((3, 2, 2, n_blk)),
        dma((3, 2, n_blk)), dma((3, 2, n_blk)),
        dma((reach,)), dma((reach,)),
        dma((n_pieces,)), dma((n_pieces,)),
        dma((n_pieces, 8)), dma((n_pieces, 8)),
    ]
    layer_own = [
        VMEM((1, depth), f32),
        VMEM((1, depth), f32),
        VMEM((1, depth), f32),
        VMEM((tokens, head), f32),
        VMEM((tokens, head), f32),
        VMEM((tokens, depth), bf16),
        VMEM((n_blk, blk_rows, width), bf16),
        VMEM((3, 16, blk_rows, chunk), bf16),
        VMEM((n_rows, tokens, 128), bf16),
        VMEM((tokens, 2 * chunk), f32),
        VMEM((2, tokens, head), bf16),
        VMEM((8, 2, share, 2 * head), bf16),
        VMEM((n_rows, blk_rows, chunk), bf16),
        VMEM((n_pieces, 8, share, piece), bf16),
        VMEM((n_pieces, 8, share, piece), bf16),
        VMEM((share, depth), f32),
    ]
    vocab_refs = [
        VMEM((3, 4, 4, 2, 4, share, third), bf16),
        VMEM((8, 8, 128), f32),
        VMEM((16, 8, 128), f32),
        dma((3,)),
        dma((3, 3)), dma((3, 3)),
        dma((3, 4)), dma((3, 4)),
        dma((3, 4, 4)), dma((3, 4, 4)),
        dma((3, 4)), dma((3, 4)),
        dma((3, 4, 4)), dma((3, 4, 4)),
        dma((8,)), dma((8,)),
        dma((16,)), dma((16,)),
    ]
    vocab_own = [
        VMEM((3, vocab_rows, third), bf16),
        VMEM((128, share, vocab_rows), f32),
        VMEM((128, share, 128), f32),
        VMEM((128, share, 128), f32),
        VMEM((128, share, 1), jnp.int32),
        VMEM((8, 8, 128), f32),
        VMEM((8, 128), f32),
    ]
    counts = (len(tables), len(layer_refs), layer_own, vocab_own)
    return pl.pallas_call(
        functools.partial(whole_kernel, counts),
        out_shape=jax.ShapeDtypeStruct((2, 128), f32),
        in_specs=[smem] * 5 + [far] * 2 + [vmem] * 6 + [far, vmem],
        out_specs=vmem,
        scratch_shapes=[VMEM((share, depth), bf16)] + layer_refs + vocab_refs,
        compiler_params=pltpu.CompilerParams(
            collective_id=1, has_side_effects=True, vmem_limit_bytes=63 * 2**20
        ),
        name="whole",
    )(
        *tables, lengths, residual, stored, frequency,
        in_gain.reshape(-1, 128), post_gain.reshape(-1, 128), final_gain.reshape(-1, 128),
        q_gain[None], k_gain[None], vocab_table, actions.reshape(-1, 128),
    )


def rope_frequency(head):
    half_size = head // 2
    frequency = rope_base ** (-2.0 * np.arange(half_size, dtype=np.float64) / head)
    return jnp.asarray(np.concatenate([frequency, frequency])[None].astype(np.float32))


def block_tables(block_list, ctx_index, tp_index, ctx_count, tp_count, blocks_dev):
    rows_per_reader = blocks_dev * ctx_count
    grid = block_list.reshape(ctx_count, tp_count, blocks_dev)
    readers = (grid * 1171) >> 16
    my_readers = lax.dynamic_slice(
        readers, (ctx_index, tp_index, 0), (1, 1, blocks_dev)
    ).reshape(-1)
    slots = jnp.arange(blocks_dev, dtype=jnp.int32)
    sources = jnp.arange(tp_count, dtype=jnp.int32)
    send_slot = jnp.sum(jnp.where(my_readers[None, :] == sources[:, None], slots[None, :], 0), axis=1)
    hit = readers == tp_index
    present = jnp.any(hit, axis=2)
    row_index = jnp.sum(jnp.where(hit, grid - readers * rows_per_reader, 0), axis=2)
    before = sources[None, :] < sources[:, None]
    rank = jnp.sum((present[:, None, :] & before[None]).astype(jnp.int32), axis=2)
    chosen = (rank[:, None, :] == slots[None, :, None]) & present[:, None, :]
    row_of = jnp.sum(jnp.where(chosen, row_index[:, None, :], 0), axis=2)
    keep_all = jnp.sum(jnp.where(chosen, sources[None, None, :], 0), axis=2)
    keep_from = lax.dynamic_index_in_dim(keep_all, ctx_index, 0, False)
    ids = jnp.arange(ctx_count, dtype=jnp.int32)
    side = (ids // 4 + ctx_index // 4) % 2
    slot = (side * 4 + (ids + 4 - ctx_index % 4) % 4)[:, None] * blocks_dev + slots[None, :]
    rows = jnp.arange(rows_per_reader, dtype=jnp.int32)
    slot_of = jnp.sum(jnp.where(row_of.reshape(1, -1) == rows[:, None], slot.reshape(1, -1), 0), axis=1)
    return send_slot, keep_from, row_of.reshape(-1), slot_of


def shards(
    residual,
    stored_blocks,
    block_list,
    lengths,
    in_gain,
    q_gain,
    k_gain,
    post_gain,
    final_gain,
    vocab_table,
    actions,
    old_logprob,
):
    ctx_count = lax.axis_size("ctx")
    tp_count = lax.axis_size("tp")
    ctx_index = lax.axis_index("ctx")
    tp_index = lax.axis_index("tp")
    row_count = residual.shape[0]
    share_rows = row_count // tp_count
    tables = block_tables(
        block_list, ctx_index, tp_index, ctx_count, tp_count, stored_blocks.shape[0]
    )
    all_rows = whole(
        tables, lengths, residual, stored_blocks, rope_frequency(HEAD_DIM),
        in_gain, q_gain, k_gain, post_gain, final_gain, vocab_table, actions,
    )
    ref_logprob = lax.dynamic_slice_in_dim(all_rows.reshape(-1), tp_index * share_rows, share_rows, 0)
    return (ref_logprob, old_logprob - ref_logprob)


def solution(mesh):
    return jax.shard_map(
        shards,
        mesh=mesh,
        in_specs=(
            P("ctx", None),
            P(("ctx", "tp"), None, None),
            P(),
            P(),
            P(),
            P(),
            P(),
            P(),
            P(),
            P(("ctx", "tp"), None),
            P(),
            P(("ctx", "tp")),
        ),
        out_specs=(P(("ctx", "tp")), P(("ctx", "tp"))),
        check_vma=False,
    )
```
